128 devices in a mesh: dp: 16 (over z_lo, x, core), seq: 8 (over y, z_hi).
Axes of the slice: x: 4, y: 4, z: 4 (z_hi: 2, z_lo: 2; z = z_hi * 2 + z_lo), core: 2. Of those that a mesh axis runs over, the one named last changes fastest.
Arguments:
- hidden_in: bfloat16 [16, 1024, 2048], P('dp', 'seq'), may hold values from -6 to 6
- norm1_gain: bfloat16 [2048], P(('dp', 'seq')), may hold values from 0.099609375 to 1.8984375
- query_weight: bfloat16 [2048, 256], P(('dp', 'seq')), may hold values from -0.125 to 0.125
- key_weight: bfloat16 [2048, 256], P(('dp', 'seq')), may hold values from -0.125 to 0.125
- value_weight: bfloat16 [2048, 2048], P(('dp', 'seq')), may hold values from -0.125 to 0.125
- out_weight: bfloat16 [2048, 2048], P(('dp', 'seq')), may hold values from -1 to 1
- norm2_gain: bfloat16 [2048], P(('dp', 'seq')), may hold values from 0.099609375 to 1.8984375
- gate_weight: bfloat16 [2048, 5504], P(('dp', 'seq')), may hold values from -0.125 to 0.125
- up_weight: bfloat16 [2048, 5504], P(('dp', 'seq')), may hold values from -0.125 to 0.125
- down_weight: bfloat16 [2048, 5504], P(('dp', 'seq')), may hold values from -0.078125 to 0.078125
- cotangent: bfloat16 [16, 1024, 2048], P('dp', 'seq'), may hold values from -6 to 6
- source_id: int32 [16], P('dp'), may hold values from 0 to 7
- source_counts: int32 [8], replicated, may hold values from 1 to 64
Outputs:
- layer_out: bfloat16 [16, 1024, 2048], P('dp', 'seq')
- grad_in: float32 [16, 1024, 2048], P('dp', 'seq')
- grad_norm1: float32 [2048], P(('dp', 'seq'))
- grad_query: float32 [2048, 256], P(('dp', 'seq'))
- grad_key: float32 [2048, 256], P(('dp', 'seq'))
- grad_value: float32 [2048, 2048], P(('dp', 'seq'))
- grad_out: float32 [2048, 2048], P(('dp', 'seq'))
- grad_norm2: float32 [2048], P(('dp', 'seq'))
- grad_gate: float32 [2048, 5504], P(('dp', 'seq'))
- grad_up: float32 [2048, 5504], P(('dp', 'seq'))
- grad_down: float32 [2048, 5504], P(('dp', 'seq'))
The draws below stay inside these ranges and needn't reach their ends.
All inputs are finite; a program needn't handle non-finite values.
Results may differ from the reference program's by a relative error of at most 0.025.
Values may be sent and summed in bfloat16 or wider, within the bound.
A program may use at most 192 MiB of HBM per device.

```python
import math
import jax
import jax.numpy as jnp
from jax import lax

D = 2048
HEADS = 16
FEAT = 16
HEAD_V = 128
FF = 5504
SOURCES = 8
SEQ_LEN = 1024
TOK_DEV = 128
ROWS = 16
TAYLOR = 273
QK = 256
VW = 2048


def set_ends(drawn, rng, smallest, largest):
    extent = drawn.shape
    place = [jax.random.randint(jax.random.fold_in(rng, axis), (), 0, extent[axis]) for axis in range(len(extent))]
    drawn = drawn.at[tuple(place)].set(smallest)
    longest = extent.index(max(extent))
    place[longest] = (place[longest] + 1) % extent[longest]
    return drawn.at[tuple(place)].set(largest)


def block_scale(rng, dims, split, least, top_value):
    def one(axis_at, parts):
        heights = jax.random.uniform(jax.random.fold_in(jax.random.fold_in(rng, 6), axis_at), (parts,), jnp.float32, least / len(split), top_value / len(split))
        return jnp.repeat(jnp.exp(heights), dims[axis_at] // parts).reshape((-1,) + (1,) * (len(dims) - axis_at - 1))

    loudness = one(*split[0])
    for cut in split[1:]:
        loudness = loudness * one(*cut)
    return loudness


def noise(key, extent, width, reach, shards=(), held_as=jnp.bfloat16):
    entries = jax.random.normal(key, extent, jnp.float32) * width
    if len(shards) > 0:
        entries = block_scale(key, extent, shards, -0.22, 0.18) * entries
    return jnp.clip(entries, min=-reach, max=reach).astype(held_as)


def setup_inputs(seed: int = 0) -> dict:
    key_of = jax.random.split(jax.random.key(seed), 14)
    hidden_in = noise(key_of[0], (ROWS, SEQ_LEN, D), 1.0, 6.0, ((0, 16), (1, 8)))
    norm1_gain = jnp.clip(1.0 + 0.18 * jax.random.normal(key_of[1], (D,), jnp.float32), 0.099609375, 1.8984375).astype(jnp.bfloat16)
    query_weight = noise(key_of[2], (D, QK), D ** -0.5, 0.125, ((0, 128),))
    key_weight = noise(key_of[3], (D, QK), D ** -0.5, 0.125, ((0, 128),))
    value_weight = noise(key_of[4], (D, VW), D ** -0.5, 0.125, ((0, 128),))
    out_weight = noise(key_of[5], (D, VW), (VW // 64) ** -0.5, 1.0, ((0, 128),))
    norm2_gain = jnp.clip(1.0 + 0.18 * jax.random.normal(key_of[6], (D,), jnp.float32), 0.099609375, 1.8984375).astype(jnp.bfloat16)
    gate_weight = noise(key_of[7], (D, FF), D ** -0.5, 0.125, ((0, 128),))
    up_weight = noise(key_of[8], (D, FF), D ** -0.5, 0.125, ((0, 128),))
    down_weight = noise(key_of[9], (D, FF), FF ** -0.5, 0.078125, ((0, 128),))
    cotangent = noise(key_of[10], (ROWS, SEQ_LEN, D), 1.0, 6.0, ((0, 16), (1, 8)))
    source_id = set_ends(jax.random.randint(key_of[11], (ROWS,), 0, SOURCES), jax.random.fold_in(key_of[11], 1), 0, SOURCES - 1).astype(jnp.int32)
    source_counts = set_ends(jax.random.randint(key_of[12], (SOURCES,), 1, 65), jax.random.fold_in(key_of[12], 1), 1, 64).astype(jnp.int32)
    return {"hidden_in": hidden_in, "norm1_gain": norm1_gain, "query_weight": query_weight, "key_weight": key_weight, "value_weight": value_weight, "out_weight": out_weight, "norm2_gain": norm2_gain, "gate_weight": gate_weight, "up_weight": up_weight, "down_weight": down_weight, "cotangent": cotangent, "source_id": source_id, "source_counts": source_counts}


norm_eps = 1e-05
highest = lax.Precision.HIGHEST

@jax.custom_vjp
def low(v):
    return lax.optimization_barrier(v.astype(jnp.bfloat16)).astype(jnp.float32)

@jax.custom_vjp
def low_back(v):
    return v

def low_keep(v):
    return (low(v), None)

def low_pass(kept, grad):
    return (grad,)

def back_keep(v):
    return (v, None)

def back_low(kept, grad):
    return (low(grad),)
low.defvjp(low_keep, low_pass)
low_back.defvjp(back_keep, back_low)

def taylor(inputs):
    inner = inputs.shape[-1]
    lead = inputs.shape[:-1]
    first = inputs / inner ** 0.25
    second = (inputs[..., :, None] * inputs[..., None, :]).reshape(lead + (inner * inner,)) / math.sqrt(2.0 * inner)
    return jnp.concatenate([jnp.ones(lead + (1,), jnp.float32), first, second], axis=-1)

def normalize(inputs, gain):
    return inputs * lax.rsqrt(lax.optimization_barrier(jnp.mean(inputs * inputs, axis=-1, keepdims=True)) + norm_eps) * gain

def attend_block(carry, block):
    state, total = carry
    feat_q, feat_k, values = block
    length = feat_q.shape[0]
    causal = jnp.arange(length)[:, None] >= jnp.arange(length)[None, :]
    scores = jnp.einsum('thf,shf->hts', feat_q, feat_k, precision=highest)
    scores = jnp.where(causal[None], scores, 0.0)
    numer = jnp.einsum('hts,shv->thv', scores, values, precision=highest)
    numer = numer + jnp.einsum('thf,hfv->thv', feat_q, state, precision=highest)
    denom_sum = lax.optimization_barrier(jnp.sum(scores, axis=-1)).T + jnp.einsum('thf,hf->th', feat_q, total, precision=highest)
    state = state + jnp.einsum('shf,shv->hfv', feat_k, values, precision=highest)
    total = total + lax.optimization_barrier(jnp.sum(feat_k, axis=0))
    return ((state, total), numer / denom_sum[:, :, None])

def layer(params, row):
    norm1, w_query, w_key, w_value, w_out, norm2, w_gate, w_up, w_down = params
    length = row.shape[0]
    blocks = length // TOK_DEV
    normed = low(normalize(row, norm1))
    query = low_back(jnp.dot(normed, w_query, precision=highest))
    keys = low_back(jnp.dot(normed, w_key, precision=highest))
    values = low(low_back(jnp.dot(normed, w_value, precision=highest)))
    feat_q = low(taylor(query.reshape(length, HEADS, FEAT)))
    feat_k = low(taylor(keys.reshape(length, HEADS, FEAT)))
    start = (jnp.zeros((HEADS, TAYLOR, HEAD_V), jnp.float32), jnp.zeros((HEADS, TAYLOR), jnp.float32))
    pieces = (feat_q.reshape(blocks, TOK_DEV, HEADS, TAYLOR), feat_k.reshape(blocks, TOK_DEV, HEADS, TAYLOR), values.reshape(blocks, TOK_DEV, HEADS, HEAD_V))
    unused, mixed = lax.scan(jax.checkpoint(attend_block), start, pieces)
    attended = low(low_back(mixed.reshape(length, VW)))
    middle = row + low_back(jnp.dot(attended, w_out.T, precision=highest))
    normed2 = low(normalize(middle, norm2))
    gate = low_back(jnp.dot(normed2, w_gate, precision=highest))
    upward = low_back(jnp.dot(normed2, w_up, precision=highest))
    hidden = low(jax.nn.silu(gate) * upward)
    return middle + low_back(jnp.dot(hidden, w_down.T, precision=highest))

def reference(hidden_in, norm1_gain, query_weight, key_weight, value_weight, out_weight, norm2_gain, gate_weight, up_weight, down_weight, cotangent, source_id, source_counts):
    params = tuple((item.astype(jnp.float32) for item in (norm1_gain, query_weight, key_weight, value_weight, out_weight, norm2_gain, gate_weight, up_weight, down_weight)))
    picked = lax.optimization_barrier(jnp.sum(jnp.where(source_id[:, None] == jnp.arange(SOURCES, dtype=jnp.int32)[None, :], source_counts[None, :], 0), axis=1))
    row_scale = 4.0 / jnp.sqrt(picked.astype(jnp.float32))

    def one_row(totals, item):
        row, cot_row, scale = item
        result, pull = jax.vjp(layer, params, row)
        grads, row_grad = pull(cot_row * scale)
        return (jax.tree.map(jnp.add, totals, grads), (result.astype(jnp.bfloat16), row_grad))
    zeros = jax.tree.map(jnp.zeros_like, params)
    totals, outputs = lax.scan(one_row, zeros, (hidden_in.astype(jnp.float32), cotangent.astype(jnp.float32), row_scale))
    layer_out, grad_in = outputs
    return (layer_out, grad_in, totals[0], totals[1], totals[2], totals[3], totals[4], totals[5], totals[6], totals[7], totals[8])
```

```python
import math

import jax
import jax.numpy as jnp
import numpy as np
from jax import lax
from jax.sharding import Mesh, PartitionSpec as P

FEAT = 16
HEAD_V = 128
PAD_FF = 768
ATT_W = 640

norm_eps = 1e-05
AXES = ("zlo", "x", "core", "y", "zhi")
DP = ("zlo", "x", "core")
SEQ = ("y", "zhi")
TOKENS = ("y", "core")
COLUMNS = ("core", "y")
CHIPS = ("zhi", "zlo", "x")


def taylor(inputs):
    inner = inputs.shape[-1]
    lead = inputs.shape[:-1]
    first = inputs / inner**0.25
    second = (inputs[..., :, None] * inputs[..., None, :]).reshape(
        lead + (inner * inner,)
    ) / math.sqrt(2.0 * inner)
    return jnp.concatenate([jnp.ones(lead + (1,), jnp.float32), first, second], axis=-1)


def dot(left, right):
    return jnp.dot(left, right, preferred_element_type=jnp.float32)


def contract_rows(left, right):
    return lax.dot_general(
        left, right, (((0,), (0,)), ((), ())), preferred_element_type=jnp.float32
    )


def contract_cols(left, right):
    return lax.dot_general(
        left, right, (((1,), (1,)), ((), ())), preferred_element_type=jnp.float32
    )


def norm_back(grad_normed, inputs, inverse, gain):
    unit = inputs * inverse
    scaled = grad_normed * gain
    grad_gain = jnp.sum(grad_normed * unit, axis=0)
    grad_inputs = inverse * (scaled - unit * jnp.mean(scaled * unit, axis=-1, keepdims=True))
    return (grad_inputs, grad_gain)


def causal_mask(toks):
    return jnp.arange(toks)[:, None] >= jnp.arange(toks)[None, :]


def attend(feat_q, feat_k, values):
    causal = causal_mask(feat_q.shape[0])
    scores = jnp.einsum("thf,shf->hts", feat_q, feat_k, preferred_element_type=jnp.float32)
    scores = jnp.where(causal, scores, 0.0)
    numer = jnp.einsum("hts,shv->thv", scores, values.astype(jnp.float32))
    denom = jnp.sum(scores, axis=-1).T
    return (scores, denom, numer / denom[..., None])


def attend_back(grad_mixed, scores, denom, mixed, feat_q, feat_k, values):
    causal = causal_mask(feat_q.shape[0])
    grad_numer = grad_mixed / denom[..., None]
    grad_denom = -jnp.sum(grad_mixed * mixed, axis=-1) / denom
    query_wide = feat_q.astype(jnp.float32)
    key_wide = feat_k.astype(jnp.float32)
    values_wide = values.astype(jnp.float32)
    grad_scores = jnp.einsum("thv,shv->hts", grad_numer, values_wide)
    grad_scores = jnp.where(causal, grad_scores + grad_denom.T[..., None], 0.0)
    grad_feat_q = jnp.einsum("hts,shf->thf", grad_scores, key_wide)
    grad_feat_k = jnp.einsum("hts,thf->shf", grad_scores, query_wide)
    grad_values = jnp.einsum("hts,thv->shv", scores, grad_numer)
    return (grad_feat_q, grad_feat_k, grad_values)


def feature_back(query, keys, grad_feat_q, grad_feat_k, count):
    unused_q, pull_query = jax.vjp(taylor, query)
    grad_q = pull_query(grad_feat_q)[0].astype(jnp.bfloat16).reshape(count, -1)
    unused_k, pull_keys = jax.vjp(taylor, keys)
    grad_k = pull_keys(grad_feat_k)[0].astype(jnp.bfloat16).reshape(count, -1)
    return (grad_q, grad_k)


def row_scale(source_id, source_counts):
    picked = jnp.sum(
        jnp.where(
            source_id[:, None] == jnp.arange(source_counts.shape[0], dtype=jnp.int32)[None, :],
            source_counts[None, :],
            0,
        ),
        axis=1,
    )
    return 4.0 / jnp.sqrt(picked.astype(jnp.float32))


def lane_order(back):
    at = np.arange(256)
    to = (at // 16 % 2) * 128 + (at // 32) * 16 + at % 16
    hot = np.zeros((256, 256), np.float32)
    hot[at, to] = 1.0
    return jnp.asarray(hot.T if back else hot, jnp.bfloat16)


def reorder(array, hot, back):
    count, width = array.shape
    runs = width // 256
    if back:
        array = jnp.swapaxes(array.reshape(count, 2, runs, 128), 1, 2)
    moved = dot(array.reshape(count * runs, 256), hot).astype(jnp.bfloat16)
    if not back:
        moved = jnp.swapaxes(moved.reshape(count, runs, 2, 128), 1, 2)
    return moved.reshape(count, width)


def swap(array):
    return lax.ppermute(array, ("core", "zhi"), [(0, 0), (1, 2), (2, 1), (3, 3)])


def whole_row(piece):
    return lax.all_gather(piece, TOKENS, axis=0, tiled=True)


def own_rows(pairs):
    total = None
    for left, right in pairs:
        part = contract_cols(left, right)
        total = part if total is None else total + part
    return lax.psum_scatter(
        total.astype(jnp.bfloat16), TOKENS, scatter_dimension=0, tiled=True
    ).astype(jnp.float32)


def split_columns(weight, pad):
    rows, width = weight.shape
    cut = weight.reshape(rows, 8, width // 8)
    return jnp.pad(cut, ((0, 0), (0, 0), (0, pad)))


def body(
    hidden_in,
    norm1_gain,
    query_weight,
    key_weight,
    value_weight,
    out_weight,
    norm2_gain,
    gate_weight,
    up_weight,
    down_weight,
    cotangent,
    source_id,
    source_counts,
):
    rows, toks, width = hidden_in.shape
    ff_here = gate_weight.shape[1] // 8
    pad_ff = PAD_FF - ff_here
    depth = norm1_gain.shape[0]
    gains = jnp.stack((norm1_gain, norm2_gain), axis=1)[:, None, :]
    gains = jnp.broadcast_to(gains, (depth, 8, 2))
    pack_att = jnp.concatenate(
        (
            split_columns(value_weight, 0),
            split_columns(out_weight, 0),
            split_columns(query_weight, 0),
            split_columns(key_weight, 0),
            jnp.pad(gains, ((0, 0), (0, 0), (0, 62))),
        ),
        axis=2,
    )
    pack_mlp = jnp.concatenate(
        (
            split_columns(gate_weight, pad_ff),
            split_columns(up_weight, pad_ff),
            split_columns(down_weight, pad_ff),
        ),
        axis=2,
    )
    pack = jnp.swapaxes(jnp.concatenate((pack_att, pack_mlp), axis=2), 0, 1)
    pack = lax.all_to_all(pack, COLUMNS, split_axis=0, concat_axis=0, tiled=True)
    pack = pack.reshape(8 * depth, -1)
    att = lax.all_gather(pack[:, :ATT_W], CHIPS, axis=0, tiled=True)
    mlp = lax.all_gather(pack[:, ATT_W:], CHIPS, axis=0, tiled=True)
    w_value, w_out = att[:, :256], att[:, 256:512]
    w_query, w_key = att[:, 512:544], att[:, 544:576]
    norm1 = att[:, 576].astype(jnp.float32)
    norm2 = att[:, 577].astype(jnp.float32)
    w_gate, w_up, w_down = mlp[:, :PAD_FF], mlp[:, PAD_FF : 2 * PAD_FF], mlp[:, 2 * PAD_FF :]

    forth, back = lane_order(False), lane_order(True)
    raw = swap(reorder(hidden_in.reshape(toks, width), forth, False))
    scale = row_scale(source_id, source_counts)
    top = (cotangent.astype(jnp.float32) * scale[:, None, None]).reshape(toks, width)
    top_low = swap(reorder(top.astype(jnp.bfloat16), forth, False))
    grad_top = top_low.astype(jnp.float32)

    inputs = raw.astype(jnp.float32)
    inverse1 = lax.rsqrt(jnp.mean(inputs * inputs, axis=-1, keepdims=True) + norm_eps)
    normed = whole_row((inputs * inverse1 * norm1).astype(jnp.bfloat16))
    length = normed.shape[0]
    heads_here = w_query.shape[1] // FEAT
    query = dot(normed, w_query).reshape(length, heads_here, FEAT)
    keys = dot(normed, w_key).reshape(length, heads_here, FEAT)
    values = dot(normed, w_value).astype(jnp.bfloat16).reshape(length, heads_here, HEAD_V)
    feat_q = taylor(query).astype(jnp.bfloat16)
    feat_k = taylor(keys).astype(jnp.bfloat16)
    scores, denom, mixed = attend(feat_q, feat_k, values)
    attended = mixed.astype(jnp.bfloat16).reshape(length, heads_here * HEAD_V)
    middle = inputs + own_rows(((attended, w_out),))
    inverse2 = lax.rsqrt(jnp.mean(middle * middle, axis=-1, keepdims=True) + norm_eps)
    normed2 = whole_row((middle * inverse2 * norm2).astype(jnp.bfloat16))
    grad_low = whole_row(top_low)
    gate = dot(normed2, w_gate)
    upward = dot(normed2, w_up)
    sigma = jax.nn.sigmoid(gate)
    hidden = (gate * sigma * upward).astype(jnp.bfloat16)
    grad_down = contract_rows(grad_low, hidden).astype(jnp.bfloat16)
    grad_hidden = dot(grad_low, w_down)
    gate_act = (grad_hidden * upward * sigma * (1.0 + gate * (1.0 - sigma))).astype(jnp.bfloat16)
    up_act = (grad_hidden * gate * sigma).astype(jnp.bfloat16)
    grad_normed2 = own_rows(((gate_act, w_gate), (up_act, w_up)))
    layer_out = (middle + own_rows(((hidden, w_down),))).astype(jnp.bfloat16)
    grad_gate = contract_rows(normed2, gate_act).astype(jnp.bfloat16)
    grad_up = contract_rows(normed2, up_act).astype(jnp.bfloat16)
    grad_mid_norm, grad_norm2 = norm_back(grad_normed2, middle, inverse2, norm2)
    grad_middle = grad_top + grad_mid_norm
    middle_low = whole_row(grad_middle.astype(jnp.bfloat16))
    grads_mlp = lax.psum_scatter(
        jnp.concatenate((grad_gate, grad_up, grad_down), axis=1),
        CHIPS,
        scatter_dimension=0,
        tiled=True,
    )
    grad_out = contract_rows(middle_low, attended).astype(jnp.bfloat16)
    grad_mixed = dot(middle_low, w_out).reshape(length, heads_here, HEAD_V)
    grad_feat_q, grad_feat_k, grad_values = attend_back(
        grad_mixed, scores, denom, mixed, feat_q, feat_k, values
    )
    grad_values = grad_values.astype(jnp.bfloat16).reshape(length, heads_here * HEAD_V)
    grad_q, grad_k = feature_back(query, keys, grad_feat_q, grad_feat_k, length)
    grad_query = contract_rows(normed, grad_q).astype(jnp.bfloat16)
    grad_key = contract_rows(normed, grad_k).astype(jnp.bfloat16)
    grad_value = contract_rows(normed, grad_values).astype(jnp.bfloat16)
    grad_normed = own_rows(((grad_q, w_query), (grad_k, w_key), (grad_values, w_value)))
    grad_in_norm, grad_norm1 = norm_back(grad_normed, inputs, inverse1, norm1)
    grad_in = (grad_middle + grad_in_norm).astype(jnp.bfloat16)
    grad_pair = jnp.stack((grad_norm1, grad_norm2), axis=1).astype(jnp.bfloat16)
    grads_att = lax.psum_scatter(
        jnp.concatenate(
            (grad_value, grad_out, grad_query, grad_key, jnp.pad(grad_pair, ((0, 0), (0, 62)))),
            axis=1,
        ),
        CHIPS,
        scatter_dimension=0,
        tiled=True,
    )
    summed = jnp.concatenate((grads_att, grads_mlp), axis=1).reshape(8, depth, -1)
    summed = lax.all_to_all(summed, COLUMNS, split_axis=0, concat_axis=0, tiled=True)
    summed = jnp.swapaxes(summed, 0, 1).astype(jnp.float32)

    def joined(start, size):
        return summed[:, :, start : start + size].reshape(depth, 8 * size)

    pair = jnp.sum(summed[:, :, 576:578], axis=1)
    layer_out = reorder(swap(layer_out), back, True).reshape(rows, toks, width)
    grad_in = reorder(swap(grad_in), back, True).astype(jnp.float32).reshape(rows, toks, width)
    return (
        layer_out,
        grad_in,
        pair[:, 0],
        joined(512, 32),
        joined(544, 32),
        joined(0, 256),
        joined(256, 256),
        pair[:, 1],
        joined(ATT_W, ff_here),
        joined(ATT_W + PAD_FF, ff_here),
        joined(ATT_W + 2 * PAD_FF, ff_here),
    )


def solution(mesh):
    zlo, chips_x, cores, chips_y, zhi = 2, 4, 2, 4, 2
    whole = Mesh(mesh.devices.reshape(zlo, chips_x, cores, chips_y, zhi), AXES)
    weight = P(AXES, None)
    gain = P(AXES)
    tokens = P(DP, SEQ, None)
    return jax.shard_map(
        body,
        mesh=whole,
        in_specs=(
            tokens,
            gain,
            weight,
            weight,
            weight,
            weight,
            gain,
            weight,
            weight,
            weight,
            tokens,
            P(DP),
            P(),
        ),
        out_specs=(
            tokens,
            tokens,
            gain,
            weight,
            weight,
            weight,
            weight,
            gain,
            weight,
            weight,
            weight,
        ),
        check_vma=False,
    )
```

```python
import math

import jax
import jax.numpy as jnp
import numpy as np
from jax import lax
from jax.experimental import pallas as pl
from jax.experimental.pallas import tpu as pltpu
from jax.sharding import Mesh, PartitionSpec as P

FEAT = 16
HEAD_V = 128
PAD_FF = 768
ATT_W = 640

norm_eps = 1e-05
AXES = ("zlo", "x", "core", "y", "zhi")
DP = ("zlo", "x", "core")
SEQ = ("y", "zhi")
TOKENS = ("y", "core")
COLUMNS = ("core", "y")
CHIPS = ("zhi", "zlo", "x")


def taylor(inputs):
    inner = inputs.shape[-1]
    lead = inputs.shape[:-1]
    first = inputs / inner**0.25
    second = (inputs[..., :, None] * inputs[..., None, :]).reshape(
        lead + (inner * inner,)
    ) / math.sqrt(2.0 * inner)
    return jnp.concatenate([jnp.ones(lead + (1,), jnp.float32), first, second], axis=-1)


def dot(left, right):
    return jnp.dot(left, right, preferred_element_type=jnp.float32)


def contract_rows(left, right):
    return lax.dot_general(
        left, right, (((0,), (0,)), ((), ())), preferred_element_type=jnp.float32
    )


def contract_cols(left, right):
    return lax.dot_general(
        left, right, (((1,), (1,)), ((), ())), preferred_element_type=jnp.float32
    )


def causal_mask(toks):
    return jnp.arange(toks)[:, None] >= jnp.arange(toks)[None, :]


def attend(feat_q, feat_k, values):
    causal = causal_mask(feat_q.shape[0])
    scores = jnp.einsum("thf,shf->hts", feat_q, feat_k, preferred_element_type=jnp.float32)
    scores = jnp.where(causal, scores, 0.0)
    numer = jnp.einsum("hts,shv->thv", scores, values.astype(jnp.float32))
    denom = jnp.sum(scores, axis=-1).T
    return (scores, denom, numer / denom[..., None])


def attend_back(grad_mixed, scores, denom, mixed, feat_q, feat_k, values):
    causal = causal_mask(feat_q.shape[0])
    grad_numer = grad_mixed / denom[..., None]
    grad_denom = -jnp.sum(grad_mixed * mixed, axis=-1) / denom
    query_wide = feat_q.astype(jnp.float32)
    key_wide = feat_k.astype(jnp.float32)
    values_wide = values.astype(jnp.float32)
    grad_scores = jnp.einsum("thv,shv->hts", grad_numer, values_wide)
    grad_scores = jnp.where(causal, grad_scores + grad_denom.T[..., None], 0.0)
    grad_feat_q = jnp.einsum("hts,shf->thf", grad_scores, key_wide)
    grad_feat_k = jnp.einsum("hts,thf->shf", grad_scores, query_wide)
    grad_values = jnp.einsum("hts,thv->shv", scores, grad_numer)
    return (grad_feat_q, grad_feat_k, grad_values)


def feature_back(query, keys, grad_feat_q, grad_feat_k, count):
    unused_q, pull_query = jax.vjp(taylor, query)
    grad_q = pull_query(grad_feat_q)[0].astype(jnp.bfloat16).reshape(count, -1)
    unused_k, pull_keys = jax.vjp(taylor, keys)
    grad_k = pull_keys(grad_feat_k)[0].astype(jnp.bfloat16).reshape(count, -1)
    return (grad_q, grad_k)


def row_scale(source_id, source_counts):
    picked = jnp.sum(
        jnp.where(
            source_id[:, None] == jnp.arange(source_counts.shape[0], dtype=jnp.int32)[None, :],
            source_counts[None, :],
            0,
        ),
        axis=1,
    )
    return 4.0 / jnp.sqrt(picked.astype(jnp.float32))


def lane_order(back):
    at = np.arange(256)
    to = (at // 16 % 2) * 128 + (at // 32) * 16 + at % 16
    hot = np.zeros((256, 256), np.float32)
    hot[at, to] = 1.0
    return jnp.asarray(hot.T if back else hot, jnp.bfloat16)


def reorder(array, hot, back):
    count, width = array.shape
    runs = width // 256
    if back:
        array = jnp.swapaxes(array.reshape(count, 2, runs, 128), 1, 2)
    moved = dot(array.reshape(count * runs, 256), hot).astype(jnp.bfloat16)
    if not back:
        moved = jnp.swapaxes(moved.reshape(count, runs, 2, 128), 1, 2)
    return moved.reshape(count, width)


def swap(array):
    return lax.ppermute(array, ("core", "zhi"), [(0, 0), (1, 2), (2, 1), (3, 3)])


def whole_row(piece):
    return lax.all_gather(piece, TOKENS, axis=0, tiled=True)


def own_rows(pairs):
    total = None
    for left, right in pairs:
        part = contract_cols(left, right)
        total = part if total is None else total + part
    return lax.psum_scatter(
        total.astype(jnp.bfloat16), TOKENS, scatter_dimension=0, tiled=True
    ).astype(jnp.float32)


MESH = pl.DeviceIdType.MESH
VMEM_LIMIT = 52 * 2**20
PIECES = 4
TILE = 256


def place():
    z = lax.axis_index("zhi") * 2 + lax.axis_index("zlo")
    return lax.axis_index("x"), lax.axis_index("y"), z, lax.axis_index("core")


def at_y(y):
    return {"y": lax.rem(y + 8, 4)}


def at_core(core):
    return {"core": core}


def at_xz(x, z):
    x, z = lax.rem(x + 8, 4), lax.rem(z + 8, 4)
    return {"x": x, "zhi": z // 2, "zlo": lax.rem(z, 2)}


def greet(devices):
    barrier = pltpu.get_barrier_semaphore()
    for device in devices:
        pl.semaphore_signal(barrier, inc=1, device_id=device, device_id_type=MESH)
    pl.semaphore_wait(barrier, len(devices))


class Copies:
    def __init__(self, send, recv):
        self.send, self.recv, self.used, self.open = send, recv, 0, []

    def start(self, src, dst, device):
        copy = pltpu.make_async_remote_copy(
            src_ref=src,
            dst_ref=dst,
            send_sem=self.send.at[self.used],
            recv_sem=self.recv.at[self.used],
            device_id=device,
            device_id_type=MESH,
        )
        copy.start()
        self.used += 1
        self.open.append(copy)
        return copy

    def local(self, src, dst):
        copy = pltpu.make_async_copy(src, dst, self.send.at[self.used])
        copy.start()
        self.used += 1
        return copy

    def finish(self):
        for copy in self.open:
            copy.wait_send()


def way(piece):
    return 1 if piece % 2 == 0 else -1


def rows_of(piece, rows):
    size = rows // PIECES
    return pl.ds(piece * size, size)


def gather_ring(copies, to, mine, full, block_of, me, rows):
    sent = {}
    for piece in range(PIECES):
        for step in (way(piece), -way(piece)):
            part = rows_of(piece, rows)
            sent[step, piece] = copies.start(
                mine.at[part], full.at[block_of(me), part], to(me + step)
            )
    onward = {}

    def forward():
        for piece in range(PIECES):
            step = way(piece)
            sent[step, piece].wait_recv()
            here = full.at[block_of(me - step), rows_of(piece, rows)]
            onward[piece] = copies.start(here, here, to(me + step))

    def near():
        for piece in range(PIECES):
            sent[-way(piece), piece].wait_recv()

    def far():
        for piece in range(PIECES):
            onward[piece].wait_recv()

    return forward, near, far


def gather_tokens(copies, mine, full, y, core):
    rows = mine.shape[0]
    other = at_core(1 - core)

    def block_of(index):
        return lax.rem(index + 8, 4) * 2 + core

    own = copies.local(mine, full.at[block_of(y)])
    shared = [copies.start(mine, full.at[block_of(y)], other)]
    forward, near, far = gather_ring(copies, at_y, mine, full, block_of, y, rows)

    def finish():
        forward()
        near()
        for step in (1, -1):
            here = full.at[block_of(y + step)]
            shared.append(copies.start(here, here, other))
        far()
        here = full.at[block_of(y + 2)]
        shared.append(copies.start(here, here, other))
        for copy in shared:
            copy.wait_recv()
        own.wait()

    return finish


def gather_plane(copies, mine, full, x, z, core):
    rows = mine.shape[0]

    def block(a, b):
        a, b = lax.rem(a + 8, 4), lax.rem(b + 8, 4)
        return jnp.where(core == 0, 4 * b + a, 4 * a + b)

    first, second = jnp.where(core == 0, x, z), jnp.where(core == 0, z, x)

    def to_first(index):
        return at_xz(jnp.where(core == 0, index, x), jnp.where(core == 0, z, index))

    def to_second(index):
        return at_xz(jnp.where(core == 0, x, index), jnp.where(core == 0, index, z))

    own = copies.local(mine, full.at[block(first, second)])
    forward, near, far = gather_ring(
        copies, to_first, mine, full, lambda a: block(a, second), first, rows
    )

    def onto_second(a, source):
        return gather_ring(
            copies, to_second, source, full, lambda b: block(a, b), second, rows
        )

    def finish():
        rings = [onto_second(first, mine)]
        forward()
        near()
        for step in (1, -1):
            rings.append(onto_second(first + step, full.at[block(first + step, second)]))
        rings[0][0]()
        far()
        rings.append(onto_second(first + 2, full.at[block(first + 2, second)]))
        for ring in rings[1:]:
            ring[0]()
        for ring in rings:
            ring[1]()
            ring[2]()
        own.wait()

    return finish


def reduce_ring(copies, to, me, part, out, got, rows, step_rows=16):
    size = rows // PIECES

    def each(piece, act):
        @pl.loop(0, size // step_rows)
        def _(at):
            act(pl.ds(piece * size + at * step_rows, step_rows))

    sent = {}
    for piece in range(PIECES):
        step = way(piece)
        span = rows_of(piece, rows)

        def far(span):
            out[0, span] = part(2, span).astype(jnp.bfloat16)

        each(piece, far)
        sent[0, piece] = copies.start(out.at[0, span], got.at[0, span], to(me + step))
    for piece in range(PIECES):
        step = way(piece)
        span = rows_of(piece, rows)

        def near(span):
            out[1, span] = part(-step, span).astype(jnp.bfloat16)

        each(piece, near)
        sent[1, piece] = copies.start(out.at[1, span], got.at[1, span], to(me - step))
    for piece in range(PIECES):
        step = way(piece)
        span = rows_of(piece, rows)
        sent[0, piece].wait_recv()

        def onward(span):
            out[2, span] = (part(step, span) + got[0, span].astype(jnp.float32)).astype(jnp.bfloat16)

        each(piece, onward)
        sent[2, piece] = copies.start(out.at[2, span], got.at[2, span], to(me + step))

    def arrive(piece):
        sent[1, piece].wait_recv()
        sent[2, piece].wait_recv()

    def total(span):
        return part(0, span) + got[1, span].astype(jnp.float32) + got[2, span].astype(jnp.float32)

    return arrive, total


def spread_kernel(att, mlp, raw, top, att_out, mlp_out, raw_out, top_out, send, recv):
    unused_x, y, z, core = place()
    zhi = z // 2
    copies = Copies(send, recv)
    others = [(dc, dy) for dc in (0, 1) for dy in range(4) if (dc, dy) != (0, 0)]

    def there(dc, dy):
        return lax.rem(core + dc, 2), lax.rem(y + dy, 4)

    barrier = pltpu.get_barrier_semaphore()
    for dc, dy in others:
        to_core, to_y = there(dc, dy)
        pl.semaphore_signal(barrier, inc=1, device_id={"core": to_core, "y": to_y}, device_id_type=MESH)
    partner = {"core": 1 - core, "zhi": 1 - zhi}

    @pl.when(core != zhi)
    def _():
        pl.semaphore_signal(barrier, inc=1, device_id=partner, device_id_type=MESH)

    pl.semaphore_wait(barrier, len(others) + jnp.where(core != zhi, 1, 0))
    me = core * 4 + y
    local = [copies.local(att.at[me], att_out.at[me]), copies.local(mlp.at[me], mlp_out.at[me])]
    pairs = ((raw, raw_out), (top, top_out))
    sems = []
    for _ in pairs:
        sems.append(copies.used)
        copies.used += 1

    def over(pair, sem):
        return pltpu.make_async_remote_copy(
            src_ref=pair[0],
            dst_ref=pair[1],
            send_sem=send.at[sem],
            recv_sem=recv.at[sem],
            device_id=partner,
            device_id_type=MESH,
        )

    def stay(pair, sem):
        return pltpu.make_async_copy(pair[0], pair[1], send.at[sem])

    @pl.when(core != zhi)
    def _():
        for pair, sem in zip(pairs, sems):
            over(pair, sem).start()

    @pl.when(core == zhi)
    def _():
        for pair, sem in zip(pairs, sems):
            stay(pair, sem).start()

    for dc, dy in others:
        to_core, to_y = there(dc, dy)
        to = {"core": to_core, "y": to_y}
        copies.start(att.at[to_core * 4 + to_y], att_out.at[me], to)
        copies.start(mlp.at[to_core * 4 + to_y], mlp_out.at[me], to)
    for copy in copies.open:
        copy.wait_recv()
    copies.finish()
    for copy in local:
        copy.wait()

    @pl.when(core != zhi)
    def _():
        for pair, sem in zip(pairs, sems):
            over(pair, sem).wait()

    @pl.when(core == zhi)
    def _():
        for pair, sem in zip(pairs, sems):
            stay(pair, sem).wait()


def first_kernel(raw, att, raw_full, att_full, send, recv):
    x, y, z, core = place()
    greet(
        [at_y(y + 1), at_y(y - 1), at_core(1 - core)]
        + [at_xz(x + 1, z), at_xz(x - 1, z), at_xz(x, z + 1), at_xz(x, z - 1)]
    )
    copies = Copies(send, recv)
    tokens = gather_tokens(copies, raw, raw_full, y, core)
    plane = gather_plane(copies, att, att_full, x, z, core)
    tokens()
    plane()
    copies.finish()


def tile_parts(lefts, rights, block, core, mine, theirs):
    rows = pl.ds(pl.multiple_of(block * 256, 256), 256)

    @pl.loop(0, mine.shape[-1] // TILE)
    def _(tile):
        columns = pl.ds(pl.multiple_of(tile * TILE, TILE), TILE)
        total = None
        for left, (right, lanes) in zip(lefts, rights):
            term = lax.dot_general(
                left[rows, :],
                right[columns, lanes],
                (((1,), (1,)), ((), ())),
                preferred_element_type=jnp.float32,
            )
            total = term if total is None else total + term
        low, high = total[:128], total[128:]
        mine[:, columns] = jnp.where(core == 0, low, high)
        theirs[:, columns] = jnp.where(core == 0, high, low).astype(jnp.bfloat16)


def reduce_tokens(copies, lefts, rights, y, core, own, sib, got_sib, out, got):
    shared = {}
    for k in (2, 1, 3, 0):
        tile_parts(lefts, rights, lax.rem(y + k, 4), core, own.at[k], sib.at[k])
        shared[k] = copies.start(sib.at[k], got_sib.at[k], at_core(1 - core))
    for k in (2, 1, 3, 0):
        shared[k].wait_recv()

    def part(k, span):
        k = k % 4
        return own[k, span] + got_sib[k, span].astype(jnp.float32)

    return reduce_ring(copies, at_y, y, part, out, got, own.shape[1])


def greet_tokens(y, core):
    greet([at_y(y + 1), at_y(y - 1), at_core(1 - core)])


def middle_kernel(
    attended, att, raw, gain, middle, normed2, own, sib, got_sib, out, got, low, send, recv
):
    unused_x, y, unused_z, core = place()
    greet_tokens(y, core)
    copies = Copies(send, recv)
    arrive, total = reduce_tokens(
        copies, [attended], [(att, slice(256, 512))], y, core, own, sib, got_sib, out, got
    )
    for piece in range(PIECES):
        arrive(piece)

    @pl.loop(0, 128 // 16)
    def _(at):
        span = pl.ds(at * 16, 16)
        value = raw[span].astype(jnp.float32) + total(span)
        middle[span] = value
        inverse = lax.rsqrt(jnp.mean(value * value, axis=-1, keepdims=True) + norm_eps)
        low[span] = (value * inverse * gain[...]).astype(jnp.bfloat16)

    finish = gather_tokens(copies, low, normed2, y, core)
    finish()
    copies.finish()


def norm_back_rows(grad, value, gain):
    inverse = lax.rsqrt(jnp.mean(value * value, axis=-1, keepdims=True) + norm_eps)
    unit = value * inverse
    scaled = grad * gain
    moved = inverse * (scaled - unit * jnp.mean(scaled * unit, axis=-1, keepdims=True))
    return moved, grad * unit


def eight(terms):
    return terms[:8] + terms[8:]


def middle_back_kernel(
    gate_act,
    up_act,
    mlp,
    middle,
    top,
    gain,
    grad_middle,
    grad_gain,
    middle_low,
    own,
    sib,
    got_sib,
    out,
    got,
    low,
    send,
    recv,
):
    unused_x, y, unused_z, core = place()
    greet_tokens(y, core)
    copies = Copies(send, recv)
    arrive, total = reduce_tokens(
        copies,
        [gate_act, up_act],
        [(mlp, slice(0, PAD_FF)), (mlp, slice(PAD_FF, 2 * PAD_FF))],
        y,
        core,
        own,
        sib,
        got_sib,
        out,
        got,
    )
    for piece in range(PIECES):
        arrive(piece)
    grad_gain[...] = jnp.zeros_like(grad_gain)

    @pl.loop(0, 128 // 16)
    def _(at):
        span = pl.ds(at * 16, 16)
        moved, terms = norm_back_rows(total(span), middle[span], gain[...])
        grad_gain[...] += eight(terms)
        value = top[span].astype(jnp.float32) + moved
        grad_middle[span] = value
        low[span] = value.astype(jnp.bfloat16)

    finish = gather_tokens(copies, low, middle_low, y, core)
    finish()
    copies.finish()


def input_back_kernel(
    grad_qk, grad_values, att, raw, grad_middle, gain, grad_in, grad_gain, own, sib, got_sib, out, got, send, recv
):
    unused_x, y, unused_z, core = place()
    greet_tokens(y, core)
    copies = Copies(send, recv)
    arrive, total = reduce_tokens(
        copies,
        [grad_values, grad_qk],
        [(att, slice(0, 256)), (att, slice(512, 640))],
        y,
        core,
        own,
        sib,
        got_sib,
        out,
        got,
    )
    for piece in range(PIECES):
        arrive(piece)
    grad_gain[...] = jnp.zeros_like(grad_gain)

    @pl.loop(0, 128 // 16)
    def _(at):
        span = pl.ds(at * 16, 16)
        moved, terms = norm_back_rows(total(span), raw[span].astype(jnp.float32), gain[...])
        grad_gain[...] += eight(terms)
        grad_in[span] = (grad_middle[span] + moved).astype(jnp.bfloat16)

    copies.finish()


def reduce_plane(copies, parts, x, z, core, out1, got1, mid, out2, got2):
    rows = parts.shape[1]

    def block(a, b):
        a, b = lax.rem(a + 8, 4), lax.rem(b + 8, 4)
        return jnp.where(core == 0, 4 * b + a, 4 * a + b)

    last, first = jnp.where(core == 0, x, z), jnp.where(core == 0, z, x)

    def to_last(index):
        return at_xz(jnp.where(core == 0, index, x), jnp.where(core == 0, z, index))

    def to_first(index):
        return at_xz(jnp.where(core == 0, x, index), jnp.where(core == 0, index, z))

    rings = {}
    for k in (2, 1, 3, 0):

        def part(step, span, k=k):
            return parts[block(last + k, first + step), span].astype(jnp.float32)

        rings[k] = reduce_ring(copies, to_first, first, part, out1.at[k], got1.at[k], rows, rows // PIECES)
    for k in (2, 1, 3, 0):
        arrive, total = rings[k]
        for piece in range(PIECES):
            arrive(piece)
            span = rows_of(piece, rows)
            mid[k, span] = total(span)

    def part2(step, span):
        return mid[step % 4, span]

    return reduce_ring(copies, to_last, last, part2, out2, got2, rows, rows // PIECES)


def last_kernel(
    att, mlp, att_out, mlp_out, out1, got1, mid, out2, got2, summed, send, recv
):
    x, y, z, core = place()
    others = [(dc, dy) for dc in (0, 1) for dy in range(4) if (dc, dy) != (0, 0)]

    def there(dc, dy):
        return lax.rem(core + dc, 2), lax.rem(y + dy, 4)

    greet(
        [{"core": there(dc, dy)[0], "y": there(dc, dy)[1]} for dc, dy in others]
        + [at_xz(x + 1, z), at_xz(x - 1, z), at_xz(x, z + 1), at_xz(x, z - 1)]
    )
    copies = Copies(send, recv)
    me = core * 4 + y
    local = [copies.local(mlp.at[me], mlp_out.at[me])]
    back = []
    for dc, dy in others:
        to_core, to_y = there(dc, dy)
        to = {"core": to_core, "y": to_y}
        back.append(copies.start(mlp.at[to_core * 4 + to_y], mlp_out.at[me], to))
    arrive, total = reduce_plane(copies, att, x, z, core, out1, got1, mid, out2, got2)
    size = summed.shape[0] * summed.shape[1] // PIECES
    for piece in range(PIECES):
        arrive(piece)
        for at in range(size // 16):
            summed[piece * (size // 16) + at] = total(pl.ds(piece * size + at * 16, 16)).astype(jnp.bfloat16)
    local.append(copies.local(summed.at[me], att_out.at[me]))
    for dc, dy in others:
        to_core, to_y = there(dc, dy)
        to = {"core": to_core, "y": to_y}
        back.append(copies.start(summed.at[to_core * 4 + to_y], att_out.at[me], to))
    for copy in back:
        copy.wait_recv()
    copies.finish()
    for copy in local:
        copy.wait()


def call(kernel, number, ins, in_spaces, outs, out_spaces, scratch, sems, cost):
    def spec(space):
        return pl.BlockSpec(memory_space=space)

    return pl.pallas_call(
        kernel,
        out_shape=[jax.ShapeDtypeStruct(shape, dtype) for shape, dtype in outs],
        in_specs=[spec(space) for space in in_spaces],
        out_specs=[spec(space) for space in out_spaces],
        scratch_shapes=list(scratch)
        + [pltpu.SemaphoreType.DMA((sems,)), pltpu.SemaphoreType.DMA((sems,))],
        compiler_params=pltpu.CompilerParams(
            collective_id=number, has_side_effects=True, vmem_limit_bytes=VMEM_LIMIT
        ),
        cost_estimate=pl.CostEstimate(flops=cost, bytes_accessed=64 * 2**20, transcendentals=0),
        name=kernel.__name__,
    )(*ins)


def ring_scratch(width):
    return [
        pltpu.VMEM((4, 128, width), jnp.float32),
        pltpu.VMEM((4, 128, width), jnp.bfloat16),
        pltpu.VMEM((4, 128, width), jnp.bfloat16),
        pltpu.VMEM((3, 128, width), jnp.bfloat16),
        pltpu.VMEM((3, 128, width), jnp.bfloat16),
    ]


def split_columns(weight, pad):
    rows, width = weight.shape
    cut = weight.reshape(rows, 8, width // 8)
    return jnp.pad(cut, ((0, 0), (0, 0), (0, pad)))


def body(
    hidden_in,
    norm1_gain,
    query_weight,
    key_weight,
    value_weight,
    out_weight,
    norm2_gain,
    gate_weight,
    up_weight,
    down_weight,
    cotangent,
    source_id,
    source_counts,
):
    rows, toks, width = hidden_in.shape
    ff_here = gate_weight.shape[1] // 8
    pad_ff = PAD_FF - ff_here
    depth = norm1_gain.shape[0]
    gains = jnp.stack((norm1_gain, norm2_gain), axis=1)[:, None, :]
    gains = jnp.broadcast_to(gains, (depth, 8, 2))
    pack_att = jnp.concatenate(
        (
            split_columns(value_weight, 0),
            split_columns(out_weight, 0),
            split_columns(query_weight, 0),
            split_columns(key_weight, 0),
            jnp.pad(gains, ((0, 0), (0, 0), (0, 62))),
        ),
        axis=2,
    )
    pack_mlp = jnp.concatenate(
        (
            split_columns(gate_weight, pad_ff),
            split_columns(up_weight, pad_ff),
            split_columns(down_weight, pad_ff),
        ),
        axis=2,
    )
    hbm, vmem = pl.ANY, pltpu.VMEM
    low_type, wide_type = jnp.bfloat16, jnp.float32
    forth, back = lane_order(False), lane_order(True)
    raw = reorder(hidden_in.reshape(toks, width), forth, False)
    scale = row_scale(source_id, source_counts)
    top = (cotangent.astype(jnp.float32) * scale[:, None, None]).reshape(toks, width)
    top = reorder(top.astype(jnp.bfloat16), forth, False)
    att, mlp, raw, top = call(
        spread_kernel,
        0,
        (jnp.swapaxes(pack_att, 0, 1), jnp.swapaxes(pack_mlp, 0, 1), raw, top),
        [hbm] * 4,
        [
            ((8, depth, ATT_W), low_type),
            ((8, depth, 3 * PAD_FF), low_type),
            ((toks, width), low_type),
            ((toks, width), low_type),
        ],
        [hbm] * 4,
        [],
        18,
        0,
    )
    mlp = lax.all_gather(mlp.reshape(8 * depth, 3 * PAD_FF), CHIPS, axis=0, tiled=True)
    grad_low = whole_row(top)
    raw_full, att = call(
        first_kernel,
        1,
        (raw, att.reshape(8 * depth, ATT_W)),
        [hbm] * 2,
        [((8, toks, width), low_type), ((16, 8 * depth, ATT_W), low_type)],
        [hbm] * 2,
        [],
        80,
        0,
    )
    length = 8 * toks
    raw_full = raw_full.reshape(length, width)
    att = att.reshape(width, ATT_W)
    w_value, w_out = att[:, :256], att[:, 256:512]
    w_query, w_key = att[:, 512:544], att[:, 544:576]
    gains = att[:, 576:578].astype(jnp.float32).T
    norm1, norm2 = gains[:1], gains[1:]
    w_gate, w_up, w_down = mlp[:, :PAD_FF], mlp[:, PAD_FF : 2 * PAD_FF], mlp[:, 2 * PAD_FF :]

    inputs = raw_full.astype(jnp.float32)
    inverse1 = lax.rsqrt(jnp.mean(inputs * inputs, axis=-1, keepdims=True) + norm_eps)
    normed = (inputs * inverse1 * norm1).astype(jnp.bfloat16)
    heads_here = w_query.shape[1] // FEAT
    query = dot(normed, w_query).reshape(length, heads_here, FEAT)
    keys = dot(normed, w_key).reshape(length, heads_here, FEAT)
    values = dot(normed, w_value).astype(jnp.bfloat16).reshape(length, heads_here, HEAD_V)
    feat_q = taylor(query).astype(jnp.bfloat16)
    feat_k = taylor(keys).astype(jnp.bfloat16)
    scores, denom, mixed = attend(feat_q, feat_k, values)
    attended = mixed.astype(jnp.bfloat16).reshape(length, heads_here * HEAD_V)
    middle, normed2 = call(
        middle_kernel,
        2,
        (attended, att, raw, norm2),
        [vmem] * 4,
        [((toks, width), wide_type), ((8, toks, width), low_type)],
        [vmem, hbm],
        ring_scratch(width) + [vmem((toks, width), low_type)],
        36,
        10**9,
    )
    normed2 = normed2.reshape(length, width)
    gate = dot(normed2, w_gate)
    upward = dot(normed2, w_up)
    sigma = jax.nn.sigmoid(gate)
    hidden = (gate * sigma * upward).astype(jnp.bfloat16)
    grad_hidden = dot(grad_low, w_down)
    gate_act = (grad_hidden * upward * sigma * (1.0 + gate * (1.0 - sigma))).astype(jnp.bfloat16)
    up_act = (grad_hidden * gate * sigma).astype(jnp.bfloat16)
    grad_middle, grad_norm2, middle_low = call(
        middle_back_kernel,
        3,
        (gate_act, up_act, mlp, middle, top, norm2),
        [vmem] * 6,
        [((toks, width), wide_type), ((8, width), wide_type), ((8, toks, width), low_type)],
        [vmem, vmem, hbm],
        ring_scratch(width) + [vmem((toks, width), low_type)],
        36,
        6 * 10**9,
    )
    middle_low = middle_low.reshape(length, width)
    layer_out = (middle + own_rows(((hidden, w_down),))).astype(jnp.bfloat16)
    grad_down = contract_rows(grad_low, hidden).astype(jnp.bfloat16)
    grad_gate = contract_rows(normed2, gate_act).astype(jnp.bfloat16)
    grad_up = contract_rows(normed2, up_act).astype(jnp.bfloat16)
    grads_mlp = lax.psum_scatter(
        jnp.concatenate((grad_gate, grad_up, grad_down), axis=1),
        CHIPS,
        scatter_dimension=0,
        tiled=True,
    )
    grad_out = contract_rows(middle_low, attended).astype(jnp.bfloat16)
    grad_mixed = dot(middle_low, w_out).reshape(length, heads_here, HEAD_V)
    grad_feat_q, grad_feat_k, grad_values = attend_back(
        grad_mixed, scores, denom, mixed, feat_q, feat_k, values
    )
    grad_values = grad_values.astype(jnp.bfloat16).reshape(length, heads_here * HEAD_V)
    grad_q, grad_k = feature_back(query, keys, grad_feat_q, grad_feat_k, length)
    grad_qk = jnp.pad(jnp.concatenate((grad_q, grad_k), axis=1), ((0, 0), (0, 64)))
    grad_in, grad_norm1 = call(
        input_back_kernel,
        4,
        (grad_qk, grad_values, att, raw, grad_middle, norm1),
        [vmem] * 6,
        [((toks, width), low_type), ((8, width), wide_type)],
        [vmem] * 2,
        ring_scratch(width),
        36,
        10**9,
    )
    grad_qk = contract_rows(normed, grad_qk)
    grad_value = contract_rows(normed, grad_values).astype(jnp.bfloat16)
    grad_pair = jnp.stack((jnp.sum(grad_norm1, axis=0), jnp.sum(grad_norm2, axis=0)), axis=1)
    grads_att = jnp.concatenate(
        (
            grad_value,
            grad_out,
            grad_qk[:, :64].astype(jnp.bfloat16),
            jnp.pad(grad_pair, ((0, 0), (0, 62))).astype(jnp.bfloat16),
        ),
        axis=1,
    )
    rows_here = 8 * depth
    grads_att, grads_mlp = call(
        last_kernel,
        5,
        (grads_att.reshape(16, rows_here, ATT_W), grads_mlp.reshape(8, depth, 3 * PAD_FF)),
        [vmem, hbm],
        [((8, depth, ATT_W), low_type), ((8, depth, 3 * PAD_FF), low_type)],
        [hbm] * 2,
        [
            vmem((4, 3, rows_here, ATT_W), low_type),
            vmem((4, 3, rows_here, ATT_W), low_type),
            vmem((4, rows_here, ATT_W), wide_type),
            vmem((3, rows_here, ATT_W), low_type),
            vmem((3, rows_here, ATT_W), low_type),
            vmem((8, depth, ATT_W), low_type),
        ],
        80,
        0,
    )
    att_sums = jnp.swapaxes(grads_att, 0, 1).astype(jnp.float32)
    mlp_sums = jnp.swapaxes(grads_mlp, 0, 1).astype(jnp.float32)

    def joined(sums, start, size):
        return sums[:, :, start : start + size].reshape(depth, 8 * size)

    pair = jnp.sum(att_sums[:, :, 576:578], axis=1)
    layer_out = reorder(swap(layer_out), back, True).reshape(rows, toks, width)
    grad_in = reorder(swap(grad_in), back, True).astype(jnp.float32).reshape(rows, toks, width)
    return (
        layer_out,
        grad_in,
        pair[:, 0],
        joined(att_sums, 512, 32),
        joined(att_sums, 544, 32),
        joined(att_sums, 0, 256),
        joined(att_sums, 256, 256),
        pair[:, 1],
        joined(mlp_sums, 0, ff_here),
        joined(mlp_sums, PAD_FF, ff_here),
        joined(mlp_sums, 2 * PAD_FF, ff_here),
    )


def solution(mesh):
    zlo, chips_x, cores, chips_y, zhi = 2, 4, 2, 4, 2
    whole = Mesh(mesh.devices.reshape(zlo, chips_x, cores, chips_y, zhi), AXES)
    weight = P(AXES, None)
    gain = P(AXES)
    tokens = P(DP, SEQ, None)
    return jax.shard_map(
        body,
        mesh=whole,
        in_specs=(
            tokens,
            gain,
            weight,
            weight,
            weight,
            weight,
            gain,
            weight,
            weight,
            weight,
            tokens,
            P(DP),
            P(),
        ),
        out_specs=(
            tokens,
            tokens,
            gain,
            weight,
            weight,
            weight,
            weight,
            gain,
            weight,
            weight,
            weight,
        ),
        check_vma=False,
    )
```

```python
import jax
import jax.numpy as jnp
import numpy as np
from jax import lax
from jax.experimental import pallas as pl
from jax.experimental.pallas import tpu as pltpu
from jax.sharding import Mesh, PartitionSpec as P

FEAT = 16
HEAD_V = 128
PAD_FF = 768
ATT_W = 640
QK_AT = slice(512, 640)
OUT_AT = slice(256, 512)
VALUE_AT = slice(0, 256)

norm_eps = 1e-05
AXES = ("zlo", "x", "core", "y", "zhi")
DP = ("zlo", "x", "core")
SEQ = ("y", "zhi")
CHIPS = ("zhi", "zlo", "x")

MESH = pl.DeviceIdType.MESH
VMEM_LIMIT = 61 * 2**20
PIECES = 4
TILE = 256
STEP = 16
BF16, F32 = jnp.bfloat16, jnp.float32


def row_scale(source_id, source_counts):
    picked = jnp.sum(
        jnp.where(
            source_id[:, None] == jnp.arange(source_counts.shape[0], dtype=jnp.int32)[None, :],
            source_counts[None, :],
            0,
        ),
        axis=1,
    )
    return 4.0 / jnp.sqrt(picked.astype(F32))


def lane_order(back):
    at = np.arange(256)
    to = (at // 16 % 2) * 128 + (at // 32) * 16 + at % 16
    hot = np.zeros((256, 256), np.float32)
    hot[at, to] = 1.0
    return jnp.asarray(hot.T if back else hot, BF16)


def place():
    z = lax.axis_index("zhi") * 2 + lax.axis_index("zlo")
    return lax.axis_index("x"), lax.axis_index("y"), z, lax.axis_index("core")


def around(index):
    return lax.rem(index + 8, 4)


def at_y(y):
    return {"y": around(y)}


def at_core(core):
    return {"core": core}


def at_xz(x, z):
    x, z = around(x), around(z)
    return {"x": x, "zhi": z // 2, "zlo": lax.rem(z, 2)}


def ring_peers(y, core):
    return [at_y(y + 1), at_y(y - 1), at_core(1 - core)]


def plane_peers(x, z):
    return [at_xz(x + 1, z), at_xz(x - 1, z), at_xz(x, z + 1), at_xz(x, z - 1)]


def group_peers(y, core):
    return [
        (lax.rem(core + dc, 2), lax.rem(y + dy, 4))
        for dc in (0, 1)
        for dy in range(4)
        if (dc, dy) != (0, 0)
    ]


def greet(devices, partner=None, swaps=None):
    barrier = pltpu.get_barrier_semaphore()
    for device in devices:
        pl.semaphore_signal(barrier, inc=1, device_id=device, device_id_type=MESH)
    count = len(devices)
    if partner is not None:

        @pl.when(swaps)
        def _():
            pl.semaphore_signal(barrier, inc=1, device_id=partner, device_id_type=MESH)

        count = count + jnp.where(swaps, 1, 0)
    pl.semaphore_wait(barrier, count)


class Copies:
    def __init__(self, send, recv):
        self.send, self.recv, self.used, self.open = send, recv, 0, []

    def start(self, src, dst, device):
        copy = pltpu.make_async_remote_copy(
            src_ref=src,
            dst_ref=dst,
            send_sem=self.send.at[self.used],
            recv_sem=self.recv.at[self.used],
            device_id=device,
            device_id_type=MESH,
        )
        copy.start()
        self.used += 1
        self.open.append(copy)
        return copy

    def local(self, src, dst):
        copy = pltpu.make_async_copy(src, dst, self.send.at[self.used])
        copy.start()
        self.used += 1
        return copy

    def swap(self, src, dst, partner, swaps):
        at = self.used
        self.used += 1

        def over():
            return pltpu.make_async_remote_copy(
                src_ref=src,
                dst_ref=dst,
                send_sem=self.send.at[at],
                recv_sem=self.recv.at[at],
                device_id=partner,
                device_id_type=MESH,
            )

        def stay():
            return pltpu.make_async_copy(src, dst, self.send.at[at])

        @pl.when(swaps)
        def _():
            over().start()

        @pl.when(jnp.logical_not(swaps))
        def _():
            stay().start()

        def wait():
            @pl.when(swaps)
            def _():
                over().wait()

            @pl.when(jnp.logical_not(swaps))
            def _():
                stay().wait()

        return wait

    def finish(self):
        for copy in self.open:
            copy.wait_send()


def way(piece):
    return 1 if piece % 2 == 0 else -1


def slab(ref, block, rows, piece=None):
    if piece is None:
        return ref.at[pl.ds(pl.multiple_of(block * rows, 128), rows)]
    size = rows // PIECES
    return ref.at[pl.ds(pl.multiple_of(block * rows + piece * size, 32), size)]


def row_steps(start, size, act, step=STEP):
    @pl.loop(0, size // step)
    def _(at):
        act(pl.ds(pl.multiple_of(start + at * step, step), step))


class GatherRing:
    def __init__(self, copies, to, mine, full, block_of, me, rows):
        self.copies, self.to, self.full, self.block_of = copies, to, full, block_of
        self.me, self.rows, self.sent, self.onward = me, rows, {}, {}
        size = rows // PIECES
        for piece in range(PIECES):
            for step in (way(piece), -way(piece)):
                self.sent[step, piece] = copies.start(
                    mine.at[pl.ds(piece * size, size)],
                    slab(full, block_of(me), rows, piece),
                    to(me + step),
                )

    def forward(self):
        for piece in range(PIECES):
            step = way(piece)
            self.sent[step, piece].wait_recv()
            here = slab(self.full, self.block_of(self.me - step), self.rows, piece)
            self.onward[piece] = self.copies.start(here, here, self.to(self.me + step))

    def near(self):
        for piece in range(PIECES):
            self.sent[-way(piece), piece].wait_recv()

    def far(self):
        for piece in range(PIECES):
            self.onward[piece].wait_recv()


class GatherTokens:
    def __init__(self, copies, mine, full, y, core):
        self.copies, self.full, self.y, self.core = copies, full, y, core
        self.rows = mine.shape[0]
        self.shared = {}
        self.own = copies.local(mine, slab(full, self.block_of(y), self.rows))
        self.shared[0] = copies.start(mine, slab(full, self.block_of(y), self.rows), at_core(1 - core))
        self.ring = GatherRing(copies, at_y, mine, full, self.block_of, y, self.rows)

    def block_of(self, index):
        return around(index) * 2 + self.core

    def share(self, k):
        here = slab(self.full, self.block_of(self.y + k), self.rows)
        self.shared[k] = self.copies.start(here, here, at_core(1 - self.core))

    def forward(self):
        self.ring.forward()

    def near(self):
        self.ring.near()
        self.share(1)
        self.share(-1)

    def far(self):
        self.ring.far()
        self.share(2)

    def finish(self):
        self.own.wait()
        for copy in self.shared.values():
            copy.wait_recv()


class GatherPlane:
    def __init__(self, copies, mine, full, x, z, core):
        self.copies, self.full = copies, full
        rows = mine.shape[0]

        def block(a, b):
            a, b = around(a), around(b)
            return jnp.where(core == 0, 4 * b + a, 4 * a + b)

        first, second = jnp.where(core == 0, x, z), jnp.where(core == 0, z, x)

        def to_first(index):
            return at_xz(jnp.where(core == 0, index, x), jnp.where(core == 0, z, index))

        def to_second(index):
            return at_xz(jnp.where(core == 0, x, index), jnp.where(core == 0, index, z))

        def onto(k, source=None):
            a = first + k
            if source is None:
                source = slab(full, block(a, second), rows)
            return GatherRing(copies, to_second, source, full, lambda b: block(a, b), second, rows)

        self.onto = onto
        self.own = copies.local(mine, slab(full, block(first, second), rows))
        self.ring = GatherRing(
            copies, to_first, mine, full, lambda a: block(a, second), first, rows
        )
        self.rings = {0: onto(0, mine)}

    def stages(self):
        def one():
            self.ring.forward()

        def two():
            self.ring.near()
            self.rings[1] = self.onto(1)
            self.rings[-1] = self.onto(-1)

        def three():
            self.rings[0].forward()

        def four():
            self.ring.far()
            self.rings[2] = self.onto(2)

        def five():
            self.rings[1].forward()
            self.rings[-1].forward()

        def six():
            self.rings[2].forward()
            self.rings[0].near()
            self.rings[0].far()

        def seven():
            for k in (1, -1, 2):
                self.rings[k].near()
                self.rings[k].far()
            self.own.wait()

        return [one, two, three, four, five, six, seven]


class ReduceRing:
    def __init__(self, copies, to, me, read, out, got, rows, source=None):
        self.copies, self.to, self.me, self.read = copies, to, me, read
        self.out, self.got, self.rows, self.source, self.sent = out, got, rows, source, {}
        self.size = rows // PIECES

    def span(self, piece):
        return pl.ds(piece * self.size, self.size)

    def push(self, slot, k, piece, device):
        span = self.span(piece)
        if self.source is not None:
            ref = self.source(k, span)
        else:

            def fill(rows):
                self.out[slot, rows] = self.read(k, rows).astype(BF16)

            row_steps(piece * self.size, self.size, fill)
            ref = self.out.at[slot, span]
        self.sent[slot, piece] = self.copies.start(ref, self.got.at[slot, span], device)

    def far(self, pieces=range(PIECES)):
        for piece in pieces:
            self.push(0, 2, piece, self.to(self.me + way(piece)))

    def direct(self, k):
        for piece in range(PIECES):
            if way(piece) == -k:
                self.push(1, k, piece, self.to(self.me + k))

    def onward(self, k):
        slot = 2 if self.source is None else 0
        for piece in range(PIECES):
            if way(piece) == k:
                self.sent[0, piece].wait_recv()

                def fill(rows):
                    self.out[slot, rows] = (
                        self.read(k, rows) + self.got[0, rows].astype(F32)
                    ).astype(BF16)

                row_steps(piece * self.size, self.size, fill)
                span = self.span(piece)
                self.sent[2, piece] = self.copies.start(
                    self.out.at[slot, span], self.got.at[2, span], self.to(self.me + k)
                )

    def arrive(self, piece):
        self.sent[1, piece].wait_recv()
        self.sent[2, piece].wait_recv()

    def total(self, rows):
        return self.read(0, rows) + self.got[1, rows].astype(F32) + self.got[2, rows].astype(F32)


class ReduceTokens:
    def __init__(self, copies, make, y, core, own, sib, got_sib, out, got):
        self.copies, self.make, self.y, self.core = copies, make, y, core
        self.own, self.sib, self.got_sib, self.shared = own, sib, got_sib, {}
        self.ring = ReduceRing(copies, at_y, y, self.read, out, got, own.shape[1])

    def read(self, k, rows):
        return self.own[k % 4, rows] + self.got_sib[k % 4, rows].astype(F32)

    def part(self, k):
        self.make(k, self.own.at[k % 4], self.sib.at[k % 4])
        self.shared[k] = self.copies.start(
            self.sib.at[k % 4], self.got_sib.at[k % 4], at_core(1 - self.core)
        )

    def run(self):
        self.part(2)
        self.part(1)
        self.shared[2].wait_recv()
        self.ring.far()
        self.part(-1)
        self.shared[1].wait_recv()
        self.ring.direct(1)
        self.part(0)
        self.shared[-1].wait_recv()
        self.ring.direct(-1)
        self.ring.onward(1)
        self.ring.onward(-1)
        self.shared[0].wait_recv()

    def each(self, act):
        for piece in range(PIECES):
            self.ring.arrive(piece)

            def take(rows):
                act(rows, self.ring.total(rows))

            row_steps(piece * self.ring.size, self.ring.size, take)


class ReducePlane:
    def __init__(self, copies, parts, x, z, core, out1, got1, mid, out2, got2):
        rows = mid.shape[1]

        def block(a, b):
            a, b = around(a), around(b)
            return jnp.where(core == 0, 4 * b + a, 4 * a + b)

        last, first = jnp.where(core == 0, x, z), jnp.where(core == 0, z, x)

        def to_last(index):
            return at_xz(jnp.where(core == 0, index, x), jnp.where(core == 0, z, index))

        def to_first(index):
            return at_xz(jnp.where(core == 0, x, index), jnp.where(core == 0, index, z))

        def ring(k):
            def place_of(step, span):
                start = block(last + k, first + step) * rows + span.start
                return pl.ds(pl.multiple_of(start, STEP), span.size)

            def read(step, span):
                return parts[place_of(step, span)].astype(F32)

            def source(step, span):
                return parts.at[place_of(step, span)]

            return ReduceRing(copies, to_first, first, read, out1.at[k % 4], got1.at[k % 4], rows, source)

        self.mid = mid
        self.rings = {k: ring(k) for k in (2, 1, -1, 0)}

        def read2(step, span):
            return mid[step % 4, span].astype(F32)

        def source2(step, span):
            return mid.at[step % 4, span]

        self.ring = ReduceRing(copies, to_last, last, read2, out2, got2, rows, source2)

    def start(self):
        for ring in self.rings.values():
            ring.far()
            ring.direct(1)
            ring.direct(-1)

    def onward(self, k):
        self.rings[k].onward(1)
        self.rings[k].onward(-1)

    def middle(self, k):
        ring = self.rings[k]
        for piece in range(PIECES):
            ring.arrive(piece)

            def fill(rows):
                self.mid[k % 4, rows] = ring.total(rows).astype(BF16)

            row_steps(piece * ring.size, ring.size, fill)

    def stages(self):
        def ends(k, then):
            def act():
                self.middle(k)
                then()

            return act

        return (
            [self.start]
            + [lambda k=k: self.onward(k) for k in (2, 1, -1, 0)]
            + [
                ends(2, self.ring.far),
                ends(1, lambda: self.ring.direct(1)),
                ends(-1, lambda: self.ring.direct(-1)),
                ends(0, lambda: None),
                lambda: (self.ring.onward(1), self.ring.onward(-1)),
            ]
        )

    def each(self, act):
        for piece in range(PIECES):
            self.ring.arrive(piece)

            def take(rows):
                act(rows, self.ring.total(rows))

            row_steps(piece * self.ring.size, self.ring.size, take)


def nt(left, right):
    return lax.dot_general(left, right, (((1,), (1,)), ((), ())), preferred_element_type=F32)


def tn(left, right):
    return lax.dot_general(left, right, (((0,), (0,)), ((), ())), preferred_element_type=F32)


def nn(left, right):
    return jnp.dot(left, right, preferred_element_type=F32)


def chip_rows(block):
    return pl.ds(pl.multiple_of(block * 256, 256), 256)


def part_maker(pairs, y, core):
    def make(k, mine, theirs):
        rows = chip_rows(around(y + k))

        @pl.loop(0, mine.shape[-1] // TILE)
        def _(tile):
            columns = pl.ds(pl.multiple_of(tile * TILE, TILE), TILE)
            total = None
            for left, right, lanes in pairs:
                term = nt(left[rows, :], right[columns, lanes])
                total = term if total is None else total + term
            low, high = total[:128], total[128:]
            mine[:, columns] = jnp.where(core == 0, low, high)
            theirs[:, columns] = jnp.where(core == 0, high, low).astype(BF16)

    return make


def inverse_of(value):
    return lax.rsqrt(jnp.mean(value * value, axis=-1, keepdims=True) + norm_eps)


def norm_back_rows(grad, value, gain):
    inverse = inverse_of(value)
    unit = value * inverse
    scaled = grad * gain
    moved = inverse * (scaled - unit * jnp.mean(scaled * unit, axis=-1, keepdims=True))
    return moved, grad * unit


def reorder_into(target, source, hot):
    runs = source.shape[1] // 256
    for run in range(runs):
        moved = nn(source[:, run * 256 : (run + 1) * 256], hot[...]).astype(BF16)
        target[:, run * 128 : (run + 1) * 128] = moved[:, :128]
        target[:, (runs + run) * 128 : (runs + run + 1) * 128] = moved[:, 128:]


def spread_kernel(
    hidden,
    cotangent,
    scale,
    hot,
    query,
    key,
    value,
    out,
    gate,
    up,
    down,
    gains,
    att_out,
    mlp_out,
    raw_out,
    top_out,
    att,
    mlp,
    raw,
    top,
    send,
    recv,
):
    unused_x, y, z, core = place()
    zhi = z // 2
    partner = {"core": 1 - core, "zhi": 1 - zhi}
    swaps = core != zhi
    peers = group_peers(y, core)
    greet([{"core": c, "y": d} for c, d in peers], partner, swaps)
    copies = Copies(send, recv)
    me = core * 4 + y
    depth, here = gate.shape[0], gate.shape[1] // 8
    gap = jnp.zeros((depth, PAD_FF - here), BF16)
    for block in range(8):
        for at, weight in enumerate((gate, up, down)):
            cut = weight[:, block * here : (block + 1) * here]
            mlp[block, :, at * PAD_FF : (at + 1) * PAD_FF] = jnp.concatenate((cut, gap), axis=1)
    local = [copies.local(mlp.at[me], mlp_out.at[me])]
    got = []
    for c, d in peers:
        got.append(copies.start(mlp.at[c * 4 + d], mlp_out.at[me], {"core": c, "y": d}))
    reorder_into(raw, hidden, hot)
    waits = [copies.swap(raw, raw_out, partner, swaps)]
    gap = jnp.zeros((depth, 62), BF16)
    for block in range(8):
        att[block, :, VALUE_AT] = value[:, block * 256 : (block + 1) * 256]
        att[block, :, OUT_AT] = out[:, block * 256 : (block + 1) * 256]
        att[block, :, QK_AT] = jnp.concatenate(
            (
                query[:, block * 32 : (block + 1) * 32],
                key[:, block * 32 : (block + 1) * 32],
                gains[...],
                gap,
            ),
            axis=1,
        )
    local.append(copies.local(att.at[me], att_out.at[me]))
    for c, d in peers:
        got.append(copies.start(att.at[c * 4 + d], att_out.at[me], {"core": c, "y": d}))

    def weigh(rows):
        top[rows] = (cotangent[rows].astype(F32) * scale[...]).astype(BF16)

    row_steps(0, top.shape[0], weigh)
    reorder_into(top, top[...], hot)
    waits.append(copies.swap(top, top_out, partner, swaps))
    for copy in got:
        copy.wait_recv()
    copies.finish()
    for copy in local:
        copy.wait()
    for wait in waits:
        wait()


def gain_rows(att):
    row = lax.broadcasted_iota(jnp.int32, (8, 128), 0)
    lane = lax.broadcasted_iota(jnp.int32, (8, 128), 1)
    pick = jnp.where((lane == row + 64) & (row < 2), 1.0, 0.0).astype(BF16)
    return nt(pick, att[:, QK_AT])


def head_lanes(head):
    lane = lax.broadcasted_iota(jnp.int32, (1, 128), 1)
    return (lane >= head * FEAT) & (lane < (head + 1) * FEAT)


def scores_of(q, k, block, extent):
    x = nt(q, k) * 0.25
    row = lax.broadcasted_iota(jnp.int32, (256, extent), 0) + block * 256
    keep = row >= lax.broadcasted_iota(jnp.int32, (256, extent), 1)
    return x, jnp.where(keep, 1.0 + x + 0.5 * (x * x), 0.0), keep


def forward_kernel(
    raw,
    att,
    top,
    att_out,
    normed_out,
    low_out,
    qs,
    ks,
    values,
    attended,
    shares,
    gains,
    middle,
    normed2,
    raw_all,
    att_all,
    normed,
    own,
    sib,
    got_sib,
    out,
    got,
    low,
    send,
    recv,
):
    x, y, z, core = place()
    greet(ring_peers(y, core) + plane_peers(x, z))
    copies = Copies(send, recv)
    tokens = GatherTokens(copies, raw, raw_all, y, core)
    plane = GatherPlane(copies, att, att_all, x, z, core)
    one, two, three, four, five, six, seven = plane.stages()
    one()
    two()
    tokens.forward()
    three()
    four()
    tokens.near()
    five()
    six()
    tokens.far()
    seven()
    tokens.finish()
    tops = GatherTokens(copies, top, low_out, y, core)
    kept = [copies.local(att_all, att_out)]
    gains[...] = gain_rows(att_all)

    @pl.loop(0, 4)
    def _(chip):
        def norm(rows):
            value = raw_all[rows].astype(F32)
            normed[rows] = (value * inverse_of(value) * gains[0:1]).astype(BF16)

        row_steps(chip * 256, 256, norm)
        rows = chip_rows(chip)
        block = normed[rows]
        values[rows] = nn(block, att_all[:, VALUE_AT]).astype(BF16)
        both = nn(block, att_all[:, QK_AT])
        lane = lax.broadcasted_iota(jnp.int32, (1, 128), 1)
        qs[rows] = jnp.where(lane < 32, both, 0.0).astype(BF16)
        ks[rows] = jnp.where(lane < 32, pltpu.roll(both, 96, 1), 0.0).astype(BF16)

    kept.append(copies.local(normed, normed_out))
    for head in range(2):
        lanes = slice(head * HEAD_V, (head + 1) * HEAD_V)
        for block in range(4):
            rows, extent = slice(block * 256, (block + 1) * 256), (block + 1) * 256
            q = jnp.where(head_lanes(head), qs[rows], 0)
            unused, scores, unused_keep = scores_of(q, ks[0:extent], block, extent)
            share = 1.0 / jnp.sum(scores, axis=-1, keepdims=True)
            numer = nn(scores.astype(BF16), values[0:extent, lanes])
            attended[rows, lanes] = (numer * share).astype(BF16)
            shares[rows, lanes] = jnp.broadcast_to(share, (256, HEAD_V))
    sums = ReduceTokens(
        copies, part_maker([(attended, att_all, OUT_AT)], y, core), y, core, own, sib, got_sib, out, got
    )
    sums.run()
    tops.forward()

    def norm2(rows, total):
        value = raw[rows].astype(F32) + total
        middle[rows] = value
        low[rows] = (value * inverse_of(value) * gains[1:2]).astype(BF16)

    sums.each(norm2)
    back = GatherTokens(copies, low, normed2, y, core)
    tops.near()
    tops.far()
    back.forward()
    back.near()
    back.far()
    tops.finish()
    back.finish()
    for copy in kept:
        copy.wait()
    copies.finish()


def mlp_kernel(
    normed2_in,
    low_in,
    weights_in,
    middle,
    top,
    gains,
    grad_middle,
    grad_gain,
    middle_low,
    grads,
    layer_out,
    normed2,
    grad_low,
    weights,
    hidden,
    gate_act,
    up_act,
    stage,
    own,
    sib,
    got_sib,
    out,
    got,
    sib2,
    got_sib2,
    out2,
    got2,
    low,
    layer,
    send,
    recv,
):
    unused_x, y, z, core = place()
    zhi = z // 2
    partner = {"core": 1 - core, "zhi": 1 - zhi}
    swaps = core != zhi
    copies = Copies(send, recv)
    loads = [copies.local(weights_in, weights)]
    rows_in = {}
    for k in (2, 1, -1, 0):
        rows = chip_rows(around(y + k))
        rows_in[k] = [
            copies.local(normed2_in.at[rows], normed2.at[rows]),
            copies.local(low_in.at[rows], grad_low.at[rows]),
        ]
    greet(ring_peers(y, core), partner, swaps)
    for copy in loads:
        copy.wait()

    def act_block(k):
        for copy in rows_in[k]:
            copy.wait()
        rows = chip_rows(around(y + k))

        @pl.loop(0, PAD_FF // TILE)
        def _(tile):
            def lanes(at):
                return pl.ds(pl.multiple_of(at * PAD_FF + tile * TILE, TILE), TILE)

            block = normed2[rows]
            gate = nn(block, weights[:, lanes(0)])
            upward = nn(block, weights[:, lanes(1)])
            grad_hidden = nn(grad_low[rows], weights[:, lanes(2)])
            sigma = jax.nn.sigmoid(gate)
            silu = gate * sigma
            hidden[rows, lanes(0)] = (silu * upward).astype(BF16)
            slope = sigma + silu * (1.0 - sigma)
            gate_act[rows, lanes(0)] = (grad_hidden * upward * slope).astype(BF16)
            up_act[rows, lanes(0)] = (grad_hidden * silu).astype(BF16)

    base = part_maker(
        [(gate_act, weights, slice(0, PAD_FF)), (up_act, weights, slice(PAD_FF, 2 * PAD_FF))], y, core
    )

    def make(k, mine, theirs):
        act_block(k)
        base(k, mine, theirs)

    stored = []

    def grad_block(at, left, right):
        if stored:
            stored[-1].wait()

        @pl.loop(0, left.shape[1] // TILE)
        def _(tile):
            columns = pl.ds(pl.multiple_of(tile * TILE, TILE), TILE)
            stage[columns] = tn(left[:, columns], right[...]).astype(BF16)

        stored.append(copies.local(stage, grads.at[:, pl.ds(at * PAD_FF, PAD_FF)]))

    sums = ReduceTokens(copies, make, y, core, own, sib, got_sib, out, got)
    sums.run()
    grad_block(0, normed2, gate_act)
    grad_gain[...] = jnp.zeros_like(grad_gain)

    def back(rows, total):
        moved, terms = norm_back_rows(total, middle[rows], gains[1:2])
        grad_gain[...] += terms[:8] + terms[8:]
        value = top[rows].astype(F32) + moved
        grad_middle[rows] = value
        low[rows] = value.astype(BF16)

    sums.each(back)
    gather = GatherTokens(copies, low, middle_low, y, core)
    layers = ReduceTokens(
        copies,
        part_maker([(hidden, weights, slice(2 * PAD_FF, 3 * PAD_FF))], y, core),
        y,
        core,
        own,
        sib2,
        got_sib2,
        out2,
        got2,
    )
    for k in (2, 1, -1, 0):
        layers.part(k)
    grad_block(1, normed2, up_act)
    gather.forward()
    for k in (2, 1, -1, 0):
        layers.shared[k].wait_recv()
    layers.ring.far()
    layers.ring.direct(1)
    layers.ring.direct(-1)
    gather.near()
    gather.far()
    grad_block(2, grad_low, hidden)
    layers.ring.onward(1)
    layers.ring.onward(-1)

    def add(rows, total):
        layer[rows] = (middle[rows] + total).astype(BF16)

    layers.each(add)
    wait = copies.swap(layer, layer_out, partner, swaps)
    gather.finish()
    stored[-1].wait()
    wait()
    copies.finish()


def back_kernel(
    low_in,
    normed_in,
    att,
    qs,
    ks,
    values,
    attended,
    shares,
    raw,
    grad_middle,
    gains,
    grad_gain2,
    mlp_in,
    att_out,
    mlp_out,
    grad_in,
    gain_out,
    tokens,
    mlp,
    parts,
    grad_numer,
    grad_denom,
    grad_q,
    grad_k,
    grad_v,
    grad_qk,
    grad_values,
    own,
    sib,
    got_sib,
    out,
    got,
    mlp_out1,
    mlp_got1,
    mlp_mid,
    mlp_out2,
    mlp_got2,
    att_out1,
    att_got1,
    att_mid,
    att_out2,
    att_got2,
    mlp_sum,
    att_sum,
    last,
    gain_part,
    gain_got,
    gain_sum,
    gain_back,
    send,
    recv,
):
    x, y, z, core = place()
    zhi = z // 2
    partner = {"core": 1 - core, "zhi": 1 - zhi}
    swaps = core != zhi
    copies = Copies(send, recv)
    load_mlp = copies.local(mlp_in, mlp)
    load_low = copies.local(low_in, tokens)
    peers = group_peers(y, core)
    planes = [
        (lax.rem(x + dx, 4), lax.rem(z + dz, 4))
        for dx in range(4)
        for dz in range(4)
        if (dx, dz) != (0, 0)
    ]
    greet(
        [{"core": c, "y": d} for c, d in peers] + [at_xz(a, b) for a, b in planes], partner, swaps
    )
    load_mlp.wait()
    mlp_plane = ReducePlane(
        copies, mlp, x, z, core, mlp_out1, mlp_got1, mlp_mid, mlp_out2, mlp_got2
    )
    mlp_stages = iter(mlp_plane.stages())
    next(mlp_stages)()
    load_low.wait()

    @pl.loop(0, 4)
    def _(chip):
        rows = chip_rows(chip)
        grad_mixed = nn(tokens[rows], att[:, OUT_AT]).astype(BF16).astype(F32)
        numer = grad_mixed * shares[rows]
        grad_numer[rows] = numer.astype(BF16)
        product = numer * attended[rows].astype(F32)
        for head in range(2):
            lanes = slice(head * HEAD_V, (head + 1) * HEAD_V)
            total = -jnp.sum(product[:, lanes], axis=-1, keepdims=True)
            grad_denom[rows, lanes] = jnp.broadcast_to(total, (256, HEAD_V))

    @pl.loop(0, tokens.shape[1] // TILE)
    def _(tile):
        columns = pl.ds(pl.multiple_of(tile * TILE, TILE), TILE)
        parts[columns, OUT_AT] = tn(tokens[:, columns], attended[...]).astype(BF16)

    load_normed = copies.local(normed_in, tokens)
    grad_k[...] = jnp.zeros_like(grad_k)
    grad_v[...] = jnp.zeros_like(grad_v)
    for head in range(2):
        lanes = slice(head * HEAD_V, (head + 1) * HEAD_V)
        for block in range(4):
            rows, extent = slice(block * 256, (block + 1) * 256), (block + 1) * 256
            q = jnp.where(head_lanes(head), qs[rows], 0)
            k = ks[0:extent]
            half, scores, keep = scores_of(q, k, block, extent)
            numer = grad_numer[rows, lanes]
            grad_scores = nt(numer, values[0:extent, lanes]) + grad_denom[rows, head * HEAD_V : head * HEAD_V + 1]
            grad_s = jnp.where(keep, grad_scores * (0.25 + 0.25 * half), 0.0).astype(BF16)
            moved = nn(grad_s, k)
            if head == 0:
                grad_q[rows] = jnp.where(head_lanes(0), moved, 0.0)
            else:
                grad_q[rows] += jnp.where(head_lanes(1), moved, 0.0)
            grad_k[0:extent] += tn(grad_s, q)
            grad_v[0:extent, lanes] += tn(scores.astype(BF16), numer)
        next(mlp_stages)()
        next(mlp_stages)()

    def join(rows):
        grad_qk[rows] = (grad_q[rows] + pltpu.roll(grad_k[rows], 32, 1)).astype(BF16)
        grad_values[rows] = grad_v[rows].astype(BF16)

    row_steps(0, 1024, join, 128)
    sums = ReduceTokens(
        copies,
        part_maker([(grad_values, att, VALUE_AT), (grad_qk, att, QK_AT)], y, core),
        y,
        core,
        own,
        sib,
        got_sib,
        out,
        got,
    )
    sums.run()
    load_normed.wait()

    @pl.loop(0, tokens.shape[1] // TILE)
    def _(tile):
        columns = pl.ds(pl.multiple_of(tile * TILE, TILE), TILE)
        left = tokens[:, columns]
        parts[columns, VALUE_AT] = tn(left, grad_values[...]).astype(BF16)
        parts[columns, QK_AT] = tn(left, grad_qk[...]).astype(BF16)

    att_plane = ReducePlane(
        copies, parts, x, z, core, att_out1, att_got1, att_mid, att_out2, att_got2
    )
    att_stages = iter(att_plane.stages())
    next(att_stages)()
    for _ in range(2):
        next(mlp_stages)()
    gain_part[...] = jnp.zeros_like(gain_part)

    def back(rows, total):
        moved, terms = norm_back_rows(total, raw[rows].astype(F32), gains[0:1])
        gain_part[...] += terms[:8] + terms[8:]
        last[rows] = (grad_middle[rows] + moved).astype(BF16)

    sums.each(back)
    wait_in = copies.swap(last, grad_in, partner, swaps)
    row = lax.broadcasted_iota(jnp.int32, (8, 1), 0)
    gain_part[...] = jnp.where(
        row == 0,
        jnp.sum(gain_part[...], axis=0, keepdims=True),
        jnp.where(row == 1, jnp.sum(grad_gain2[...], axis=0, keepdims=True), 0.0),
    )
    here = 4 * z + x

    def lanes_of(block):
        return pl.ds(pl.multiple_of(block * 128, 128), 128)

    gain_copies = [
        copies.start(gain_part.at[:, lanes_of(4 * b + a)], gain_got.at[here], at_xz(a, b))
        for a, b in planes
    ]
    gain_own = copies.local(gain_part.at[:, lanes_of(here)], gain_got.at[here])
    for _ in range(4):
        next(att_stages)()
    for stage in mlp_stages:
        stage()
    for stage in att_stages:
        stage()
    me = core * 4 + y

    def take(target):
        def act(rows, total):
            target[rows] = total.astype(BF16)

        return act

    mlp_plane.each(take(mlp_sum))
    back_copies, local = [], []

    def send_back(sums_ref, out_ref):
        def cut(index):
            return sums_ref.at[pl.ds(pl.multiple_of(index * 16, 16), 16)]

        local.append(copies.local(cut(me), out_ref.at[me]))
        for c, d in peers:
            back_copies.append(copies.start(cut(c * 4 + d), out_ref.at[me], {"core": c, "y": d}))

    send_back(mlp_sum, mlp_out)
    for copy in gain_copies:
        copy.wait_recv()
    gain_own.wait()
    gain_sum[...] = jnp.sum(gain_got[...], axis=0)
    for c, d in peers:
        back_copies.append(copies.start(gain_sum, gain_back.at[me], {"core": c, "y": d}))
    local.append(copies.local(gain_sum, gain_back.at[me]))
    att_plane.each(take(att_sum))
    send_back(att_sum, att_out)
    for copy in back_copies:
        copy.wait_recv()
    for copy in local:
        copy.wait()
    gain_out[...] = jnp.sum(gain_back[...], axis=0)
    wait_in()
    copies.finish()


def unpack_kernel(
    att, mlp, layer, last, hot, query, key, value, out, gate, up, down, layer_out, grad_in
):
    here = gate.shape[1] // 8
    for block in range(8):
        for at, grad in enumerate((gate, up, down)):
            cut = mlp[block, :, at * PAD_FF : at * PAD_FF + here]
            grad[:, block * here : (block + 1) * here] = cut.astype(F32)
        value[:, block * 256 : (block + 1) * 256] = att[block, :, VALUE_AT].astype(F32)
        out[:, block * 256 : (block + 1) * 256] = att[block, :, OUT_AT].astype(F32)
        query[:, block * 32 : (block + 1) * 32] = att[block, :, 512:544].astype(F32)
        key[:, block * 32 : (block + 1) * 32] = att[block, :, 544:576].astype(F32)
    runs = layer.shape[1] // 256
    for run in range(runs):
        for source, target in ((layer, layer_out), (last, grad_in)):
            low = source[:, run * 128 : (run + 1) * 128]
            high = source[:, (runs + run) * 128 : (runs + run + 1) * 128]
            both = jnp.concatenate((low, high), axis=1)
            target[:, run * 256 : (run + 1) * 256] = nn(both, hot[...]).astype(target.dtype)


HBM, VMEM = pl.ANY, pltpu.VMEM


def call(kernel, number, ins, outs, scratch, sems, flops):
    def spec(space):
        return pl.BlockSpec(memory_space=space)

    remote = {}
    if number is not None:
        scratch = list(scratch) + [pltpu.SemaphoreType.DMA((sems,)), pltpu.SemaphoreType.DMA((sems,))]
        remote = dict(collective_id=number, has_side_effects=True)
    return pl.pallas_call(
        kernel,
        out_shape=[jax.ShapeDtypeStruct(shape, dtype) for shape, dtype, _ in outs],
        in_specs=[spec(space) for _, space in ins],
        out_specs=[spec(space) for _, _, space in outs],
        scratch_shapes=scratch,
        compiler_params=pltpu.CompilerParams(vmem_limit_bytes=VMEM_LIMIT, **remote),
        cost_estimate=pl.CostEstimate(flops=flops, bytes_accessed=2**26, transcendentals=0),
        name=kernel.__name__,
    )(*[array for array, _ in ins])


def ring_scratch(width, own=True):
    sums = [VMEM((4, 128, width), F32)] if own else []
    return sums + [
        VMEM((4, 128, width), BF16),
        VMEM((4, 128, width), BF16),
        VMEM((3, 128, width), BF16),
        VMEM((3, 128, width), BF16),
    ]


def plane_scratch(width):
    return [
        VMEM((4, 1, 128, width), BF16),
        VMEM((4, 3, 128, width), BF16),
        VMEM((4, 128, width), BF16),
        VMEM((1, 128, width), BF16),
        VMEM((3, 128, width), BF16),
    ]


def body(
    hidden_in,
    norm1_gain,
    query_weight,
    key_weight,
    value_weight,
    out_weight,
    norm2_gain,
    gate_weight,
    up_weight,
    down_weight,
    cotangent,
    source_id,
    source_counts,
):
    rows, toks, width = hidden_in.shape
    depth, ff = gate_weight.shape
    length, held = 8 * toks, 8 * depth
    mlp_w = 3 * PAD_FF
    scale = row_scale(source_id, source_counts).reshape(1, 1)
    att, mlp, raw, top = call(
        spread_kernel,
        0,
        [
            (array, VMEM)
            for array in (
                hidden_in.reshape(toks, width),
                cotangent.reshape(toks, width),
                scale,
                lane_order(False),
                query_weight,
                key_weight,
                value_weight,
                out_weight,
                gate_weight,
                up_weight,
                down_weight,
                jnp.stack((norm1_gain, norm2_gain), axis=1),
            )
        ],
        [
            ((8, depth, ATT_W), BF16, HBM),
            ((8, depth, mlp_w), BF16, HBM),
            ((toks, width), BF16, HBM),
            ((toks, width), BF16, HBM),
        ],
        [
            VMEM((8, depth, ATT_W), BF16),
            VMEM((8, depth, mlp_w), BF16),
            VMEM((toks, width), BF16),
            VMEM((toks, width), BF16),
        ],
        20,
        0,
    )
    weights = lax.all_gather(mlp.reshape(held, mlp_w), CHIPS, axis=0, tiled=True)
    att, normed, low, qs, ks, values, attended, shares, gains, middle, normed2 = call(
        forward_kernel,
        1,
        [(raw, VMEM), (att.reshape(held, ATT_W), VMEM), (top, HBM)],
        [
            ((width, ATT_W), BF16, HBM),
            ((length, width), BF16, HBM),
            ((length, width), BF16, HBM),
            ((length, 128), BF16, VMEM),
            ((length, 128), BF16, VMEM),
            ((length, 256), BF16, VMEM),
            ((length, 256), BF16, VMEM),
            ((length, 256), F32, VMEM),
            ((8, width), F32, VMEM),
            ((toks, width), F32, VMEM),
            ((length, width), BF16, HBM),
        ],
        [
            VMEM((length, width), BF16),
            VMEM((width, ATT_W), BF16),
            VMEM((length, width), BF16),
        ]
        + ring_scratch(width)
        + [VMEM((toks, width), BF16)],
        140,
        4 * 10**9,
    )
    grad_middle, grad_gain2, middle_low, grads, layer = call(
        mlp_kernel,
        2,
        [
            (normed2, HBM),
            (low, HBM),
            (weights, HBM),
            (middle, VMEM),
            (top, VMEM),
            (gains, VMEM),
        ],
        [
            ((toks, width), F32, VMEM),
            ((8, width), F32, VMEM),
            ((length, width), BF16, HBM),
            ((width, mlp_w), BF16, HBM),
            ((toks, width), BF16, HBM),
        ],
        [
            VMEM((length, width), BF16),
            VMEM((length, width), BF16),
            VMEM((width, mlp_w), BF16),
            VMEM((length, PAD_FF), BF16),
            VMEM((length, PAD_FF), BF16),
            VMEM((length, PAD_FF), BF16),
            VMEM((width, PAD_FF), BF16),
        ]
        + ring_scratch(width)
        + ring_scratch(width, own=False)
        + [VMEM((toks, width), BF16), VMEM((toks, width), BF16)],
        80,
        30 * 10**9,
    )
    att_back, mlp_back, last, gain_sums = call(
        back_kernel,
        3,
        [
            (middle_low, HBM),
            (normed, HBM),
            (att, VMEM),
            (qs, VMEM),
            (ks, VMEM),
            (values, VMEM),
            (attended, VMEM),
            (shares, VMEM),
            (raw, VMEM),
            (grad_middle, VMEM),
            (gains, VMEM),
            (grad_gain2, VMEM),
            (grads, HBM),
        ],
        [
            ((8, depth, ATT_W), BF16, HBM),
            ((8, depth, mlp_w), BF16, HBM),
            ((toks, width), BF16, HBM),
            ((8, 128), F32, VMEM),
        ],
        [
            VMEM((length, width), BF16),
            VMEM((width, mlp_w), BF16),
            VMEM((width, ATT_W), BF16),
            VMEM((length, 256), BF16),
            VMEM((length, 256), F32),
            VMEM((length, 128), F32),
            VMEM((length, 128), F32),
            VMEM((length, 256), F32),
            VMEM((length, 128), BF16),
            VMEM((length, 256), BF16),
        ]
        + ring_scratch(width)
        + plane_scratch(mlp_w)
        + plane_scratch(ATT_W)
        + [
            VMEM((held, mlp_w), BF16),
            VMEM((held, ATT_W), BF16),
            VMEM((toks, width), BF16),
            VMEM((8, width), F32),
            VMEM((16, 8, 128), F32),
            VMEM((8, 128), F32),
            VMEM((8, 8, 128), F32),
        ],
        200,
        8 * 10**9,
    )
    grads_out = call(
        unpack_kernel,
        None,
        [(array, VMEM) for array in (att_back, mlp_back, layer, last, lane_order(True))],
        [
            ((depth, query_weight.shape[1]), F32, VMEM),
            ((depth, key_weight.shape[1]), F32, VMEM),
            ((depth, value_weight.shape[1]), F32, VMEM),
            ((depth, out_weight.shape[1]), F32, VMEM),
            ((depth, ff), F32, VMEM),
            ((depth, ff), F32, VMEM),
            ((depth, ff), F32, VMEM),
            ((toks, width), BF16, VMEM),
            ((toks, width), F32, VMEM),
        ],
        [],
        0,
        0,
    )
    grad_query, grad_key, grad_value, grad_out, grad_gate, grad_up, grad_down = grads_out[:7]
    at = (lax.axis_index("core") * 4 + lax.axis_index("y")) * depth
    pair = lax.dynamic_slice(gain_sums, (0, at), (8, depth))
    return (
        grads_out[7].reshape(rows, toks, width),
        grads_out[8].reshape(rows, toks, width),
        pair[0],
        grad_query,
        grad_key,
        grad_value,
        grad_out,
        pair[1],
        grad_gate,
        grad_up,
        grad_down,
    )


def solution(mesh):
    zlo, chips_x, cores, chips_y, zhi = 2, 4, 2, 4, 2
    whole = Mesh(mesh.devices.reshape(zlo, chips_x, cores, chips_y, zhi), AXES)
    weight = P(AXES, None)
    gain = P(AXES)
    tokens = P(DP, SEQ, None)
    return jax.shard_map(
        body,
        mesh=whole,
        in_specs=(
            tokens,
            gain,
            weight,
            weight,
            weight,
            weight,
            gain,
            weight,
            weight,
            weight,
            tokens,
            P(DP),
            P(),
        ),
        out_specs=(
            tokens,
            tokens,
            gain,
            weight,
            weight,
            weight,
            weight,
            gain,
            weight,
            weight,
            weight,
        ),
        check_vma=False,
    )
```

```python
import jax
import jax.numpy as jnp
import numpy as np
from jax import lax
from jax.experimental import pallas as pl
from jax.experimental.pallas import tpu as pltpu
from jax.sharding import Mesh, PartitionSpec as P

FEAT = 16
HEAD_V = 128
PAD_FF = 768
ATT_W = 640
QK_AT = slice(512, 640)
OUT_AT = slice(256, 512)
VALUE_AT = slice(0, 256)

norm_eps = 1e-05
AXES = ("zlo", "x", "core", "y", "zhi")
DP = ("zlo", "x", "core")
SEQ = ("y", "zhi")

MESH = pl.DeviceIdType.MESH
VMEM_LIMIT = 61 * 2**20
PIECES = 4
TILE = 256
STEP = 16
BF16, F32 = jnp.bfloat16, jnp.float32


def row_scale(source_id, source_counts):
    picked = jnp.sum(
        jnp.where(
            source_id[:, None] == jnp.arange(source_counts.shape[0], dtype=jnp.int32)[None, :],
            source_counts[None, :],
            0,
        ),
        axis=1,
    )
    return 4.0 / jnp.sqrt(picked.astype(F32))


def lane_order(back):
    at = np.arange(256)
    to = (at // 16 % 2) * 128 + (at // 32) * 16 + at % 16
    hot = np.zeros((256, 256), np.float32)
    hot[at, to] = 1.0
    return jnp.asarray(hot.T if back else hot, BF16)


def place():
    z = lax.axis_index("zhi") * 2 + lax.axis_index("zlo")
    return lax.axis_index("x"), lax.axis_index("y"), z, lax.axis_index("core")


def around(index):
    return lax.rem(index + 8, 4)


def at_y(y):
    return {"y": around(y)}


def at_core(core):
    return {"core": core}


def at_xz(x, z):
    x, z = around(x), around(z)
    return {"x": x, "zhi": z // 2, "zlo": lax.rem(z, 2)}


def ring_peers(y, core):
    return [at_y(y + 1), at_y(y - 1), at_core(1 - core)]


def plane_peers(x, z):
    return [at_xz(x + 1, z), at_xz(x - 1, z), at_xz(x, z + 1), at_xz(x, z - 1)]


def group_peers(y, core):
    return [
        (lax.rem(core + dc, 2), lax.rem(y + dy, 4))
        for dc in (0, 1)
        for dy in range(4)
        if (dc, dy) != (0, 0)
    ]


def hello(devices, partner=None, swaps=None):
    barrier = pltpu.get_barrier_semaphore()
    for device in devices:
        pl.semaphore_signal(barrier, inc=1, device_id=device, device_id_type=MESH)
    count = len(devices)
    if partner is not None:

        @pl.when(swaps)
        def _():
            pl.semaphore_signal(barrier, inc=1, device_id=partner, device_id_type=MESH)

        count = count + jnp.where(swaps, 1, 0)

    def wait():
        pl.semaphore_wait(barrier, count)

    return wait


class Copies:
    def __init__(self, send, recv):
        self.send, self.recv, self.used, self.open = send, recv, 0, []

    def start(self, src, dst, device):
        copy = pltpu.make_async_remote_copy(
            src_ref=src,
            dst_ref=dst,
            send_sem=self.send.at[self.used],
            recv_sem=self.recv.at[self.used],
            device_id=device,
            device_id_type=MESH,
        )
        copy.start()
        self.used += 1
        self.open.append(copy)
        return copy

    def local(self, src, dst):
        copy = pltpu.make_async_copy(src, dst, self.send.at[self.used])
        copy.start()
        self.used += 1
        return copy

    def swap(self, src, dst, partner, swaps):
        at = self.used
        self.used += 1

        def over():
            return pltpu.make_async_remote_copy(
                src_ref=src,
                dst_ref=dst,
                send_sem=self.send.at[at],
                recv_sem=self.recv.at[at],
                device_id=partner,
                device_id_type=MESH,
            )

        def stay():
            return pltpu.make_async_copy(src, dst, self.send.at[at])

        @pl.when(swaps)
        def _():
            over().start()

        @pl.when(jnp.logical_not(swaps))
        def _():
            stay().start()

        def wait():
            @pl.when(swaps)
            def _():
                over().wait()

            @pl.when(jnp.logical_not(swaps))
            def _():
                stay().wait()

        return wait

    def finish(self):
        for copy in self.open:
            copy.wait_send()


def way(piece):
    return 1 if piece % 2 == 0 else -1


def slab(ref, block, rows, piece=None):
    if piece is None:
        return ref.at[pl.ds(pl.multiple_of(block * rows, 128), rows)]
    size = rows // PIECES
    return ref.at[pl.ds(pl.multiple_of(block * rows + piece * size, 32), size)]


def row_steps(start, size, act, step=STEP):
    @pl.loop(0, size // step)
    def _(at):
        act(pl.ds(pl.multiple_of(start + at * step, step), step))


class GatherRing:
    def __init__(self, copies, to, mine, full, block_of, me, rows):
        self.copies, self.to, self.full, self.block_of = copies, to, full, block_of
        self.me, self.rows, self.sent, self.onward = me, rows, {}, {}
        size = rows // PIECES
        for piece in range(PIECES):
            for step in (way(piece), -way(piece)):
                self.sent[step, piece] = copies.start(
                    mine.at[pl.ds(piece * size, size)],
                    slab(full, block_of(me), rows, piece),
                    to(me + step),
                )

    def forward(self):
        for piece in range(PIECES):
            step = way(piece)
            self.sent[step, piece].wait_recv()
            here = slab(self.full, self.block_of(self.me - step), self.rows, piece)
            self.onward[piece] = self.copies.start(here, here, self.to(self.me + step))

    def near(self):
        for piece in range(PIECES):
            self.sent[-way(piece), piece].wait_recv()

    def far(self):
        for piece in range(PIECES):
            self.onward[piece].wait_recv()


class GatherTokens:
    def __init__(self, copies, mine, full, y, core):
        self.copies, self.full, self.y, self.core = copies, full, y, core
        self.rows = mine.shape[0]
        self.shared = {}
        self.own = copies.local(mine, slab(full, self.block_of(y), self.rows))
        self.shared[0] = copies.start(mine, slab(full, self.block_of(y), self.rows), at_core(1 - core))
        self.ring = GatherRing(copies, at_y, mine, full, self.block_of, y, self.rows)

    def block_of(self, index):
        return around(index) * 2 + self.core

    def share(self, k):
        here = slab(self.full, self.block_of(self.y + k), self.rows)
        self.shared[k] = self.copies.start(here, here, at_core(1 - self.core))

    def forward(self):
        self.ring.forward()

    def near(self):
        self.ring.near()
        self.share(1)
        self.share(-1)

    def far(self):
        self.ring.far()
        self.share(2)

    def finish(self):
        self.own.wait()
        for copy in self.shared.values():
            copy.wait_recv()


class GatherPlane:
    def __init__(self, copies, mine, full, x, z, core):
        self.copies, self.full = copies, full
        rows = mine.shape[0]

        def block(a, b):
            a, b = around(a), around(b)
            return jnp.where(core == 0, 4 * b + a, 4 * a + b)

        first, second = jnp.where(core == 0, x, z), jnp.where(core == 0, z, x)

        def to_first(index):
            return at_xz(jnp.where(core == 0, index, x), jnp.where(core == 0, z, index))

        def to_second(index):
            return at_xz(jnp.where(core == 0, x, index), jnp.where(core == 0, index, z))

        def onto(k, source=None):
            a = first + k
            if source is None:
                source = slab(full, block(a, second), rows)
            return GatherRing(copies, to_second, source, full, lambda b: block(a, b), second, rows)

        self.onto = onto
        self.own = copies.local(mine, slab(full, block(first, second), rows))
        self.ring = GatherRing(
            copies, to_first, mine, full, lambda a: block(a, second), first, rows
        )
        self.rings = {0: onto(0, mine)}

    def stages(self):
        def one():
            self.ring.forward()

        def two():
            self.ring.near()
            self.rings[1] = self.onto(1)
            self.rings[-1] = self.onto(-1)

        def three():
            self.rings[0].forward()

        def four():
            self.ring.far()
            self.rings[2] = self.onto(2)

        def five():
            self.rings[1].forward()
            self.rings[-1].forward()

        def six():
            self.rings[2].forward()
            self.rings[0].near()
            self.rings[0].far()

        def seven():
            for k in (1, -1, 2):
                self.rings[k].near()
                self.rings[k].far()
            self.own.wait()

        return [one, two, three, four, five, six, seven]


class ReduceRing:
    def __init__(self, copies, to, me, read, out, got, rows, source=None):
        self.copies, self.to, self.me, self.read = copies, to, me, read
        self.out, self.got, self.rows, self.source, self.sent = out, got, rows, source, {}
        self.size = rows // PIECES

    def span(self, piece):
        return pl.ds(piece * self.size, self.size)

    def push(self, slot, k, piece, device):
        span = self.span(piece)
        if self.source is not None:
            ref = self.source(k, span)
        else:

            def fill(rows):
                self.out[slot, rows] = self.read(k, rows).astype(BF16)

            row_steps(piece * self.size, self.size, fill)
            ref = self.out.at[slot, span]
        self.sent[slot, piece] = self.copies.start(ref, self.got.at[slot, span], device)

    def far(self, pieces=range(PIECES)):
        for piece in pieces:
            self.push(0, 2, piece, self.to(self.me + way(piece)))

    def direct(self, k):
        for piece in range(PIECES):
            if way(piece) == -k:
                self.push(1, k, piece, self.to(self.me + k))

    def onward(self, k):
        slot = 2 if self.source is None else 0
        for piece in range(PIECES):
            if way(piece) == k:
                self.sent[0, piece].wait_recv()

                def fill(rows):
                    self.out[slot, rows] = (
                        self.read(k, rows) + self.got[0, rows].astype(F32)
                    ).astype(BF16)

                row_steps(piece * self.size, self.size, fill)
                span = self.span(piece)
                self.sent[2, piece] = self.copies.start(
                    self.out.at[slot, span], self.got.at[2, span], self.to(self.me + k)
                )

    def arrive(self, piece):
        self.sent[1, piece].wait_recv()
        self.sent[2, piece].wait_recv()

    def total(self, rows):
        return self.read(0, rows) + self.got[1, rows].astype(F32) + self.got[2, rows].astype(F32)


class ReduceTokens:
    def __init__(self, copies, make, y, core, own, sib, got_sib, out, got):
        self.copies, self.make, self.y, self.core = copies, make, y, core
        self.own, self.sib, self.got_sib, self.shared = own, sib, got_sib, {}
        self.ring = ReduceRing(copies, at_y, y, self.read, out, got, own.shape[1])

    def read(self, k, rows):
        return self.own[k % 4, rows] + self.got_sib[k % 4, rows].astype(F32)

    def share(self, k):
        self.shared[k] = self.copies.start(
            self.sib.at[k % 4], self.got_sib.at[k % 4], at_core(1 - self.core)
        )

    def part(self, k):
        self.make(k, self.own.at[k % 4], self.sib.at[k % 4])
        self.share(k)

    def one(self):
        self.shared[2].wait_recv()
        self.ring.far()
        self.shared[1].wait_recv()
        self.ring.direct(1)

    def two(self):
        self.shared[-1].wait_recv()
        self.ring.direct(-1)
        self.ring.onward(1)
        self.ring.onward(-1)
        self.shared[0].wait_recv()

    def run(self):
        self.part(2)
        self.part(1)
        self.part(-1)
        self.one()
        self.part(0)
        self.two()

    def each(self, act):
        for piece in range(PIECES):
            self.ring.arrive(piece)

            def take(rows):
                act(rows, self.ring.total(rows))

            row_steps(piece * self.ring.size, self.ring.size, take)


class ReducePlane:
    def __init__(self, copies, parts, lanes, x, z, core, out1, got1, mid, out2, got2):
        rows = mid.shape[1]

        def block(a, b):
            a, b = around(a), around(b)
            return jnp.where(core == 0, 4 * b + a, 4 * a + b)

        last, first = jnp.where(core == 0, x, z), jnp.where(core == 0, z, x)

        def to_last(index):
            return at_xz(jnp.where(core == 0, index, x), jnp.where(core == 0, z, index))

        def to_first(index):
            return at_xz(jnp.where(core == 0, x, index), jnp.where(core == 0, index, z))

        def ring(k):
            def place_of(step, span):
                start = block(last + k, first + step) * rows + span.start
                return pl.ds(pl.multiple_of(start, STEP), span.size)

            def read(step, span):
                return parts[place_of(step, span), lanes].astype(F32)

            def source(step, span):
                return parts.at[place_of(step, span), lanes]

            return ReduceRing(copies, to_first, first, read, out1.at[k % 4], got1.at[k % 4], rows, source)

        self.mid = mid
        self.rings = {k: ring(k) for k in (2, 1, -1, 0)}

        def read2(step, span):
            return mid[step % 4, span].astype(F32)

        def source2(step, span):
            return mid.at[step % 4, span]

        self.ring = ReduceRing(copies, to_last, last, read2, out2, got2, rows, source2)

    def start(self):
        for ring in self.rings.values():
            ring.far()
            ring.direct(1)
            ring.direct(-1)

    def onward(self, k):
        self.rings[k].onward(1)
        self.rings[k].onward(-1)

    def middle(self, k):
        ring = self.rings[k]
        for piece in range(PIECES):
            ring.arrive(piece)

            def fill(rows):
                self.mid[k % 4, rows] = ring.total(rows).astype(BF16)

            row_steps(piece * ring.size, ring.size, fill)

    def stages(self):
        def ends(k, then):
            def act():
                self.middle(k)
                then()

            return act

        return (
            [self.start]
            + [lambda k=k: self.onward(k) for k in (2, 1, -1, 0)]
            + [
                ends(2, self.ring.far),
                ends(1, lambda: self.ring.direct(1)),
                ends(-1, lambda: self.ring.direct(-1)),
                ends(0, lambda: None),
                lambda: (self.ring.onward(1), self.ring.onward(-1)),
            ]
        )

    def each(self, act):
        for piece in range(PIECES):
            self.ring.arrive(piece)

            def take(rows):
                act(rows, self.ring.total(rows))

            row_steps(piece * self.ring.size, self.ring.size, take)


def nt(left, right):
    return lax.dot_general(left, right, (((1,), (1,)), ((), ())), preferred_element_type=F32)


def tn(left, right):
    return lax.dot_general(left, right, (((0,), (0,)), ((), ())), preferred_element_type=F32)


def nn(left, right):
    return jnp.dot(left, right, preferred_element_type=F32)


def chip_rows(block):
    return pl.ds(pl.multiple_of(block * 256, 256), 256)


def part_maker(pairs, y, core):
    def make(k, mine, theirs):
        rows = chip_rows(around(y + k))

        @pl.loop(0, mine.shape[-1] // TILE)
        def _(tile):
            columns = pl.ds(pl.multiple_of(tile * TILE, TILE), TILE)
            total = None
            for left, right, lanes in pairs:
                term = nt(left[rows, :], right[columns, lanes])
                total = term if total is None else total + term
            low, high = total[:128], total[128:]
            mine[:, columns] = jnp.where(core == 0, low, high)
            theirs[:, columns] = jnp.where(core == 0, high, low).astype(BF16)

    return make


def inverse_of(value):
    return lax.rsqrt(jnp.mean(value * value, axis=-1, keepdims=True) + norm_eps)


def norm_back_rows(grad, value, gain):
    inverse = inverse_of(value)
    unit = value * inverse
    scaled = grad * gain
    moved = inverse * (scaled - unit * jnp.mean(scaled * unit, axis=-1, keepdims=True))
    return moved, grad * unit


def reorder_into(target, source, hot):
    runs = source.shape[1] // 256
    for run in range(runs):
        moved = nn(source[:, run * 256 : (run + 1) * 256], hot[...]).astype(BF16)
        target[:, run * 128 : (run + 1) * 128] = moved[:, :128]
        target[:, (runs + run) * 128 : (runs + run + 1) * 128] = moved[:, 128:]


def gain_rows(att):
    row = lax.broadcasted_iota(jnp.int32, (8, 128), 0)
    lane = lax.broadcasted_iota(jnp.int32, (8, 128), 1)
    pick = jnp.where((lane == row + 64) & (row < 2), 1.0, 0.0).astype(BF16)
    return nt(pick, att[:, QK_AT])


def head_lanes(head):
    lane = lax.broadcasted_iota(jnp.int32, (1, 128), 1)
    return (lane >= head * FEAT) & (lane < (head + 1) * FEAT)


def scores_of(q, k, block, extent):
    x = nt(q, k) * 0.25
    row = lax.broadcasted_iota(jnp.int32, (256, extent), 0) + block * 256
    keep = row >= lax.broadcasted_iota(jnp.int32, (256, extent), 1)
    return x, jnp.where(keep, 1.0 + x + 0.5 * (x * x), 0.0), keep


def forward_kernel(
    hidden,
    cotangent,
    scale,
    hot,
    query,
    key,
    value,
    out_weight,
    gate,
    up,
    down,
    gain_pair,
    att_out,
    weights,
    raw_out,
    low_out,
    qs,
    ks,
    values,
    attended,
    shares,
    inverses,
    gains,
    raw,
    top,
    middle,
    normed2,
    att_cut,
    mlp_cut,
    raw_cut,
    top_cut,
    att_own,
    mlp_own,
    raw_all,
    att_all,
    att_scaled,
    own,
    sib,
    got_sib,
    out,
    got,
    low,
    send,
    recv,
):
    x, y, z, core = place()
    zhi = z // 2
    partner = {"core": 1 - core, "zhi": 1 - zhi}
    swaps = core != zhi
    peers = group_peers(y, core)
    ready = hello(
        [{"core": c, "y": d} for c, d in peers] + plane_peers(x, z), partner, swaps
    )
    copies = Copies(send, recv)
    me = core * 4 + y
    depth, here = gate.shape[0], gate.shape[1] // 8

    def spread(cuts, target):
        rows = pl.ds(pl.multiple_of(me * depth, depth), depth)
        kept = copies.local(cuts.at[me], target.at[rows])
        got = [
            copies.start(cuts.at[c * 4 + d], target.at[rows], {"core": c, "y": d}) for c, d in peers
        ]

        def wait():
            kept.wait()
            for copy in got:
                copy.wait_recv()

        return wait

    reorder_into(raw_cut, hidden, hot)
    gap = jnp.zeros((depth, 62), BF16)
    for block in range(8):
        att_cut[block, :, VALUE_AT] = value[:, block * 256 : (block + 1) * 256]
        att_cut[block, :, OUT_AT] = out_weight[:, block * 256 : (block + 1) * 256]
        att_cut[block, :, QK_AT] = jnp.concatenate(
            (
                query[:, block * 32 : (block + 1) * 32],
                key[:, block * 32 : (block + 1) * 32],
                gain_pair[...],
                gap,
            ),
            axis=1,
        )
    ready()
    wait_raw = copies.swap(raw_cut, raw, partner, swaps)
    wait_att = spread(att_cut, att_own)
    gap = jnp.zeros((depth, PAD_FF - here), BF16)
    for block in range(8):
        for at, weight in enumerate((gate, up, down)):
            cut = weight[:, block * here : (block + 1) * here]
            mlp_cut[block, :, at * PAD_FF : (at + 1) * PAD_FF] = jnp.concatenate((cut, gap), axis=1)
    wait_raw()
    tokens = GatherTokens(copies, raw, raw_all, y, core)
    wait_mlp = spread(mlp_cut, mlp_own)

    def weigh(rows):
        top_cut[rows] = (cotangent[rows].astype(F32) * scale[...]).astype(BF16)

    row_steps(0, top_cut.shape[0], weigh)
    reorder_into(top_cut, top_cut[...], hot)
    wait_att()
    plane = GatherPlane(copies, att_own, att_all, x, z, core)
    wait_top = copies.swap(top_cut, top, partner, swaps)

    def invert(block):
        def act(rows):
            inverse = inverse_of(raw_all[rows].astype(F32))
            inverses[rows] = jnp.broadcast_to(inverse, (STEP, 128))

        row_steps(block * 128, 128, act)

    one, two, three, four, five, six, seven = plane.stages()
    one()
    two()
    tokens.forward()
    three()
    four()
    wait_mlp()
    mlp_plane = GatherPlane(copies, mlp_own, weights, x, z, core)
    mlp_stages = iter(mlp_plane.stages())
    tokens.shared[0].wait_recv()
    tokens.own.wait()
    invert(2 * y)
    invert(2 * y + 1)
    five()
    six()
    tokens.near()
    invert(2 * around(y + 1) + core)
    invert(2 * around(y - 1) + core)
    tokens.far()
    invert(2 * around(y + 2) + core)
    seven()
    gains[...] = gain_rows(att_all)

    def scale_rows(rows):
        gain = att_all[rows, 576:577].astype(F32)
        att_scaled[rows, 0:256] = (att_all[rows, VALUE_AT].astype(F32) * gain).astype(BF16)
        att_scaled[rows, 256:384] = (att_all[rows, QK_AT].astype(F32) * gain).astype(BF16)

    row_steps(0, att_all.shape[0], scale_rows, 128)
    tokens.shared[1].wait_recv()
    tokens.shared[-1].wait_recv()
    invert(2 * around(y + 1) + 1 - core)
    invert(2 * around(y - 1) + 1 - core)
    tokens.shared[2].wait_recv()
    invert(2 * around(y + 2) + 1 - core)
    wait_top()
    tops = GatherTokens(copies, top, low_out, y, core)
    kept = [copies.local(att_all, att_out), copies.local(raw_all, raw_out)]
    next(mlp_stages)()
    next(mlp_stages)()

    @pl.loop(0, 2, unroll=True)
    def _(half):
        rows = pl.ds(pl.multiple_of(half * 512, 512), 512)
        inverse = inverses[rows]
        block = raw_all[rows]
        both = nn(block, att_scaled[:, 0:256])
        values[rows] = (both * jnp.concatenate((inverse, inverse), axis=1)).astype(BF16)
        both = nn(block, att_scaled[:, 256:384]) * inverse
        lane = lax.broadcasted_iota(jnp.int32, (1, 128), 1)
        qs[rows] = jnp.where(lane < 32, both, 0.0).astype(BF16)
        ks[rows] = jnp.where(lane < 32, pltpu.roll(both, 96, 1), 0.0).astype(BF16)

    for head in range(2):
        lanes = slice(head * HEAD_V, (head + 1) * HEAD_V)
        for block in range(4):
            rows, extent = slice(block * 256, (block + 1) * 256), (block + 1) * 256
            q = jnp.where(head_lanes(head), qs[rows], 0)
            unused, scores, unused_keep = scores_of(q, ks[0:extent], block, extent)
            share = 1.0 / jnp.sum(scores, axis=-1, keepdims=True)
            numer = nn(scores.astype(BF16), values[0:extent, lanes])
            attended[rows, lanes] = (numer * share).astype(BF16)
            shares[rows, lanes] = jnp.broadcast_to(share, (256, HEAD_V))
        next(mlp_stages)()
    tops.forward()
    sums = ReduceTokens(
        copies, part_maker([(attended, att_all, OUT_AT)], y, core), y, core, own, sib, got_sib, out, got
    )
    sums.run()
    next(mlp_stages)()
    tops.near()

    def norm2(rows, total):
        value = raw[rows].astype(F32) + total
        middle[rows] = value
        low[rows] = (value * inverse_of(value) * gains[1:2]).astype(BF16)

    sums.each(norm2)
    back = GatherTokens(copies, low, normed2, y, core)
    next(mlp_stages)()
    tops.far()
    back.forward()
    back.near()
    back.far()
    next(mlp_stages)()
    tops.finish()
    back.finish()
    for copy in kept:
        copy.wait()
    copies.finish()


def mlp_kernel(
    normed2_in,
    low_in,
    weights_in,
    middle,
    top,
    gains,
    grad_middle,
    grad_gain,
    middle_low,
    grads,
    gate_sum,
    layer_parts,
    normed2,
    grad_low,
    weights,
    hidden,
    gate_act,
    up_act,
    own,
    sib,
    got_sib,
    out,
    got,
    sib2,
    got_sib2,
    layer,
    low,
    plane_out1,
    plane_got1,
    plane_mid,
    plane_out2,
    plane_got2,
    send,
    recv,
):
    x, y, z, core = place()
    copies = Copies(send, recv)
    ready = hello(ring_peers(y, core) + plane_peers(x, z))
    order = (2, 1, -1, 0)
    loads = {}

    def load(k):
        slot = order.index(k)
        for at, owner in enumerate((core, 1 - core)):
            block = around(y + k) * 2 + owner
            rows = pl.ds(slot * 256 + at * 128, 128)
            for source, target in ((normed2_in, normed2), (low_in, grad_low)):
                loads.setdefault(k, []).append(copies.local(slab(source, block, 128), target.at[rows]))

    def lanes(at):
        return slice(at * PAD_FF, (at + 1) * PAD_FF)

    load(2)
    load(1)
    loads["w"] = [copies.local(weights_in.at[:, lanes(at)], weights.at[:, lanes(at)]) for at in range(3)]
    load(-1)
    load(0)
    ready()

    def act_tile(half, tile):
        rows = slice(half * 512, (half + 1) * 512)
        here = slice(tile * TILE, (tile + 1) * TILE)

        def cut(at):
            return weights[:, at * PAD_FF + tile * TILE : at * PAD_FF + (tile + 1) * TILE]

        block = normed2[rows]
        gate = nn(block, cut(0))
        upward = nn(block, cut(1))
        grad_hidden = nn(grad_low[rows], cut(2))
        sigma = jax.nn.sigmoid(gate)
        silu = gate * sigma
        hidden[rows, here] = (silu * upward).astype(BF16)
        slope = sigma + silu * (1.0 - sigma)
        gate_act[rows, here] = (grad_hidden * upward * slope).astype(BF16)
        up_act[rows, here] = (grad_hidden * silu).astype(BF16)

    def part_pair(half, pairs, sib_ref):
        rows = slice(half * 512, (half + 1) * 512)

        @pl.loop(0, own.shape[-1] // 512)
        def _(tile):
            columns = pl.ds(pl.multiple_of(tile * 512, 512), 512)
            total = None
            for left, right in pairs:
                term = nt(left[rows, :], weights[columns, right])
                total = term if total is None else total + term
            for at in range(2):
                k = order[2 * half + at] % 4
                own[k, :, columns] = total[at * 256 : at * 256 + 128]
                sib_ref[k, :, columns] = total[at * 256 + 128 : at * 256 + 256].astype(BF16)

    def grad_block(at, left, right):
        @pl.loop(0, left.shape[1] // 512)
        def _(tile):
            columns = pl.ds(pl.multiple_of(tile * 512, 512), 512)
            weights[columns, lanes(at)] = tn(left[:, columns], right[...]).astype(BF16)

    sums = ReduceTokens(copies, None, y, core, own, sib, got_sib, out, got)
    acts = [(gate_act, lanes(0)), (up_act, lanes(1))]
    for copy in loads[2] + loads[1] + loads["w"]:
        copy.wait()
    for tile in range(3):
        act_tile(0, tile)
    part_pair(0, acts, sib)
    sums.share(2)
    sums.share(1)
    for copy in loads[-1] + loads[0]:
        copy.wait()
    act_tile(1, 0)
    sums.one()
    act_tile(1, 1)
    act_tile(1, 2)
    part_pair(1, acts, sib)
    sums.share(-1)
    sums.share(0)
    sums.two()
    grad_block(0, normed2, gate_act)
    plane = ReducePlane(
        copies, weights, lanes(0), x, z, core, plane_out1, plane_got1, plane_mid, plane_out2, plane_got2
    )
    stages = iter(plane.stages())
    next(stages)()
    grad_gain[...] = jnp.zeros_like(grad_gain)

    def back(rows, total):
        moved, terms = norm_back_rows(total, middle[rows], gains[1:2])
        grad_gain[...] += terms[:8] + terms[8:]
        value = top[rows].astype(F32) + moved
        grad_middle[rows] = value
        low[rows] = value.astype(BF16)

    sums.each(back)
    gather = GatherTokens(copies, low, middle_low, y, core)
    next(stages)()
    next(stages)()
    grad_block(1, normed2, up_act)
    next(stages)()
    next(stages)()
    gather.forward()
    layers = ReduceTokens(copies, None, y, core, own, sib2, got_sib2, None, None)
    part_pair(0, [(hidden, lanes(2))], sib2)
    layers.share(2)
    layers.share(1)
    next(stages)()
    next(stages)()
    gather.near()
    part_pair(1, [(hidden, lanes(2))], sib2)
    layers.share(-1)
    layers.share(0)
    next(stages)()
    next(stages)()
    gather.far()
    grad_block(2, grad_low, hidden)
    stored = [
        copies.local(weights.at[:, PAD_FF : 3 * PAD_FF], grads),
    ]
    for stage in stages:
        stage()
    for k in order:
        layers.shared[k].wait_recv()

        def add(rows, k=k):
            layer[k % 4, rows] = layers.read(k, rows).astype(BF16)

        row_steps(0, 128, add)
    stored.append(copies.local(layer, layer_parts))

    def take(rows, total):
        gate_sum[rows] = total.astype(BF16)

    plane.each(take)
    gather.finish()
    for copy in stored:
        copy.wait()
    copies.finish()


def back_kernel(
    low_in,
    raw_in,
    att,
    qs,
    ks,
    values,
    attended,
    shares,
    inverses,
    raw,
    grad_middle,
    middle,
    gains,
    grad_gain2,
    grads_in,
    layer_in,
    gate_sum,
    att_out,
    mlp_out,
    gate_out,
    grad_in,
    layer_out,
    gain_out,
    tokens,
    mlp,
    parts,
    layer_parts,
    grad_numer,
    grad_denom,
    grad_q,
    grad_k,
    grad_v,
    grad_qk,
    grad_values,
    scaled_qk,
    scaled_values,
    own,
    sib,
    got_sib,
    out,
    got,
    layer_sent,
    layer_got,
    mlp_out1,
    mlp_got1,
    mlp_mid,
    mlp_out2,
    mlp_got2,
    att_out1,
    att_got1,
    att_mid,
    att_out2,
    att_got2,
    mlp_sum,
    att_sum,
    last,
    layer,
    gain_part,
    gain_got,
    gain_sum,
    gain_back,
    send,
    recv,
):
    x, y, z, core = place()
    zhi = z // 2
    partner = {"core": 1 - core, "zhi": 1 - zhi}
    swaps = core != zhi
    copies = Copies(send, recv)
    peers = group_peers(y, core)
    planes = [
        (lax.rem(x + dx, 4), lax.rem(z + dz, 4))
        for dx in range(4)
        for dz in range(4)
        if (dx, dz) != (0, 0)
    ]
    ready = hello(
        [{"core": c, "y": d} for c, d in peers] + [at_xz(a, b) for a, b in planes], partner, swaps
    )
    load_low = copies.local(low_in, tokens)
    load_mlp = copies.local(grads_in, mlp)
    load_layer = copies.local(layer_in, layer_parts)
    ready()
    load_low.wait()
    load_mlp.wait()
    mlp_plane = ReducePlane(
        copies,
        mlp,
        slice(0, 2 * PAD_FF),
        x,
        z,
        core,
        mlp_out1,
        mlp_got1,
        mlp_mid,
        mlp_out2,
        mlp_got2,
    )
    mlp_stages = iter(mlp_plane.stages())
    next(mlp_stages)()
    load_layer.wait()
    layers = ReduceRing(
        copies,
        at_y,
        y,
        lambda k, rows: layer_parts[k % 4, rows].astype(F32),
        layer_sent,
        layer_got,
        128,
        lambda k, span: layer_parts.at[k % 4, span],
    )
    layers.far()
    layers.direct(1)
    layers.direct(-1)
    me = core * 4 + y
    back_copies, local = [], []

    def send_back(sums_ref, out_ref):
        def cut(index):
            return sums_ref.at[pl.ds(pl.multiple_of(index * 16, 16), 16)]

        local.append(copies.local(cut(me), out_ref.at[me]))
        for c, d in peers:
            back_copies.append(copies.start(cut(c * 4 + d), out_ref.at[me], {"core": c, "y": d}))

    send_back(gate_sum, gate_out)

    @pl.loop(0, 2, unroll=True)
    def _(half):
        rows = pl.ds(pl.multiple_of(half * 512, 512), 512)
        grad_mixed = nn(tokens[rows], att[:, OUT_AT]).astype(BF16).astype(F32)
        numer = grad_mixed * shares[rows]
        grad_numer[rows] = numer.astype(BF16)
        product = numer * attended[rows].astype(F32)
        for head in range(2):
            lanes = slice(head * HEAD_V, (head + 1) * HEAD_V)
            total = -jnp.sum(product[:, lanes], axis=-1, keepdims=True)
            grad_denom[rows, lanes] = jnp.broadcast_to(total, (512, HEAD_V))

    grad_k[...] = jnp.zeros_like(grad_k)
    grad_v[...] = jnp.zeros_like(grad_v)

    def attend_back(head, block):
        lanes = slice(head * HEAD_V, (head + 1) * HEAD_V)
        rows, extent = slice(block * 256, (block + 1) * 256), (block + 1) * 256
        q = jnp.where(head_lanes(head), qs[rows], 0)
        k = ks[0:extent]
        half, scores, keep = scores_of(q, k, block, extent)
        numer = grad_numer[rows, lanes]
        total = grad_denom[rows, head * HEAD_V : head * HEAD_V + 1]
        grad_scores = nt(numer, values[0:extent, lanes]) + total
        grad_s = jnp.where(keep, grad_scores * (0.25 + 0.25 * half), 0.0).astype(BF16)
        moved = nn(grad_s, k)
        if head == 0:
            grad_q[rows] = jnp.where(head_lanes(0), moved, 0.0)
        else:
            grad_q[rows] += jnp.where(head_lanes(1), moved, 0.0)
        grad_k[0:extent] += tn(grad_s, q)
        grad_v[0:extent, lanes] += tn(scores.astype(BF16), numer)

    for block in range(4):
        attend_back(0, block)
    layers.onward(1)
    layers.onward(-1)
    next(mlp_stages)()
    next(mlp_stages)()
    for block in range(4):
        attend_back(1, block)
    next(mlp_stages)()

    def join(rows):
        inverse = inverses[rows]
        both = grad_q[rows] + pltpu.roll(grad_k[rows], 32, 1)
        grad_qk[rows] = both.astype(BF16)
        scaled_qk[rows] = (both * inverse).astype(BF16)
        both = grad_v[rows]
        grad_values[rows] = both.astype(BF16)
        scaled_values[rows] = (both * jnp.concatenate((inverse, inverse), axis=1)).astype(BF16)

    row_steps(0, 1024, join, 128)
    sums = ReduceTokens(
        copies,
        part_maker([(grad_values, att, VALUE_AT), (grad_qk, att, QK_AT)], y, core),
        y,
        core,
        own,
        sib,
        got_sib,
        out,
        got,
    )
    sums.run()

    @pl.loop(0, tokens.shape[1] // 512)
    def _(tile):
        columns = pl.ds(pl.multiple_of(tile * 512, 512), 512)
        parts[columns, OUT_AT] = tn(tokens[:, columns], attended[...]).astype(BF16)

    load_raw = copies.local(raw_in, tokens)
    next(mlp_stages)()
    load_raw.wait()

    @pl.loop(0, tokens.shape[1] // 512)
    def _(tile):
        columns = pl.ds(pl.multiple_of(tile * 512, 512), 512)
        left = tokens[:, columns]
        gain = att[columns, 576:577].astype(F32)
        parts[columns, VALUE_AT] = (tn(left, scaled_values[...]) * gain).astype(BF16)
        parts[columns, QK_AT] = (tn(left, scaled_qk[...]) * gain).astype(BF16)

    att_plane = ReducePlane(
        copies,
        parts,
        slice(0, ATT_W),
        x,
        z,
        core,
        att_out1,
        att_got1,
        att_mid,
        att_out2,
        att_got2,
    )
    att_stages = iter(att_plane.stages())
    next(att_stages)()
    next(mlp_stages)()
    next(mlp_stages)()
    gain_part[...] = jnp.zeros_like(gain_part)

    def back(rows, total):
        moved, terms = norm_back_rows(total, raw[rows].astype(F32), gains[0:1])
        gain_part[...] += terms[:8] + terms[8:]
        last[rows] = (grad_middle[rows] + moved).astype(BF16)

    sums.each(back)
    waits = [copies.swap(last, grad_in, partner, swaps)]
    row = lax.broadcasted_iota(jnp.int32, (8, 1), 0)
    gain_part[...] = jnp.where(
        row == 0,
        jnp.sum(gain_part[...], axis=0, keepdims=True),
        jnp.where(row == 1, jnp.sum(grad_gain2[...], axis=0, keepdims=True), 0.0),
    )
    here = 4 * z + x

    def lanes_of(block):
        return pl.ds(pl.multiple_of(block * 128, 128), 128)

    gain_copies = [
        copies.start(gain_part.at[:, lanes_of(4 * b + a)], gain_got.at[here], at_xz(a, b))
        for a, b in planes
    ]
    gain_own = copies.local(gain_part.at[:, lanes_of(here)], gain_got.at[here])
    for _ in range(4):
        next(att_stages)()
    for piece in range(PIECES):
        layers.arrive(piece)

    def add(rows):
        layer[rows] = (middle[rows] + layers.total(rows)).astype(BF16)

    row_steps(0, 128, add)
    waits.append(copies.swap(layer, layer_out, partner, swaps))
    for stage in mlp_stages:
        stage()
    for stage in att_stages:
        stage()

    def take(target):
        def act(rows, total):
            target[rows] = total.astype(BF16)

        return act

    mlp_plane.each(take(mlp_sum))
    send_back(mlp_sum, mlp_out)
    for copy in gain_copies:
        copy.wait_recv()
    gain_own.wait()
    gain_sum[...] = jnp.sum(gain_got[...], axis=0)
    for c, d in peers:
        back_copies.append(copies.start(gain_sum, gain_back.at[me], {"core": c, "y": d}))
    local.append(copies.local(gain_sum, gain_back.at[me]))
    att_plane.each(take(att_sum))
    send_back(att_sum, att_out)
    for copy in back_copies:
        copy.wait_recv()
    for copy in local:
        copy.wait()
    gain_out[...] = jnp.sum(gain_back[...], axis=0)
    for wait in waits:
        wait()
    copies.finish()


def unpack_kernel(
    att, mlp, gates, layer, last, hot, query, key, value, out, gate, up, down, layer_out, grad_in
):
    here = gate.shape[1] // 8
    for block in range(8):
        for source, at, grad in ((gates, 0, gate), (mlp, 0, up), (mlp, 1, down)):
            cut = source[block, :, at * PAD_FF : at * PAD_FF + here]
            grad[:, block * here : (block + 1) * here] = cut.astype(F32)
        value[:, block * 256 : (block + 1) * 256] = att[block, :, VALUE_AT].astype(F32)
        out[:, block * 256 : (block + 1) * 256] = att[block, :, OUT_AT].astype(F32)
        query[:, block * 32 : (block + 1) * 32] = att[block, :, 512:544].astype(F32)
        key[:, block * 32 : (block + 1) * 32] = att[block, :, 544:576].astype(F32)
    runs = layer.shape[1] // 256
    for run in range(runs):
        for source, target in ((layer, layer_out), (last, grad_in)):
            low = source[:, run * 128 : (run + 1) * 128]
            high = source[:, (runs + run) * 128 : (runs + run + 1) * 128]
            both = jnp.concatenate((low, high), axis=1)
            target[:, run * 256 : (run + 1) * 256] = nn(both, hot[...]).astype(target.dtype)


HBM, VMEM = pl.ANY, pltpu.VMEM


def call(kernel, number, ins, outs, scratch, sems, flops):
    def spec(space):
        return pl.BlockSpec(memory_space=space)

    remote = {}
    if number is not None:
        scratch = list(scratch) + [pltpu.SemaphoreType.DMA((sems,)), pltpu.SemaphoreType.DMA((sems,))]
        remote = dict(collective_id=number, has_side_effects=True)
    return pl.pallas_call(
        kernel,
        out_shape=[jax.ShapeDtypeStruct(shape, dtype) for shape, dtype, _ in outs],
        in_specs=[spec(space) for _, space in ins],
        out_specs=[spec(space) for _, _, space in outs],
        scratch_shapes=scratch,
        compiler_params=pltpu.CompilerParams(vmem_limit_bytes=VMEM_LIMIT, **remote),
        cost_estimate=pl.CostEstimate(flops=flops, bytes_accessed=2**26, transcendentals=0),
        name=kernel.__name__,
    )(*[array for array, _ in ins])


def ring_scratch(width, own=True):
    sums = [VMEM((4, 128, width), F32)] if own else []
    return sums + [
        VMEM((4, 128, width), BF16),
        VMEM((4, 128, width), BF16),
        VMEM((3, 128, width), BF16),
        VMEM((3, 128, width), BF16),
    ]


def plane_scratch(width):
    return [
        VMEM((4, 1, 128, width), BF16),
        VMEM((4, 3, 128, width), BF16),
        VMEM((4, 128, width), BF16),
        VMEM((1, 128, width), BF16),
        VMEM((3, 128, width), BF16),
    ]


def body(
    hidden_in,
    norm1_gain,
    query_weight,
    key_weight,
    value_weight,
    out_weight,
    norm2_gain,
    gate_weight,
    up_weight,
    down_weight,
    cotangent,
    source_id,
    source_counts,
):
    rows, toks, width = hidden_in.shape
    depth, ff = gate_weight.shape
    length, held = 8 * toks, 8 * depth
    mlp_w = 3 * PAD_FF
    scale = row_scale(source_id, source_counts).reshape(1, 1)
    (
        att,
        weights,
        raw_all,
        low,
        qs,
        ks,
        values,
        attended,
        shares,
        inverses,
        gains,
        raw,
        top,
        middle,
        normed2,
    ) = call(
        forward_kernel,
        0,
        [
            (array, VMEM)
            for array in (
                hidden_in.reshape(toks, width),
                cotangent.reshape(toks, width),
                scale,
                lane_order(False),
                query_weight,
                key_weight,
                value_weight,
                out_weight,
                gate_weight,
                up_weight,
                down_weight,
                jnp.stack((norm1_gain, norm2_gain), axis=1),
            )
        ],
        [
            ((width, ATT_W), BF16, HBM),
            ((width, mlp_w), BF16, HBM),
            ((length, width), BF16, HBM),
            ((length, width), BF16, HBM),
            ((length, 128), BF16, VMEM),
            ((length, 128), BF16, VMEM),
            ((length, 256), BF16, VMEM),
            ((length, 256), BF16, VMEM),
            ((length, 256), F32, VMEM),
            ((length, 128), F32, VMEM),
            ((8, width), F32, VMEM),
            ((toks, width), BF16, VMEM),
            ((toks, width), BF16, VMEM),
            ((toks, width), F32, VMEM),
            ((length, width), BF16, HBM),
        ],
        [
            VMEM((8, depth, ATT_W), BF16),
            VMEM((8, depth, mlp_w), BF16),
            VMEM((toks, width), BF16),
            VMEM((toks, width), BF16),
            VMEM((held, ATT_W), BF16),
            VMEM((held, mlp_w), BF16),
            VMEM((length, width), BF16),
            VMEM((width, ATT_W), BF16),
            VMEM((width, 384), BF16),
        ]
        + ring_scratch(width)
        + [VMEM((toks, width), BF16)],
        240,
        4 * 10**9,
    )
    grad_middle, grad_gain2, middle_low, grads, gate_sum, layer_parts = call(
        mlp_kernel,
        1,
        [
            (normed2, HBM),
            (low, HBM),
            (weights, HBM),
            (middle, VMEM),
            (top, VMEM),
            (gains, VMEM),
        ],
        [
            ((toks, width), F32, VMEM),
            ((8, width), F32, VMEM),
            ((length, width), BF16, HBM),
            ((width, 2 * PAD_FF), BF16, HBM),
            ((held, PAD_FF), BF16, VMEM),
            ((4, toks, width), BF16, HBM),
        ],
        [
            VMEM((length, width), BF16),
            VMEM((length, width), BF16),
            VMEM((width, mlp_w), BF16),
            VMEM((length, PAD_FF), BF16),
            VMEM((length, PAD_FF), BF16),
            VMEM((length, PAD_FF), BF16),
        ]
        + ring_scratch(width)
        + [
            VMEM((4, toks, width), BF16),
            VMEM((4, toks, width), BF16),
            VMEM((4, toks, width), BF16),
            VMEM((toks, width), BF16),
        ]
        + plane_scratch(PAD_FF),
        150,
        30 * 10**9,
    )
    att_back, mlp_back, gate_back, last, layer, gain_sums = call(
        back_kernel,
        2,
        [
            (middle_low, HBM),
            (raw_all, HBM),
            (att, VMEM),
            (qs, VMEM),
            (ks, VMEM),
            (values, VMEM),
            (attended, VMEM),
            (shares, VMEM),
            (inverses, VMEM),
            (raw, VMEM),
            (grad_middle, VMEM),
            (middle, VMEM),
            (gains, VMEM),
            (grad_gain2, VMEM),
            (grads, HBM),
            (layer_parts, HBM),
            (gate_sum, VMEM),
        ],
        [
            ((8, depth, ATT_W), BF16, HBM),
            ((8, depth, 2 * PAD_FF), BF16, HBM),
            ((8, depth, PAD_FF), BF16, HBM),
            ((toks, width), BF16, HBM),
            ((toks, width), BF16, HBM),
            ((8, 128), F32, VMEM),
        ],
        [
            VMEM((length, width), BF16),
            VMEM((width, 2 * PAD_FF), BF16),
            VMEM((width, ATT_W), BF16),
            VMEM((4, toks, width), BF16),
            VMEM((length, 256), BF16),
            VMEM((length, 256), F32),
            VMEM((length, 128), F32),
            VMEM((length, 128), F32),
            VMEM((length, 256), F32),
            VMEM((length, 128), BF16),
            VMEM((length, 256), BF16),
            VMEM((length, 128), BF16),
            VMEM((length, 256), BF16),
        ]
        + ring_scratch(width)
        + [VMEM((1, toks, width), BF16), VMEM((3, toks, width), BF16)]
        + plane_scratch(2 * PAD_FF)
        + plane_scratch(ATT_W)
        + [
            VMEM((held, 2 * PAD_FF), BF16),
            VMEM((held, ATT_W), BF16),
            VMEM((toks, width), BF16),
            VMEM((toks, width), BF16),
            VMEM((8, width), F32),
            VMEM((16, 8, 128), F32),
            VMEM((8, 128), F32),
            VMEM((8, 8, 128), F32),
        ],
        240,
        8 * 10**9,
    )
    grads_out = call(
        unpack_kernel,
        None,
        [(array, VMEM) for array in (att_back, mlp_back, gate_back, layer, last, lane_order(True))],
        [
            ((depth, query_weight.shape[1]), F32, VMEM),
            ((depth, key_weight.shape[1]), F32, VMEM),
            ((depth, value_weight.shape[1]), F32, VMEM),
            ((depth, out_weight.shape[1]), F32, VMEM),
            ((depth, ff), F32, VMEM),
            ((depth, ff), F32, VMEM),
            ((depth, ff), F32, VMEM),
            ((toks, width), BF16, VMEM),
            ((toks, width), F32, VMEM),
        ],
        [],
        0,
        0,
    )
    grad_query, grad_key, grad_value, grad_out, grad_gate, grad_up, grad_down = grads_out[:7]
    at = (lax.axis_index("core") * 4 + lax.axis_index("y")) * depth
    pair = lax.dynamic_slice(gain_sums, (0, at), (8, depth))
    return (
        grads_out[7].reshape(rows, toks, width),
        grads_out[8].reshape(rows, toks, width),
        pair[0],
        grad_query,
        grad_key,
        grad_value,
        grad_out,
        pair[1],
        grad_gate,
        grad_up,
        grad_down,
    )


def solution(mesh):
    zlo, chips_x, cores, chips_y, zhi = 2, 4, 2, 4, 2
    whole = Mesh(mesh.devices.reshape(zlo, chips_x, cores, chips_y, zhi), AXES)
    weight = P(AXES, None)
    gain = P(AXES)
    tokens = P(DP, SEQ, None)
    return jax.shard_map(
        body,
        mesh=whole,
        in_specs=(
            tokens,
            gain,
            weight,
            weight,
            weight,
            weight,
            gain,
            weight,
            weight,
            weight,
            tokens,
            P(DP),
            P(),
        ),
        out_specs=(
            tokens,
            tokens,
            gain,
            weight,
            weight,
            weight,
            weight,
            gain,
            weight,
            weight,
            weight,
        ),
        check_vma=False,
    )
```

```python
import jax
import jax.numpy as jnp
import numpy as np
from jax import lax
from jax.experimental import pallas as pl
from jax.experimental.pallas import tpu as pltpu
from jax.sharding import Mesh, PartitionSpec as P

FEAT = 16
HEAD_V = 128
PAD_FF = 768
ATT_W = 640
QK_AT = slice(512, 640)
OUT_AT = slice(256, 512)
VALUE_AT = slice(0, 256)
EARLY_W = 2 * PAD_FF + 256
LATE_W = 384

norm_eps = 1e-05
AXES = ("zlo", "x", "core", "y", "zhi")
DP = ("zlo", "x", "core")
SEQ = ("y", "zhi")

MESH = pl.DeviceIdType.MESH
VMEM_LIMIT = 61 * 2**20
PIECES = 4
TILE = 256
STEP = 16
BF16, F32 = jnp.bfloat16, jnp.float32


def row_scale(source_id, source_counts):
    picked = jnp.sum(
        jnp.where(
            source_id[:, None] == jnp.arange(source_counts.shape[0], dtype=jnp.int32)[None, :],
            source_counts[None, :],
            0,
        ),
        axis=1,
    )
    return 4.0 / jnp.sqrt(picked.astype(F32))


def lane_order(back):
    at = np.arange(256)
    to = (at // 16 % 2) * 128 + (at // 32) * 16 + at % 16
    hot = np.zeros((256, 256), np.float32)
    hot[at, to] = 1.0
    return jnp.asarray(hot.T if back else hot, BF16)


def place():
    z = lax.axis_index("zhi") * 2 + lax.axis_index("zlo")
    return lax.axis_index("x"), lax.axis_index("y"), z, lax.axis_index("core")


def around(index):
    return lax.rem(index + 8, 4)


def at_y(y):
    return {"y": around(y)}


def at_core(core):
    return {"core": core}


def at_xz(x, z):
    x, z = around(x), around(z)
    return {"x": x, "zhi": z // 2, "zlo": lax.rem(z, 2)}


def ring_peers(y, core):
    return [at_y(y + 1), at_y(y - 1), at_core(1 - core)]


def plane_peers(x, z):
    return [at_xz(x + 1, z), at_xz(x - 1, z), at_xz(x, z + 1), at_xz(x, z - 1)]


def group_peers(y, core):
    return [
        (lax.rem(core + dc, 2), lax.rem(y + dy, 4))
        for dc in (0, 1)
        for dy in range(4)
        if (dc, dy) != (0, 0)
    ]


def hello(devices, partner=None, swaps=None):
    barrier = pltpu.get_barrier_semaphore()
    for device in devices:
        pl.semaphore_signal(barrier, inc=1, device_id=device, device_id_type=MESH)
    count = len(devices)
    if partner is not None:

        @pl.when(swaps)
        def _():
            pl.semaphore_signal(barrier, inc=1, device_id=partner, device_id_type=MESH)

        count = count + jnp.where(swaps, 1, 0)

    def wait():
        pl.semaphore_wait(barrier, count)

    return wait


class Copies:
    def __init__(self, send, recv):
        self.send, self.recv, self.used, self.open = send, recv, 0, []

    def start(self, src, dst, device):
        copy = pltpu.make_async_remote_copy(
            src_ref=src,
            dst_ref=dst,
            send_sem=self.send.at[self.used],
            recv_sem=self.recv.at[self.used],
            device_id=device,
            device_id_type=MESH,
        )
        copy.start()
        self.used += 1
        self.open.append(copy)
        return copy

    def local(self, src, dst):
        copy = pltpu.make_async_copy(src, dst, self.send.at[self.used])
        copy.start()
        self.used += 1
        return copy

    def swap(self, src, dst, partner, swaps):
        at = self.used
        self.used += 1

        def over():
            return pltpu.make_async_remote_copy(
                src_ref=src,
                dst_ref=dst,
                send_sem=self.send.at[at],
                recv_sem=self.recv.at[at],
                device_id=partner,
                device_id_type=MESH,
            )

        def stay():
            return pltpu.make_async_copy(src, dst, self.send.at[at])

        @pl.when(swaps)
        def _():
            over().start()

        @pl.when(jnp.logical_not(swaps))
        def _():
            stay().start()

        def wait():
            @pl.when(swaps)
            def _():
                over().wait()

            @pl.when(jnp.logical_not(swaps))
            def _():
                stay().wait()

        return wait

    def finish(self):
        for copy in self.open:
            copy.wait_send()


def way(piece):
    return 1 if piece % 2 == 0 else -1


def slab(ref, block, rows, piece=None):
    if piece is None:
        return ref.at[pl.ds(pl.multiple_of(block * rows, 128), rows)]
    size = rows // PIECES
    return ref.at[pl.ds(pl.multiple_of(block * rows + piece * size, 32), size)]


def row_steps(start, size, act, step=STEP):
    @pl.loop(0, size // step, unroll=min(4, size // step))
    def _(at):
        act(pl.ds(pl.multiple_of(start + at * step, step), step))


class GatherRing:
    def __init__(self, copies, to, mine, full, block_of, me, rows):
        self.copies, self.to, self.full, self.block_of = copies, to, full, block_of
        self.me, self.rows, self.sent, self.onward = me, rows, {}, {}
        size = rows // PIECES
        for piece in range(PIECES):
            for step in (way(piece), -way(piece)):
                self.sent[step, piece] = copies.start(
                    mine.at[pl.ds(piece * size, size)],
                    slab(full, block_of(me), rows, piece),
                    to(me + step),
                )

    def forward(self):
        for piece in range(PIECES):
            step = way(piece)
            self.sent[step, piece].wait_recv()
            here = slab(self.full, self.block_of(self.me - step), self.rows, piece)
            self.onward[piece] = self.copies.start(here, here, self.to(self.me + step))

    def near(self):
        for piece in range(PIECES):
            self.sent[-way(piece), piece].wait_recv()

    def far(self):
        for piece in range(PIECES):
            self.onward[piece].wait_recv()


class GatherTokens:
    def __init__(self, copies, mine, full, y, core):
        self.copies, self.full, self.y, self.core = copies, full, y, core
        self.rows = mine.shape[0]
        self.shared = {}
        self.own = copies.local(mine, slab(full, self.block_of(y), self.rows))
        self.shared[0] = copies.start(mine, slab(full, self.block_of(y), self.rows), at_core(1 - core))
        self.ring = GatherRing(copies, at_y, mine, full, self.block_of, y, self.rows)

    def block_of(self, index):
        return around(index) * 2 + self.core

    def share(self, k):
        here = slab(self.full, self.block_of(self.y + k), self.rows)
        self.shared[k] = self.copies.start(here, here, at_core(1 - self.core))

    def forward(self):
        self.ring.forward()

    def near(self):
        self.ring.near()
        self.share(1)
        self.share(-1)

    def far(self):
        self.ring.far()
        self.share(2)

    def finish(self):
        self.own.wait()
        for copy in self.shared.values():
            copy.wait_recv()


class GatherPlane:
    def __init__(self, copies, mine, full, x, z, core):
        self.copies, self.full = copies, full
        rows = mine.shape[0]

        def block(a, b):
            a, b = around(a), around(b)
            return jnp.where(core == 0, 4 * b + a, 4 * a + b)

        first, second = jnp.where(core == 0, x, z), jnp.where(core == 0, z, x)

        def to_first(index):
            return at_xz(jnp.where(core == 0, index, x), jnp.where(core == 0, z, index))

        def to_second(index):
            return at_xz(jnp.where(core == 0, x, index), jnp.where(core == 0, index, z))

        def onto(k, source=None):
            a = first + k
            if source is None:
                source = slab(full, block(a, second), rows)
            return GatherRing(copies, to_second, source, full, lambda b: block(a, b), second, rows)

        self.onto = onto
        self.own = copies.local(mine, slab(full, block(first, second), rows))
        self.ring = GatherRing(
            copies, to_first, mine, full, lambda a: block(a, second), first, rows
        )
        self.rings = {0: onto(0, mine)}

    def stages(self):
        def one():
            self.ring.forward()

        def two():
            self.ring.near()
            self.rings[1] = self.onto(1)
            self.rings[-1] = self.onto(-1)

        def three():
            self.rings[0].forward()

        def four():
            self.ring.far()
            self.rings[2] = self.onto(2)

        def five():
            self.rings[1].forward()
            self.rings[-1].forward()

        def six():
            self.rings[2].forward()
            self.rings[0].near()
            self.rings[0].far()

        def seven():
            for k in (1, -1, 2):
                self.rings[k].near()
                self.rings[k].far()
            self.own.wait()

        return [one, two, three, four, five, six, seven]


class ReduceRing:
    def __init__(self, copies, to, me, read, out, got, rows, source=None):
        self.copies, self.to, self.me, self.read = copies, to, me, read
        self.out, self.got, self.rows, self.source, self.sent = out, got, rows, source, {}
        self.size = rows // PIECES

    def span(self, piece):
        return pl.ds(piece * self.size, self.size)

    def push(self, slot, k, piece, device):
        span = self.span(piece)
        if self.source is not None:
            ref = self.source(k, span)
        else:

            def fill(rows):
                self.out[slot, rows] = self.read(k, rows).astype(BF16)

            row_steps(piece * self.size, self.size, fill)
            ref = self.out.at[slot, span]
        self.sent[slot, piece] = self.copies.start(ref, self.got.at[slot, span], device)

    def far(self, pieces=range(PIECES)):
        for piece in pieces:
            self.push(0, 2, piece, self.to(self.me + way(piece)))

    def direct(self, k):
        for piece in range(PIECES):
            if way(piece) == -k:
                self.push(1, k, piece, self.to(self.me + k))

    def onward(self, k):
        slot = 2 if self.source is None else 0
        for piece in range(PIECES):
            if way(piece) == k:
                self.sent[0, piece].wait_recv()

                def fill(rows):
                    self.out[slot, rows] = (
                        self.read(k, rows) + self.got[0, rows].astype(F32)
                    ).astype(BF16)

                row_steps(piece * self.size, self.size, fill)
                span = self.span(piece)
                self.sent[2, piece] = self.copies.start(
                    self.out.at[slot, span], self.got.at[2, span], self.to(self.me + k)
                )

    def arrive(self, piece):
        self.sent[1, piece].wait_recv()
        self.sent[2, piece].wait_recv()

    def total(self, rows):
        return self.read(0, rows) + self.got[1, rows].astype(F32) + self.got[2, rows].astype(F32)


class ReduceTokens:
    def __init__(self, copies, make, y, core, own, sib, got_sib, out, got):
        self.copies, self.make, self.y, self.core = copies, make, y, core
        self.own, self.sib, self.got_sib, self.shared = own, sib, got_sib, {}
        self.ring = ReduceRing(copies, at_y, y, self.read, out, got, own.shape[1])

    def read(self, k, rows):
        return self.own[k % 4, rows] + self.got_sib[k % 4, rows].astype(F32)

    def share(self, k):
        self.shared[k] = self.copies.start(
            self.sib.at[k % 4], self.got_sib.at[k % 4], at_core(1 - self.core)
        )

    def part(self, k):
        self.make(k, self.own.at[k % 4], self.sib.at[k % 4])
        self.share(k)

    def one(self):
        self.shared[2].wait_recv()
        self.ring.far()
        self.shared[1].wait_recv()
        self.ring.direct(1)

    def two(self):
        self.shared[-1].wait_recv()
        self.ring.direct(-1)
        self.ring.onward(1)
        self.ring.onward(-1)
        self.shared[0].wait_recv()

    def each(self, act):
        for piece in range(PIECES):
            self.ring.arrive(piece)

            def take(rows):
                act(rows, self.ring.total(rows))

            row_steps(piece * self.ring.size, self.ring.size, take)


class ReducePlane:
    def __init__(self, copies, parts, lanes, x, z, core, out1, got1, mid, out2, got2, sent=None):
        rows = mid.shape[1]
        sent = parts if sent is None else sent

        def block(a, b):
            a, b = around(a), around(b)
            return jnp.where(core == 0, 4 * b + a, 4 * a + b)

        last, first = jnp.where(core == 0, x, z), jnp.where(core == 0, z, x)

        def to_last(index):
            return at_xz(jnp.where(core == 0, index, x), jnp.where(core == 0, z, index))

        def to_first(index):
            return at_xz(jnp.where(core == 0, x, index), jnp.where(core == 0, index, z))

        def ring(k):
            def place_of(step, span):
                start = block(last + k, first + step) * rows + span.start
                return pl.ds(pl.multiple_of(start, STEP), span.size)

            def read(step, span):
                return parts[place_of(step, span), lanes].astype(F32)

            def source(step, span):
                return sent.at[place_of(step, span), lanes]

            return ReduceRing(copies, to_first, first, read, out1.at[k % 4], got1.at[k % 4], rows, source)

        self.mid = mid
        self.rings = {k: ring(k) for k in (2, 1, -1, 0)}

        def read2(step, span):
            return mid[step % 4, span].astype(F32)

        def source2(step, span):
            return mid.at[step % 4, span]

        self.ring = ReduceRing(copies, to_last, last, read2, out2, got2, rows, source2)

    def start(self):
        for ring in self.rings.values():
            ring.far()

    def direct(self):
        for ring in self.rings.values():
            ring.direct(1)
            ring.direct(-1)

    def onward(self, k):
        self.rings[k].onward(1)
        self.rings[k].onward(-1)

    def middle(self, k):
        ring = self.rings[k]
        for piece in range(PIECES):
            ring.arrive(piece)

            def fill(rows):
                self.mid[k % 4, rows] = ring.total(rows).astype(BF16)

            row_steps(piece * ring.size, ring.size, fill)

    def stages(self):
        def ends(k, then):
            def act():
                self.middle(k)
                then()

            return act

        return (
            [self.start, self.direct]
            + [lambda k=k: self.onward(k) for k in (2, 1, -1, 0)]
            + [
                ends(2, self.ring.far),
                ends(1, lambda: self.ring.direct(1)),
                ends(-1, lambda: self.ring.direct(-1)),
                ends(0, lambda: None),
                lambda: (self.ring.onward(1), self.ring.onward(-1)),
            ]
        )

    def each(self, act):
        for piece in range(PIECES):
            self.ring.arrive(piece)

            def take(rows):
                act(rows, self.ring.total(rows))

            row_steps(piece * self.ring.size, self.ring.size, take)


def nt(left, right):
    return lax.dot_general(left, right, (((1,), (1,)), ((), ())), preferred_element_type=F32)


def tn(left, right):
    return lax.dot_general(left, right, (((0,), (0,)), ((), ())), preferred_element_type=F32)


def nn(left, right):
    return jnp.dot(left, right, preferred_element_type=F32)


def chip_rows(block):
    return pl.ds(pl.multiple_of(block * 256, 256), 256)


def part_maker(pairs, y, core):
    def make(k, mine, theirs):
        rows = chip_rows(around(y + k))

        @pl.loop(0, mine.shape[-1] // TILE)
        def _(tile):
            columns = pl.ds(pl.multiple_of(tile * TILE, TILE), TILE)
            total = None
            for left, right, lanes in pairs:
                term = nt(left[rows, :], right[columns, lanes])
                total = term if total is None else total + term
            low, high = total[:128], total[128:]
            mine[:, columns] = jnp.where(core == 0, low, high)
            theirs[:, columns] = jnp.where(core == 0, high, low).astype(BF16)

    return make


def inverse_of(value):
    return lax.rsqrt(jnp.mean(value * value, axis=-1, keepdims=True) + norm_eps)


def norm_back_rows(grad, value, gain):
    inverse = inverse_of(value)
    unit = value * inverse
    scaled = grad * gain
    moved = inverse * (scaled - unit * jnp.mean(scaled * unit, axis=-1, keepdims=True))
    return moved, grad * unit


def reorder_into(target, source, hot):
    runs = source.shape[1] // 256
    for run in range(runs):
        moved = nn(source[:, run * 256 : (run + 1) * 256], hot[...]).astype(BF16)
        target[:, run * 128 : (run + 1) * 128] = moved[:, :128]
        target[:, (runs + run) * 128 : (runs + run + 1) * 128] = moved[:, 128:]


def gain_rows(att):
    row = lax.broadcasted_iota(jnp.int32, (8, 128), 0)
    lane = lax.broadcasted_iota(jnp.int32, (8, 128), 1)
    pick = jnp.where((lane == row + 64) & (row < 2), 1.0, 0.0).astype(BF16)
    return nt(pick, att[:, QK_AT])


def head_lanes(head):
    lane = lax.broadcasted_iota(jnp.int32, (1, 128), 1)
    return (lane >= head * FEAT) & (lane < (head + 1) * FEAT)


def scores_of(q, k, block, extent):
    x = nt(q, k) * 0.25
    row = lax.broadcasted_iota(jnp.int32, (256, extent), 0) + block * 256
    keep = row >= lax.broadcasted_iota(jnp.int32, (256, extent), 1)
    return x, jnp.where(keep, 1.0 + x + 0.5 * (x * x), 0.0), keep


def forward_kernel(
    hidden,
    cotangent,
    scale,
    hot,
    query,
    key,
    value,
    out_weight,
    gate,
    up,
    down,
    gain_pair,
    att_out,
    weights,
    raw_out,
    low_out,
    qs,
    ks,
    values,
    attended,
    shares,
    inverses,
    gains,
    raw,
    top,
    middle,
    normed2,
    att_cut,
    mlp_cut,
    raw_cut,
    top_cut,
    att_own,
    mlp_own,
    raw_all,
    att_all,
    att_scaled,
    own,
    sib,
    got_sib,
    out,
    got,
    low,
    send,
    recv,
):
    x, y, z, core = place()
    zhi = z // 2
    partner = {"core": 1 - core, "zhi": 1 - zhi}
    swaps = core != zhi
    peers = group_peers(y, core)
    ready = hello(
        [{"core": c, "y": d} for c, d in peers] + plane_peers(x, z), partner, swaps
    )
    copies = Copies(send, recv)
    me = core * 4 + y
    depth, here = gate.shape[0], gate.shape[1] // 8

    def spread(cuts, target):
        rows = pl.ds(pl.multiple_of(me * depth, depth), depth)
        kept = copies.local(cuts.at[me], target.at[rows])
        got = [
            copies.start(cuts.at[c * 4 + d], target.at[rows], {"core": c, "y": d}) for c, d in peers
        ]

        def wait():
            kept.wait()
            for copy in got:
                copy.wait_recv()

        return wait

    reorder_into(raw_cut, hidden, hot)
    gap = jnp.zeros((depth, 62), BF16)
    for block in range(8):
        att_cut[block, :, VALUE_AT] = value[:, block * 256 : (block + 1) * 256]
        att_cut[block, :, OUT_AT] = out_weight[:, block * 256 : (block + 1) * 256]
        att_cut[block, :, QK_AT] = jnp.concatenate(
            (
                query[:, block * 32 : (block + 1) * 32],
                key[:, block * 32 : (block + 1) * 32],
                gain_pair[...],
                gap,
            ),
            axis=1,
        )
    ready()
    wait_raw = copies.swap(raw_cut, raw, partner, swaps)
    wait_att = spread(att_cut, att_own)
    gap = jnp.zeros((depth, PAD_FF - here), BF16)
    for block in range(8):
        for at, weight in enumerate((gate, up, down)):
            cut = weight[:, block * here : (block + 1) * here]
            mlp_cut[block, :, at * PAD_FF : (at + 1) * PAD_FF] = jnp.concatenate((cut, gap), axis=1)
    wait_raw()
    tokens = GatherTokens(copies, raw, raw_all, y, core)
    wait_mlp = spread(mlp_cut, mlp_own)

    def weigh(rows):
        top_cut[rows] = (cotangent[rows].astype(F32) * scale[...]).astype(BF16)

    row_steps(0, top_cut.shape[0], weigh)
    reorder_into(top_cut, top_cut[...], hot)
    wait_att()
    plane = GatherPlane(copies, att_own, att_all, x, z, core)
    wait_top = copies.swap(top_cut, top, partner, swaps)

    def invert(block):
        def act(rows):
            inverse = inverse_of(raw_all[rows].astype(F32))
            inverses[rows] = jnp.broadcast_to(inverse, (STEP, 128))

        row_steps(block * 128, 128, act)

    one, two, three, four, five, six, seven = plane.stages()
    one()
    two()
    tokens.forward()
    three()
    four()
    tokens.shared[0].wait_recv()
    tokens.own.wait()
    invert(2 * y)
    invert(2 * y + 1)
    five()
    six()
    wait_mlp()
    mlp_plane = GatherPlane(copies, mlp_own, weights, x, z, core)
    mlp_stages = iter(mlp_plane.stages())
    tokens.near()
    invert(2 * around(y + 1) + core)
    invert(2 * around(y - 1) + core)
    tokens.far()
    invert(2 * around(y + 2) + core)
    seven()
    gains[...] = gain_rows(att_all)

    def scale_rows(rows):
        gain = att_all[rows, 576:577].astype(F32)
        att_scaled[rows, 0:256] = (att_all[rows, VALUE_AT].astype(F32) * gain).astype(BF16)
        att_scaled[rows, 256:384] = (att_all[rows, QK_AT].astype(F32) * gain).astype(BF16)

    row_steps(0, att_all.shape[0], scale_rows, 128)
    tokens.shared[1].wait_recv()
    tokens.shared[-1].wait_recv()
    invert(2 * around(y + 1) + 1 - core)
    invert(2 * around(y - 1) + 1 - core)
    tokens.shared[2].wait_recv()
    invert(2 * around(y + 2) + 1 - core)
    wait_top()
    tops = GatherTokens(copies, top, low_out, y, core)
    kept = [copies.local(att_all, att_out), copies.local(raw_all, raw_out)]

    @pl.loop(0, 2, unroll=True)
    def _(half):
        rows = pl.ds(pl.multiple_of(half * 512, 512), 512)
        inverse = inverses[rows]
        block = raw_all[rows]
        both = nn(block, att_scaled[:, 0:256])
        values[rows] = (both * jnp.concatenate((inverse, inverse), axis=1)).astype(BF16)
        both = nn(block, att_scaled[:, 256:384]) * inverse
        lane = lax.broadcasted_iota(jnp.int32, (1, 128), 1)
        qs[rows] = jnp.where(lane < 32, both, 0.0).astype(BF16)
        ks[rows] = jnp.where(lane < 32, pltpu.roll(both, 96, 1), 0.0).astype(BF16)

    for head in range(2):
        lanes = slice(head * HEAD_V, (head + 1) * HEAD_V)
        for block in range(4):
            rows, extent = slice(block * 256, (block + 1) * 256), (block + 1) * 256
            q = jnp.where(head_lanes(head), qs[rows], 0)
            unused, scores, unused_keep = scores_of(q, ks[0:extent], block, extent)
            share = 1.0 / jnp.sum(scores, axis=-1, keepdims=True)
            numer = nn(scores.astype(BF16), values[0:extent, lanes])
            attended[rows, lanes] = (numer * share).astype(BF16)
            shares[rows, lanes] = jnp.broadcast_to(share, (256, HEAD_V))
    for _ in range(3):
        next(mlp_stages)()
    tops.forward()
    sums = ReduceTokens(
        copies, part_maker([(attended, att_all, OUT_AT)], y, core), y, core, own, sib, got_sib, out, got
    )
    for k in (2, 1, -1):
        sums.part(k)
    sums.one()
    sums.part(0)
    next(mlp_stages)()
    sums.two()
    next(mlp_stages)()
    tops.near()

    def norm2(rows, total):
        value = raw[rows].astype(F32) + total
        middle[rows] = value
        low[rows] = (value * inverse_of(value) * gains[1:2]).astype(BF16)

    sums.each(norm2)
    back = GatherTokens(copies, low, normed2, y, core)
    next(mlp_stages)()
    tops.far()
    back.forward()
    back.near()
    back.far()
    next(mlp_stages)()
    tops.finish()
    back.finish()
    for copy in kept:
        copy.wait()
    copies.finish()


def mlp_kernel(
    normed2_in,
    low_in,
    weights_in,
    middle,
    top,
    gains,
    grad_middle,
    grad_gain,
    middle_low,
    grads,
    gate_sum,
    layer_parts,
    normed2,
    grad_low,
    weights,
    hidden,
    gate_act,
    up_act,
    own,
    sib,
    got_sib,
    out,
    got,
    sib2,
    got_sib2,
    layer,
    low,
    plane_out1,
    plane_got1,
    plane_mid,
    plane_out2,
    plane_got2,
    send,
    recv,
):
    x, y, z, core = place()
    copies = Copies(send, recv)
    ready = hello(ring_peers(y, core) + plane_peers(x, z))
    order = (2, 1, -1, 0)
    loads = {}

    def load(k):
        slot = order.index(k)
        for at, owner in enumerate((core, 1 - core)):
            block = around(y + k) * 2 + owner
            rows = pl.ds(slot * 256 + at * 128, 128)
            for source, target in ((normed2_in, normed2), (low_in, grad_low)):
                loads.setdefault(k, []).append(copies.local(slab(source, block, 128), target.at[rows]))

    def lanes(at):
        return slice(at * PAD_FF, (at + 1) * PAD_FF)

    load(2)
    load(1)
    loads["w"] = [copies.local(weights_in.at[:, lanes(at)], weights.at[:, lanes(at)]) for at in range(3)]
    load(-1)
    load(0)
    ready()

    def act_tile(half, tile):
        rows = slice(half * 512, (half + 1) * 512)
        here = slice(tile * TILE, (tile + 1) * TILE)

        def cut(at):
            return weights[:, at * PAD_FF + tile * TILE : at * PAD_FF + (tile + 1) * TILE]

        block = normed2[rows]
        gate = nn(block, cut(0))
        upward = nn(block, cut(1))
        grad_hidden = nn(grad_low[rows], cut(2))
        sigma = jax.nn.sigmoid(gate)
        silu = gate * sigma
        hidden[rows, here] = (silu * upward).astype(BF16)
        slope = sigma + silu * (1.0 - sigma)
        gate_act[rows, here] = (grad_hidden * upward * slope).astype(BF16)
        up_act[rows, here] = (grad_hidden * silu).astype(BF16)

    def part_pair(half, pairs, sib_ref):
        rows = slice(half * 512, (half + 1) * 512)

        @pl.loop(0, own.shape[-1] // 512)
        def _(tile):
            columns = pl.ds(pl.multiple_of(tile * 512, 512), 512)
            total = None
            for left, right in pairs:
                term = nt(left[rows, :], weights[columns, right])
                total = term if total is None else total + term
            for at in range(2):
                k = order[2 * half + at] % 4
                own[k, :, columns] = total[at * 256 : at * 256 + 128]
                sib_ref[k, :, columns] = total[at * 256 + 128 : at * 256 + 256].astype(BF16)

    def grad_block(at, left, right):
        @pl.loop(0, left.shape[1] // 512)
        def _(tile):
            columns = pl.ds(pl.multiple_of(tile * 512, 512), 512)
            weights[columns, lanes(at)] = tn(left[:, columns], right[...]).astype(BF16)

    sums = ReduceTokens(copies, None, y, core, own, sib, got_sib, out, got)
    acts = [(gate_act, lanes(0)), (up_act, lanes(1))]
    for copy in loads[2] + loads[1] + loads["w"]:
        copy.wait()
    for tile in range(3):
        act_tile(0, tile)
    part_pair(0, acts, sib)
    sums.share(2)
    sums.share(1)
    for copy in loads[-1] + loads[0]:
        copy.wait()
    act_tile(1, 0)
    sums.one()
    act_tile(1, 1)
    act_tile(1, 2)
    part_pair(1, acts, sib)
    sums.share(-1)
    sums.share(0)
    sums.two()
    grad_block(0, normed2, gate_act)
    plane = ReducePlane(
        copies, weights, lanes(0), x, z, core, plane_out1, plane_got1, plane_mid, plane_out2, plane_got2
    )
    stages = iter(plane.stages())
    next(stages)()
    grad_gain[...] = jnp.zeros_like(grad_gain)

    def back(rows, total):
        moved, terms = norm_back_rows(total, middle[rows], gains[1:2])
        grad_gain[...] += terms[:8] + terms[8:]
        value = top[rows].astype(F32) + moved
        grad_middle[rows] = value
        low[rows] = value.astype(BF16)

    sums.each(back)
    gather = GatherTokens(copies, low, middle_low, y, core)
    next(stages)()
    grad_block(1, normed2, up_act)
    layers = ReduceTokens(copies, None, y, core, own, sib2, got_sib2, None, None)
    part_pair(0, [(hidden, lanes(2))], sib2)
    layers.share(2)
    layers.share(1)
    gather.forward()
    for _ in range(4):
        next(stages)()
    part_pair(1, [(hidden, lanes(2))], sib2)
    layers.share(-1)
    layers.share(0)
    gather.near()
    grad_block(2, grad_low, hidden)
    stored = [
        copies.local(weights.at[:, PAD_FF : 3 * PAD_FF], grads),
    ]
    for _ in range(4):
        next(stages)()
    gather.far()
    for stage in stages:
        stage()
    for k in order:
        layers.shared[k].wait_recv()

        def add(rows, k=k):
            layer[k % 4, rows] = layers.read(k, rows).astype(BF16)

        row_steps(0, 128, add)
    stored.append(copies.local(layer, layer_parts))

    def take(rows, total):
        gate_sum[rows] = total.astype(BF16)

    plane.each(take)
    gather.finish()
    for copy in stored:
        copy.wait()
    copies.finish()


def back_kernel(
    low_in,
    raw_in,
    att,
    qs,
    ks,
    values,
    attended,
    shares,
    inverses,
    raw,
    grad_middle,
    middle,
    gains,
    grad_gain2,
    grads_in,
    layer_in,
    gate_sum,
    late_out,
    early_out,
    gate_out,
    grad_in,
    layer_out,
    gain_out,
    tokens,
    early,
    late,
    layer_parts,
    grad_numer,
    grad_denom,
    grad_q,
    grad_k,
    grad_v,
    grad_qk,
    grad_values,
    scaled_qk,
    scaled_values,
    own,
    sib,
    got_sib,
    out,
    got,
    layer_sent,
    layer_got,
    early_out1,
    early_got1,
    early_mid,
    early_out2,
    early_got2,
    late_out1,
    late_got1,
    late_mid,
    late_out2,
    late_got2,
    early_sum,
    late_sum,
    last,
    layer,
    gain_part,
    gain_got,
    gain_sum,
    gain_back,
    send,
    recv,
):
    x, y, z, core = place()
    zhi = z // 2
    partner = {"core": 1 - core, "zhi": 1 - zhi}
    swaps = core != zhi
    copies = Copies(send, recv)
    peers = group_peers(y, core)
    planes = [
        (lax.rem(x + dx, 4), lax.rem(z + dz, 4))
        for dx in range(4)
        for dz in range(4)
        if (dx, dz) != (0, 0)
    ]
    ready = hello(
        [{"core": c, "y": d} for c, d in peers] + [at_xz(a, b) for a, b in planes], partner, swaps
    )
    load_low = copies.local(low_in, tokens)
    load_early = copies.local(grads_in, early.at[:, 0 : 2 * PAD_FF])
    load_layer = copies.local(layer_in, layer_parts)
    ready()
    layers = ReduceRing(
        copies,
        at_y,
        y,
        lambda k, rows: layer_parts[k % 4, rows].astype(F32),
        layer_sent,
        layer_got,
        128,
        lambda k, span: layer_in.at[k % 4, span],
    )
    layers.far()
    layers.direct(1)
    layers.direct(-1)
    load_low.wait()

    @pl.loop(0, tokens.shape[1] // 512)
    def _(tile):
        columns = pl.ds(pl.multiple_of(tile * 512, 512), 512)
        early[columns, 2 * PAD_FF : EARLY_W] = tn(tokens[:, columns], attended[...]).astype(BF16)

    load_early.wait()
    early_plane = ReducePlane(
        copies,
        early,
        slice(0, EARLY_W),
        x,
        z,
        core,
        early_out1,
        early_got1,
        early_mid,
        early_out2,
        early_got2,
    )
    early_stages = iter(early_plane.stages())
    next(early_stages)()
    me = core * 4 + y
    back_copies, local = [], []

    def send_back(sums_ref, out_ref):
        def cut(index):
            return sums_ref.at[pl.ds(pl.multiple_of(index * 16, 16), 16)]

        local.append(copies.local(cut(me), out_ref.at[me]))
        for c, d in peers:
            back_copies.append(copies.start(cut(c * 4 + d), out_ref.at[me], {"core": c, "y": d}))

    send_back(gate_sum, gate_out)

    @pl.loop(0, 2, unroll=True)
    def _(half):
        rows = pl.ds(pl.multiple_of(half * 512, 512), 512)
        grad_mixed = nn(tokens[rows], att[:, OUT_AT]).astype(BF16).astype(F32)
        numer = grad_mixed * shares[rows]
        grad_numer[rows] = numer.astype(BF16)
        product = numer * attended[rows].astype(F32)
        for head in range(2):
            lanes = slice(head * HEAD_V, (head + 1) * HEAD_V)
            total = -jnp.sum(product[:, lanes], axis=-1, keepdims=True)
            grad_denom[rows, lanes] = jnp.broadcast_to(total, (512, HEAD_V))

    load_raw = copies.local(raw_in, tokens)
    grad_k[...] = jnp.zeros_like(grad_k)
    grad_v[...] = jnp.zeros_like(grad_v)

    def attend_back(head, block):
        lanes = slice(head * HEAD_V, (head + 1) * HEAD_V)
        rows, extent = slice(block * 256, (block + 1) * 256), (block + 1) * 256
        q = jnp.where(head_lanes(head), qs[rows], 0)
        k = ks[0:extent]
        half, scores, keep = scores_of(q, k, block, extent)
        numer = grad_numer[rows, lanes]
        total = grad_denom[rows, head * HEAD_V : head * HEAD_V + 1]
        grad_scores = nt(numer, values[0:extent, lanes]) + total
        grad_s = jnp.where(keep, grad_scores * (0.25 + 0.25 * half), 0.0).astype(BF16)
        moved = nn(grad_s, k)
        if head == 0:
            grad_q[rows] = jnp.where(head_lanes(0), moved, 0.0)
        else:
            grad_q[rows] += jnp.where(head_lanes(1), moved, 0.0)
        grad_k[0:extent] += tn(grad_s, q)
        grad_v[0:extent, lanes] += tn(scores.astype(BF16), numer)

    for block in range(4):
        attend_back(0, block)
    next(early_stages)()
    for block in range(4):
        attend_back(1, block)

    def join(rows):
        inverse = inverses[rows]
        both = grad_q[rows] + pltpu.roll(grad_k[rows], 32, 1)
        grad_qk[rows] = both.astype(BF16)
        scaled_qk[rows] = (both * inverse).astype(BF16)
        both = grad_v[rows]
        grad_values[rows] = both.astype(BF16)
        scaled_values[rows] = (both * jnp.concatenate((inverse, inverse), axis=1)).astype(BF16)

    row_steps(0, 1024, join, 128)
    sums = ReduceTokens(
        copies,
        part_maker([(grad_values, att, VALUE_AT), (grad_qk, att, QK_AT)], y, core),
        y,
        core,
        own,
        sib,
        got_sib,
        out,
        got,
    )
    sums.part(2)
    sums.part(1)
    for _ in range(4):
        next(early_stages)()
    sums.one()
    sums.part(-1)
    sums.part(0)
    load_layer.wait()
    layers.onward(1)
    layers.onward(-1)
    load_raw.wait()

    @pl.loop(0, tokens.shape[1] // 512)
    def _(tile):
        columns = pl.ds(pl.multiple_of(tile * 512, 512), 512)
        left = tokens[:, columns]
        gain = att[columns, 576:577].astype(F32)
        late[columns, 0:256] = (tn(left, scaled_values[...]) * gain).astype(BF16)
        late[columns, 256:LATE_W] = (tn(left, scaled_qk[...]) * gain).astype(BF16)

    late_plane = ReducePlane(
        copies,
        late,
        slice(0, LATE_W),
        x,
        z,
        core,
        late_out1,
        late_got1,
        late_mid,
        late_out2,
        late_got2,
    )
    late_stages = iter(late_plane.stages())
    next(late_stages)()
    sums.two()
    next(late_stages)()
    for _ in range(4):
        next(late_stages)()

    def take(target):
        def act(rows, total):
            target[rows] = total.astype(BF16)

        return act

    gain_part[...] = jnp.zeros_like(gain_part)

    def back(rows, total):
        moved, terms = norm_back_rows(total, raw[rows].astype(F32), gains[0:1])
        gain_part[...] += terms[:8] + terms[8:]
        last[rows] = (grad_middle[rows] + moved).astype(BF16)

    sums.each(back)
    waits = [copies.swap(last, grad_in, partner, swaps)]
    row = lax.broadcasted_iota(jnp.int32, (8, 1), 0)
    gain_part[...] = jnp.where(
        row == 0,
        jnp.sum(gain_part[...], axis=0, keepdims=True),
        jnp.where(row == 1, jnp.sum(grad_gain2[...], axis=0, keepdims=True), 0.0),
    )
    here = 4 * z + x

    def lanes_of(block):
        return pl.ds(pl.multiple_of(block * 128, 128), 128)

    gain_copies = [
        copies.start(gain_part.at[:, lanes_of(4 * b + a)], gain_got.at[here], at_xz(a, b))
        for a, b in planes
    ]
    gain_own = copies.local(gain_part.at[:, lanes_of(here)], gain_got.at[here])
    for stage in early_stages:
        stage()
    for _ in range(4):
        next(late_stages)()
    for piece in range(PIECES):
        layers.arrive(piece)

    def add(rows):
        layer[rows] = (middle[rows] + layers.total(rows)).astype(BF16)

    row_steps(0, 128, add)
    waits.append(copies.swap(layer, layer_out, partner, swaps))
    early_plane.each(take(early_sum))
    send_back(early_sum, early_out)
    for stage in late_stages:
        stage()
    for copy in gain_copies:
        copy.wait_recv()
    gain_own.wait()
    gain_sum[...] = jnp.sum(gain_got[...], axis=0)
    for c, d in peers:
        back_copies.append(copies.start(gain_sum, gain_back.at[me], {"core": c, "y": d}))
    local.append(copies.local(gain_sum, gain_back.at[me]))
    late_plane.each(take(late_sum))
    send_back(late_sum, late_out)
    for copy in back_copies:
        copy.wait_recv()
    for copy in local:
        copy.wait()
    gain_out[...] = jnp.sum(gain_back[...], axis=0)
    for wait in waits:
        wait()
    copies.finish()


def unpack_kernel(
    late, early, gates, layer, last, hot, query, key, value, out, gate, up, down, layer_out, grad_in
):
    here = gate.shape[1] // 8
    for block in range(8):
        for source, at, grad in ((gates, 0, gate), (early, 0, up), (early, 1, down)):
            cut = source[block, :, at * PAD_FF : at * PAD_FF + here]
            grad[:, block * here : (block + 1) * here] = cut.astype(F32)
        value[:, block * 256 : (block + 1) * 256] = late[block, :, 0:256].astype(F32)
        out[:, block * 256 : (block + 1) * 256] = early[block, :, 2 * PAD_FF : EARLY_W].astype(F32)
        query[:, block * 32 : (block + 1) * 32] = late[block, :, 256:288].astype(F32)
        key[:, block * 32 : (block + 1) * 32] = late[block, :, 288:320].astype(F32)
    runs = layer.shape[1] // 256
    for run in range(runs):
        for source, target in ((layer, layer_out), (last, grad_in)):
            low = source[:, run * 128 : (run + 1) * 128]
            high = source[:, (runs + run) * 128 : (runs + run + 1) * 128]
            both = jnp.concatenate((low, high), axis=1)
            target[:, run * 256 : (run + 1) * 256] = nn(both, hot[...]).astype(target.dtype)


HBM, VMEM = pl.ANY, pltpu.VMEM


def call(kernel, number, ins, outs, scratch, sems, flops):
    def spec(space):
        return pl.BlockSpec(memory_space=space)

    remote = {}
    if number is not None:
        scratch = list(scratch) + [pltpu.SemaphoreType.DMA((sems,)), pltpu.SemaphoreType.DMA((sems,))]
        remote = dict(collective_id=number, has_side_effects=True)
    return pl.pallas_call(
        kernel,
        out_shape=[jax.ShapeDtypeStruct(shape, dtype) for shape, dtype, _ in outs],
        in_specs=[spec(space) for _, space in ins],
        out_specs=[spec(space) for _, _, space in outs],
        scratch_shapes=scratch,
        compiler_params=pltpu.CompilerParams(vmem_limit_bytes=VMEM_LIMIT, **remote),
        cost_estimate=pl.CostEstimate(flops=flops, bytes_accessed=2**26, transcendentals=0),
        name=kernel.__name__,
    )(*[array for array, _ in ins])


def ring_scratch(width, own=True):
    sums = [VMEM((4, 128, width), F32)] if own else []
    return sums + [
        VMEM((4, 128, width), BF16),
        VMEM((4, 128, width), BF16),
        VMEM((3, 128, width), BF16),
        VMEM((3, 128, width), BF16),
    ]


def plane_scratch(width):
    return [
        VMEM((4, 1, 128, width), BF16),
        VMEM((4, 3, 128, width), BF16),
        VMEM((4, 128, width), BF16),
        VMEM((1, 128, width), BF16),
        VMEM((3, 128, width), BF16),
    ]


def body(
    hidden_in,
    norm1_gain,
    query_weight,
    key_weight,
    value_weight,
    out_weight,
    norm2_gain,
    gate_weight,
    up_weight,
    down_weight,
    cotangent,
    source_id,
    source_counts,
):
    rows, toks, width = hidden_in.shape
    depth, ff = gate_weight.shape
    length, held = 8 * toks, 8 * depth
    mlp_w = 3 * PAD_FF
    scale = row_scale(source_id, source_counts).reshape(1, 1)
    (
        att,
        weights,
        raw_all,
        low,
        qs,
        ks,
        values,
        attended,
        shares,
        inverses,
        gains,
        raw,
        top,
        middle,
        normed2,
    ) = call(
        forward_kernel,
        0,
        [
            (array, VMEM)
            for array in (
                hidden_in.reshape(toks, width),
                cotangent.reshape(toks, width),
                scale,
                lane_order(False),
                query_weight,
                key_weight,
                value_weight,
                out_weight,
                gate_weight,
                up_weight,
                down_weight,
                jnp.stack((norm1_gain, norm2_gain), axis=1),
            )
        ],
        [
            ((width, ATT_W), BF16, HBM),
            ((width, mlp_w), BF16, HBM),
            ((length, width), BF16, HBM),
            ((length, width), BF16, HBM),
            ((length, 128), BF16, VMEM),
            ((length, 128), BF16, VMEM),
            ((length, 256), BF16, VMEM),
            ((length, 256), BF16, VMEM),
            ((length, 256), F32, VMEM),
            ((length, 128), F32, VMEM),
            ((8, width), F32, VMEM),
            ((toks, width), BF16, VMEM),
            ((toks, width), BF16, VMEM),
            ((toks, width), F32, VMEM),
            ((length, width), BF16, HBM),
        ],
        [
            VMEM((8, depth, ATT_W), BF16),
            VMEM((8, depth, mlp_w), BF16),
            VMEM((toks, width), BF16),
            VMEM((toks, width), BF16),
            VMEM((held, ATT_W), BF16),
            VMEM((held, mlp_w), BF16),
            VMEM((length, width), BF16),
            VMEM((width, ATT_W), BF16),
            VMEM((width, 384), BF16),
        ]
        + ring_scratch(width)
        + [VMEM((toks, width), BF16)],
        240,
        4 * 10**9,
    )
    grad_middle, grad_gain2, middle_low, grads, gate_sum, layer_parts = call(
        mlp_kernel,
        1,
        [
            (normed2, HBM),
            (low, HBM),
            (weights, HBM),
            (middle, VMEM),
            (top, VMEM),
            (gains, VMEM),
        ],
        [
            ((toks, width), F32, VMEM),
            ((8, width), F32, VMEM),
            ((length, width), BF16, HBM),
            ((width, 2 * PAD_FF), BF16, HBM),
            ((held, PAD_FF), BF16, VMEM),
            ((4, toks, width), BF16, HBM),
        ],
        [
            VMEM((length, width), BF16),
            VMEM((length, width), BF16),
            VMEM((width, mlp_w), BF16),
            VMEM((length, PAD_FF), BF16),
            VMEM((length, PAD_FF), BF16),
            VMEM((length, PAD_FF), BF16),
        ]
        + ring_scratch(width)
        + [
            VMEM((4, toks, width), BF16),
            VMEM((4, toks, width), BF16),
            VMEM((4, toks, width), BF16),
            VMEM((toks, width), BF16),
        ]
        + plane_scratch(PAD_FF),
        150,
        30 * 10**9,
    )
    late_back, early_back, gate_back, last, layer, gain_sums = call(
        back_kernel,
        2,
        [
            (middle_low, HBM),
            (raw_all, HBM),
            (att, VMEM),
            (qs, VMEM),
            (ks, VMEM),
            (values, VMEM),
            (attended, VMEM),
            (shares, VMEM),
            (inverses, VMEM),
            (raw, VMEM),
            (grad_middle, VMEM),
            (middle, VMEM),
            (gains, VMEM),
            (grad_gain2, VMEM),
            (grads, HBM),
            (layer_parts, HBM),
            (gate_sum, VMEM),
        ],
        [
            ((8, depth, LATE_W), BF16, HBM),
            ((8, depth, EARLY_W), BF16, HBM),
            ((8, depth, PAD_FF), BF16, HBM),
            ((toks, width), BF16, HBM),
            ((toks, width), BF16, HBM),
            ((8, 128), F32, VMEM),
        ],
        [
            VMEM((length, width), BF16),
            VMEM((width, EARLY_W), BF16),
            VMEM((width, LATE_W), BF16),
            VMEM((4, toks, width), BF16),
            VMEM((length, 256), BF16),
            VMEM((length, 256), F32),
            VMEM((length, 128), F32),
            VMEM((length, 128), F32),
            VMEM((length, 256), F32),
            VMEM((length, 128), BF16),
            VMEM((length, 256), BF16),
            VMEM((length, 128), BF16),
            VMEM((length, 256), BF16),
        ]
        + ring_scratch(width)
        + [VMEM((1, toks, width), BF16), VMEM((3, toks, width), BF16)]
        + plane_scratch(EARLY_W)
        + plane_scratch(LATE_W)
        + [
            VMEM((held, EARLY_W), BF16),
            VMEM((held, LATE_W), BF16),
            VMEM((toks, width), BF16),
            VMEM((toks, width), BF16),
            VMEM((8, width), F32),
            VMEM((16, 8, 128), F32),
            VMEM((8, 128), F32),
            VMEM((8, 8, 128), F32),
        ],
        240,
        8 * 10**9,
    )
    grads_out = call(
        unpack_kernel,
        None,
        [(array, VMEM) for array in (late_back, early_back, gate_back, layer, last, lane_order(True))],
        [
            ((depth, query_weight.shape[1]), F32, VMEM),
            ((depth, key_weight.shape[1]), F32, VMEM),
            ((depth, value_weight.shape[1]), F32, VMEM),
            ((depth, out_weight.shape[1]), F32, VMEM),
            ((depth, ff), F32, VMEM),
            ((depth, ff), F32, VMEM),
            ((depth, ff), F32, VMEM),
            ((toks, width), BF16, VMEM),
            ((toks, width), F32, VMEM),
        ],
        [],
        0,
        0,
    )
    grad_query, grad_key, grad_value, grad_out, grad_gate, grad_up, grad_down = grads_out[:7]
    at = (lax.axis_index("core") * 4 + lax.axis_index("y")) * depth
    pair = lax.dynamic_slice(gain_sums, (0, at), (8, depth))
    return (
        grads_out[7].reshape(rows, toks, width),
        grads_out[8].reshape(rows, toks, width),
        pair[0],
        grad_query,
        grad_key,
        grad_value,
        grad_out,
        pair[1],
        grad_gate,
        grad_up,
        grad_down,
    )


def solution(mesh):
    zlo, chips_x, cores, chips_y, zhi = 2, 4, 2, 4, 2
    whole = Mesh(mesh.devices.reshape(zlo, chips_x, cores, chips_y, zhi), AXES)
    weight = P(AXES, None)
    gain = P(AXES)
    tokens = P(DP, SEQ, None)
    return jax.shard_map(
        body,
        mesh=whole,
        in_specs=(
            tokens,
            gain,
            weight,
            weight,
            weight,
            weight,
            gain,
            weight,
            weight,
            weight,
            tokens,
            P(DP),
            P(),
        ),
        out_specs=(
            tokens,
            tokens,
            gain,
            weight,
            weight,
            weight,
            weight,
            gain,
            weight,
            weight,
            weight,
        ),
        check_vma=False,
    )
```

```python
import jax
import jax.numpy as jnp
import numpy as np
from jax import lax
from jax.experimental import pallas as pl
from jax.experimental.pallas import tpu as pltpu
from jax.sharding import Mesh, PartitionSpec as P

FEAT = 16
HEAD_V = 128
PAD_FF = 768
ATT_W = 640
QK_AT = slice(512, 640)
OUT_AT = slice(256, 512)
VALUE_AT = slice(0, 256)
EARLY_W = PAD_FF + 256
LATE_W = 384

norm_eps = 1e-05
AXES = ("zlo", "x", "core", "y", "zhi")
DP = ("zlo", "x", "core")
SEQ = ("y", "zhi")

MESH = pl.DeviceIdType.MESH
VMEM_LIMIT = 61 * 2**20
PIECES = 4
PLANE_PIECES = 2
TILE = 256
STEP = 16
BF16, F32 = jnp.bfloat16, jnp.float32


def row_scale(source_id, source_counts):
    picked = jnp.sum(
        jnp.where(
            source_id[:, None] == jnp.arange(source_counts.shape[0], dtype=jnp.int32)[None, :],
            source_counts[None, :],
            0,
        ),
        axis=1,
    )
    return 4.0 / jnp.sqrt(picked.astype(F32))


def lane_order(back):
    at = np.arange(256)
    to = (at // 16 % 2) * 128 + (at // 32) * 16 + at % 16
    hot = np.zeros((256, 256), np.float32)
    hot[at, to] = 1.0
    return jnp.asarray(hot.T if back else hot, BF16)


def place():
    z = lax.axis_index("zhi") * 2 + lax.axis_index("zlo")
    return lax.axis_index("x"), lax.axis_index("y"), z, lax.axis_index("core")


def around(index):
    return lax.rem(index + 8, 4)


def at_y(y):
    return {"y": around(y)}


def at_core(core):
    return {"core": core}


def at_xz(x, z):
    x, z = around(x), around(z)
    return {"x": x, "zhi": z // 2, "zlo": lax.rem(z, 2)}


def ring_peers(y, core):
    return [at_y(y + 1), at_y(y - 1), at_core(1 - core)]


def plane_peers(x, z):
    return [at_xz(x + 1, z), at_xz(x - 1, z), at_xz(x, z + 1), at_xz(x, z - 1)]


def group_peers(y, core):
    return [
        (lax.rem(core + dc, 2), lax.rem(y + dy, 4))
        for dc in (0, 1)
        for dy in range(4)
        if (dc, dy) != (0, 0)
    ]


def hello(devices, partner=None, swaps=None):
    barrier = pltpu.get_barrier_semaphore()
    for device in devices:
        pl.semaphore_signal(barrier, inc=1, device_id=device, device_id_type=MESH)
    count = len(devices)
    if partner is not None:

        @pl.when(swaps)
        def _():
            pl.semaphore_signal(barrier, inc=1, device_id=partner, device_id_type=MESH)

        count = count + jnp.where(swaps, 1, 0)

    def wait():
        pl.semaphore_wait(barrier, count)

    return wait


class Copies:
    def __init__(self, send, recv):
        self.send, self.recv, self.used, self.open = send, recv, 0, []

    def start(self, src, dst, device):
        copy = pltpu.make_async_remote_copy(
            src_ref=src,
            dst_ref=dst,
            send_sem=self.send.at[self.used],
            recv_sem=self.recv.at[self.used],
            device_id=device,
            device_id_type=MESH,
        )
        copy.start()
        self.used += 1
        self.open.append(copy)
        return copy

    def local(self, src, dst):
        copy = pltpu.make_async_copy(src, dst, self.send.at[self.used])
        copy.start()
        self.used += 1
        return copy

    def swap(self, src, dst, partner, swaps):
        at = self.used
        self.used += 1

        def over():
            return pltpu.make_async_remote_copy(
                src_ref=src,
                dst_ref=dst,
                send_sem=self.send.at[at],
                recv_sem=self.recv.at[at],
                device_id=partner,
                device_id_type=MESH,
            )

        def stay():
            return pltpu.make_async_copy(src, dst, self.send.at[at])

        @pl.when(swaps)
        def _():
            over().start()

        @pl.when(jnp.logical_not(swaps))
        def _():
            stay().start()

        def wait():
            @pl.when(swaps)
            def _():
                over().wait()

            @pl.when(jnp.logical_not(swaps))
            def _():
                stay().wait()

        return wait

    def finish(self):
        for copy in self.open:
            copy.wait_send()


def way(piece):
    return 1 if piece % 2 == 0 else -1


def slab(ref, block, rows, piece=None, pieces=PIECES):
    if piece is None:
        return ref.at[pl.ds(pl.multiple_of(block * rows, 128), rows)]
    size = rows // pieces
    return ref.at[pl.ds(pl.multiple_of(block * rows + piece * size, 32), size)]


def row_steps(start, size, act, step=STEP):
    @pl.loop(0, size // step, unroll=min(4, size // step))
    def _(at):
        act(pl.ds(pl.multiple_of(start + at * step, step), step))


class GatherRing:
    def __init__(self, copies, to, mine, full, block_of, me, rows, pieces=PIECES):
        self.copies, self.to, self.full, self.block_of = copies, to, full, block_of
        self.me, self.rows, self.sent, self.onward = me, rows, {}, {}
        self.pieces = pieces
        size = rows // pieces
        for piece in range(pieces):
            for step in (way(piece), -way(piece)):
                self.sent[step, piece] = copies.start(
                    mine.at[pl.ds(piece * size, size)],
                    slab(full, block_of(me), rows, piece, pieces),
                    to(me + step),
                )

    def forward(self):
        for piece in range(self.pieces):
            step = way(piece)
            self.sent[step, piece].wait_recv()
            here = slab(self.full, self.block_of(self.me - step), self.rows, piece, self.pieces)
            self.onward[piece] = self.copies.start(here, here, self.to(self.me + step))

    def near(self):
        for piece in range(self.pieces):
            self.sent[-way(piece), piece].wait_recv()

    def far(self):
        for piece in range(self.pieces):
            self.onward[piece].wait_recv()


class GatherTokens:
    def __init__(self, copies, mine, full, y, core):
        self.copies, self.full, self.y, self.core = copies, full, y, core
        self.rows = mine.shape[0]
        self.shared = {}
        self.own = copies.local(mine, slab(full, self.block_of(y), self.rows))
        self.shared[0] = copies.start(mine, slab(full, self.block_of(y), self.rows), at_core(1 - core))
        self.ring = GatherRing(copies, at_y, mine, full, self.block_of, y, self.rows)

    def block_of(self, index):
        return around(index) * 2 + self.core

    def share(self, k):
        here = slab(self.full, self.block_of(self.y + k), self.rows)
        self.shared[k] = self.copies.start(here, here, at_core(1 - self.core))

    def forward(self):
        self.ring.forward()

    def near(self):
        self.ring.near()
        self.share(1)
        self.share(-1)

    def far(self):
        self.ring.far()
        self.share(2)

    def finish(self):
        self.own.wait()
        for copy in self.shared.values():
            copy.wait_recv()


class GatherPlane:
    def __init__(self, copies, mine, full, x, z, core):
        self.copies, self.full = copies, full
        rows = mine.shape[0]

        def block(a, b):
            a, b = around(a), around(b)
            return jnp.where(core == 0, 4 * b + a, 4 * a + b)

        first, second = jnp.where(core == 0, x, z), jnp.where(core == 0, z, x)

        def to_first(index):
            return at_xz(jnp.where(core == 0, index, x), jnp.where(core == 0, z, index))

        def to_second(index):
            return at_xz(jnp.where(core == 0, x, index), jnp.where(core == 0, index, z))

        def onto(k, source=None):
            a = first + k
            if source is None:
                source = slab(full, block(a, second), rows)
            return GatherRing(
                copies, to_second, source, full, lambda b: block(a, b), second, rows, PLANE_PIECES
            )

        self.onto = onto
        self.own = copies.local(mine, slab(full, block(first, second), rows))
        self.ring = GatherRing(
            copies, to_first, mine, full, lambda a: block(a, second), first, rows, PLANE_PIECES
        )
        self.rings = {0: onto(0, mine)}

    def stages(self):
        def one():
            self.ring.forward()

        def two():
            self.ring.near()
            self.rings[1] = self.onto(1)
            self.rings[-1] = self.onto(-1)

        def three():
            self.rings[0].forward()

        def four():
            self.ring.far()
            self.rings[2] = self.onto(2)

        def five():
            self.rings[1].forward()
            self.rings[-1].forward()

        def six():
            self.rings[2].forward()
            self.rings[0].near()
            self.rings[0].far()

        def seven():
            for k in (1, -1, 2):
                self.rings[k].near()
                self.rings[k].far()
            self.own.wait()

        return [one, two, three, four, five, six, seven]


class ReduceRing:
    def __init__(self, copies, to, me, read, out, got, rows, source=None, pieces=PIECES):
        self.copies, self.to, self.me, self.read = copies, to, me, read
        self.out, self.got, self.rows, self.source, self.sent = out, got, rows, source, {}
        self.pieces = pieces
        self.size = rows // pieces

    def span(self, piece):
        return pl.ds(piece * self.size, self.size)

    def push(self, slot, k, piece, device):
        span = self.span(piece)
        if self.source is not None:
            ref = self.source(k, span)
        else:

            def fill(rows):
                self.out[slot, rows] = self.read(k, rows).astype(BF16)

            row_steps(piece * self.size, self.size, fill)
            ref = self.out.at[slot, span]
        self.sent[slot, piece] = self.copies.start(ref, self.got.at[slot, span], device)

    def far(self):
        for piece in range(self.pieces):
            self.push(0, 2, piece, self.to(self.me + way(piece)))

    def direct(self, k):
        for piece in range(self.pieces):
            if way(piece) == -k:
                self.push(1, k, piece, self.to(self.me + k))

    def onward(self, k):
        slot = 2 if self.source is None else 0
        for piece in range(self.pieces):
            if way(piece) == k:
                self.sent[0, piece].wait_recv()

                def fill(rows):
                    self.out[slot, rows] = (
                        self.read(k, rows) + self.got[0, rows].astype(F32)
                    ).astype(BF16)

                row_steps(piece * self.size, self.size, fill)
                span = self.span(piece)
                self.sent[2, piece] = self.copies.start(
                    self.out.at[slot, span], self.got.at[2, span], self.to(self.me + k)
                )

    def arrive(self, piece):
        self.sent[1, piece].wait_recv()
        self.sent[2, piece].wait_recv()

    def each(self, act):
        for piece in range(self.pieces):
            self.arrive(piece)

            def take(rows):
                act(rows, self.total(rows))

            row_steps(piece * self.size, self.size, take)

    def total(self, rows):
        return self.read(0, rows) + self.got[1, rows].astype(F32) + self.got[2, rows].astype(F32)


class ReduceTokens:
    def __init__(self, copies, make, y, core, own, sib, got_sib, out, got):
        self.copies, self.make, self.y, self.core = copies, make, y, core
        self.own, self.sib, self.got_sib, self.shared = own, sib, got_sib, {}
        self.ring = ReduceRing(copies, at_y, y, self.read, out, got, own.shape[1])

    def read(self, k, rows):
        return self.own[k % 4, rows] + self.got_sib[k % 4, rows].astype(F32)

    def share(self, k):
        self.shared[k] = self.copies.start(
            self.sib.at[k % 4], self.got_sib.at[k % 4], at_core(1 - self.core)
        )

    def part(self, k):
        self.make(k, self.own.at[k % 4], self.sib.at[k % 4])
        self.share(k)

    def one(self):
        self.shared[2].wait_recv()
        self.ring.far()
        self.shared[1].wait_recv()
        self.ring.direct(1)

    def two(self):
        self.shared[-1].wait_recv()
        self.ring.direct(-1)
        self.ring.onward(1)
        self.ring.onward(-1)
        self.shared[0].wait_recv()

    def each(self, act):
        for piece in range(PIECES):
            self.ring.arrive(piece)

            def take(rows):
                act(rows, self.ring.total(rows))

            row_steps(piece * self.ring.size, self.ring.size, take)


def second_ring(copies, mid, x, z, core, out2, got2):
    last = jnp.where(core == 0, x, z)

    def to_last(index):
        return at_xz(jnp.where(core == 0, index, x), jnp.where(core == 0, z, index))

    def read(step, span):
        return mid[step % 4, span].astype(F32)

    def source(step, span):
        return mid.at[step % 4, span]

    rows = mid.shape[1]
    return ReduceRing(copies, to_last, last, read, out2, got2, rows, source, PLANE_PIECES)


class ReducePlane:
    def __init__(self, copies, parts, lanes, x, z, core, out1, got1, mid, out2, got2, sent=None):
        rows = mid.shape[1]
        sent = parts if sent is None else sent

        def block(a, b):
            a, b = around(a), around(b)
            return jnp.where(core == 0, 4 * b + a, 4 * a + b)

        last, first = jnp.where(core == 0, x, z), jnp.where(core == 0, z, x)

        def to_first(index):
            return at_xz(jnp.where(core == 0, x, index), jnp.where(core == 0, index, z))

        def ring(k):
            def place_of(step, span):
                start = block(last + k, first + step) * rows + span.start
                return pl.ds(pl.multiple_of(start, STEP), span.size)

            def read(step, span):
                return parts[place_of(step, span), lanes].astype(F32)

            def source(step, span):
                return sent.at[place_of(step, span), lanes]

            return ReduceRing(
                copies,
                to_first,
                first,
                read,
                out1.at[k % 4],
                got1.at[k % 4],
                rows,
                source,
                PLANE_PIECES,
            )

        self.mid = mid
        self.rings = {k: ring(k) for k in (2, 1, -1, 0)}

        if got2 is not None:
            self.ring = second_ring(copies, mid, x, z, core, out2, got2)

    def start(self):
        for ring in self.rings.values():
            ring.far()

    def direct(self):
        for ring in self.rings.values():
            ring.direct(1)
            ring.direct(-1)

    def onward(self, k):
        self.rings[k].onward(1)
        self.rings[k].onward(-1)

    def middle(self, k):
        ring = self.rings[k]
        for piece in range(PLANE_PIECES):
            ring.arrive(piece)

            def fill(rows):
                self.mid[k % 4, rows] = ring.total(rows).astype(BF16)

            row_steps(piece * ring.size, ring.size, fill)

    def stages(self):
        def ends(k, then):
            def act():
                self.middle(k)
                then()

            return act

        return (
            [self.start, self.direct]
            + [lambda k=k: self.onward(k) for k in (2, 1, -1, 0)]
            + [
                ends(2, self.ring.far),
                ends(1, lambda: self.ring.direct(1)),
                ends(-1, lambda: self.ring.direct(-1)),
                ends(0, lambda: None),
                lambda: (self.ring.onward(1), self.ring.onward(-1)),
            ]
        )

    def first_stages(self):
        return (
            [self.start, self.direct]
            + [lambda k=k: self.onward(k) for k in (2, 1, -1, 0)]
            + [lambda k=k: self.middle(k) for k in (2, 1, -1, 0)]
        )

    def each(self, act):
        self.ring.each(act)


def nt(left, right):
    return lax.dot_general(left, right, (((1,), (1,)), ((), ())), preferred_element_type=F32)


def tn(left, right):
    return lax.dot_general(left, right, (((0,), (0,)), ((), ())), preferred_element_type=F32)


def nn(left, right):
    return jnp.dot(left, right, preferred_element_type=F32)


def chip_rows(block):
    return pl.ds(pl.multiple_of(block * 256, 256), 256)


def part_maker(pairs, y, core):
    def make(k, mine, theirs):
        rows = chip_rows(around(y + k))

        @pl.loop(0, mine.shape[-1] // TILE)
        def _(tile):
            columns = pl.ds(pl.multiple_of(tile * TILE, TILE), TILE)
            total = None
            for left, right, lanes in pairs:
                term = nt(left[rows, :], right[columns, lanes])
                total = term if total is None else total + term
            low, high = total[:128], total[128:]
            mine[:, columns] = jnp.where(core == 0, low, high)
            theirs[:, columns] = jnp.where(core == 0, high, low).astype(BF16)

    return make


def inverse_of(value):
    return lax.rsqrt(jnp.mean(value * value, axis=-1, keepdims=True) + norm_eps)


def norm_back_rows(grad, value, gain):
    inverse = inverse_of(value)
    unit = value * inverse
    scaled = grad * gain
    moved = inverse * (scaled - unit * jnp.mean(scaled * unit, axis=-1, keepdims=True))
    return moved, grad * unit


def reorder_into(target, source, hot):
    runs = source.shape[1] // 256
    for run in range(runs):
        moved = nn(source[:, run * 256 : (run + 1) * 256], hot[...]).astype(BF16)
        target[:, run * 128 : (run + 1) * 128] = moved[:, :128]
        target[:, (runs + run) * 128 : (runs + run + 1) * 128] = moved[:, 128:]


def gain_rows(att):
    row = lax.broadcasted_iota(jnp.int32, (8, 128), 0)
    lane = lax.broadcasted_iota(jnp.int32, (8, 128), 1)
    pick = jnp.where((lane == row + 64) & (row < 2), 1.0, 0.0).astype(BF16)
    return nt(pick, att[:, QK_AT])


def head_lanes(head):
    lane = lax.broadcasted_iota(jnp.int32, (1, 128), 1)
    return (lane >= head * FEAT) & (lane < (head + 1) * FEAT)


def scores_of(q, k, block, extent):
    x = nt(q, k) * 0.25
    row = lax.broadcasted_iota(jnp.int32, (256, extent), 0) + block * 256
    keep = row >= lax.broadcasted_iota(jnp.int32, (256, extent), 1)
    return x, jnp.where(keep, 1.0 + x + 0.5 * (x * x), 0.0), keep


def forward_kernel(
    hidden,
    cotangent,
    scale,
    hot,
    query,
    key,
    value,
    out_weight,
    gate,
    up,
    down,
    gain_pair,
    att_out,
    weights,
    raw_out,
    low_out,
    qs_out,
    ks_out,
    values_out,
    attended_out,
    shares_out,
    inverses_out,
    gains,
    raw,
    top,
    middle,
    normed2,
    att_cut,
    mlp_cut,
    raw_cut,
    top_cut,
    att_own,
    mlp_own,
    raw_all,
    att_all,
    att_scaled,
    own,
    sib,
    got_sib,
    out,
    got,
    low,
    qs,
    ks,
    values,
    attended,
    shares,
    inverses,
    send,
    recv,
):
    x, y, z, core = place()
    zhi = z // 2
    partner = {"core": 1 - core, "zhi": 1 - zhi}
    swaps = core != zhi
    peers = group_peers(y, core)
    ready = hello(
        [{"core": c, "y": d} for c, d in peers] + plane_peers(x, z), partner, swaps
    )
    copies = Copies(send, recv)
    me = core * 4 + y
    depth, here = gate.shape[0], gate.shape[1] // 8

    def spread(cuts, target):
        rows = pl.ds(pl.multiple_of(me * depth, depth), depth)
        kept = copies.local(cuts.at[me], target.at[rows])
        got = [
            copies.start(cuts.at[c * 4 + d], target.at[rows], {"core": c, "y": d}) for c, d in peers
        ]

        def wait():
            kept.wait()
            for copy in got:
                copy.wait_recv()

        return wait

    reorder_into(raw_cut, hidden, hot)
    gap = jnp.zeros((depth, 62), BF16)
    for block in range(8):
        att_cut[block, :, VALUE_AT] = value[:, block * 256 : (block + 1) * 256]
        att_cut[block, :, OUT_AT] = out_weight[:, block * 256 : (block + 1) * 256]
        att_cut[block, :, QK_AT] = jnp.concatenate(
            (
                query[:, block * 32 : (block + 1) * 32],
                key[:, block * 32 : (block + 1) * 32],
                gain_pair[...],
                gap,
            ),
            axis=1,
        )
    ready()
    wait_raw = copies.swap(raw_cut, raw, partner, swaps)
    wait_att = spread(att_cut, att_own)
    gap = jnp.zeros((depth, PAD_FF - here), BF16)
    for block in range(8):
        for at, weight in enumerate((gate, up, down)):
            cut = weight[:, block * here : (block + 1) * here]
            mlp_cut[block, :, at * PAD_FF : (at + 1) * PAD_FF] = jnp.concatenate((cut, gap), axis=1)
    wait_raw()
    tokens = GatherTokens(copies, raw, raw_all, y, core)
    wait_mlp = spread(mlp_cut, mlp_own)

    def weigh(rows):
        top_cut[rows] = (cotangent[rows].astype(F32) * scale[...]).astype(BF16)

    row_steps(0, top_cut.shape[0], weigh)
    reorder_into(top_cut, top_cut[...], hot)
    wait_att()
    plane = GatherPlane(copies, att_own, att_all, x, z, core)
    wait_top = copies.swap(top_cut, top, partner, swaps)

    def invert(block):
        def act(rows):
            inverse = inverse_of(raw_all[rows].astype(F32))
            inverses[rows] = jnp.broadcast_to(inverse, (STEP, 128))

        row_steps(block * 128, 128, act)

    one, two, three, four, five, six, seven = plane.stages()
    one()
    two()
    tokens.forward()
    three()
    four()
    tokens.shared[0].wait_recv()
    tokens.own.wait()
    invert(2 * y)
    invert(2 * y + 1)
    five()
    six()
    wait_mlp()
    mlp_plane = GatherPlane(copies, mlp_own, weights, x, z, core)
    mlp_stages = iter(mlp_plane.stages())
    tokens.near()
    invert(2 * around(y + 1) + core)
    invert(2 * around(y - 1) + core)
    tokens.far()
    wait_top()
    tops = GatherTokens(copies, top, low_out, y, core)
    invert(2 * around(y + 2) + core)
    seven()
    gains[...] = gain_rows(att_all)

    def scale_rows(rows):
        gain = att_all[rows, 576:577].astype(F32)
        att_scaled[rows, 0:256] = (att_all[rows, VALUE_AT].astype(F32) * gain).astype(BF16)
        att_scaled[rows, 256:384] = (att_all[rows, QK_AT].astype(F32) * gain).astype(BF16)

    row_steps(0, att_all.shape[0], scale_rows, 128)
    tokens.shared[1].wait_recv()
    tokens.shared[-1].wait_recv()
    invert(2 * around(y + 1) + 1 - core)
    invert(2 * around(y - 1) + 1 - core)
    tokens.shared[2].wait_recv()
    invert(2 * around(y + 2) + 1 - core)
    kept = [copies.local(att_all, att_out), copies.local(raw_all, raw_out)]

    def stores():
        pairs = (
            (qs, qs_out),
            (ks, ks_out),
            (values, values_out),
            (attended, attended_out),
            (shares, shares_out),
            (inverses, inverses_out),
        )
        for source, target in pairs:
            kept.append(copies.local(source, target))


    @pl.loop(0, 2, unroll=True)
    def _(half):
        rows = pl.ds(pl.multiple_of(half * 512, 512), 512)
        inverse = inverses[rows]
        block = raw_all[rows]
        both = nn(block, att_scaled[:, 0:256])
        values[rows] = (both * jnp.concatenate((inverse, inverse), axis=1)).astype(BF16)
        both = nn(block, att_scaled[:, 256:384]) * inverse
        lane = lax.broadcasted_iota(jnp.int32, (1, 128), 1)
        qs[rows] = jnp.where(lane < 32, both, 0.0).astype(BF16)
        ks[rows] = jnp.where(lane < 32, pltpu.roll(both, 96, 1), 0.0).astype(BF16)

    for head in range(2):
        lanes = slice(head * HEAD_V, (head + 1) * HEAD_V)
        for block in range(4):
            rows, extent = slice(block * 256, (block + 1) * 256), (block + 1) * 256
            q = jnp.where(head_lanes(head), qs[rows], 0)
            unused, scores, unused_keep = scores_of(q, ks[0:extent], block, extent)
            share = 1.0 / jnp.sum(scores, axis=-1, keepdims=True)
            numer = nn(scores.astype(BF16), values[0:extent, lanes])
            attended[rows, lanes] = (numer * share).astype(BF16)
            shares[rows, lanes] = jnp.broadcast_to(share, (256, HEAD_V))
        if head == 0:
            tops.forward()
    stores()
    for _ in range(3):
        next(mlp_stages)()
    sums = ReduceTokens(
        copies, part_maker([(attended, att_all, OUT_AT)], y, core), y, core, own, sib, got_sib, out, got
    )
    for k in (2, 1, -1):
        sums.part(k)
    sums.one()
    sums.part(0)
    next(mlp_stages)()
    sums.two()
    next(mlp_stages)()
    tops.near()

    def norm2(rows, total):
        value = raw[rows].astype(F32) + total
        middle[rows] = value
        low[rows] = (value * inverse_of(value) * gains[1:2]).astype(BF16)

    sums.each(norm2)
    back = GatherTokens(copies, low, normed2, y, core)
    next(mlp_stages)()
    tops.far()
    back.forward()
    back.near()
    back.far()
    next(mlp_stages)()
    tops.finish()
    back.finish()
    for copy in kept:
        copy.wait()
    copies.finish()


def mlp_kernel(
    normed2_in,
    low_in,
    weights_in,
    middle,
    top,
    gains,
    grad_middle,
    grad_gain,
    middle_low,
    grads,
    gate_sum,
    up_mid,
    layer_parts,
    normed2,
    grad_low,
    weights,
    hidden,
    gate_act,
    up_act,
    own,
    sib,
    got_sib,
    out,
    got,
    sib2,
    got_sib2,
    layer,
    low,
    plane_out1,
    plane_got1,
    plane_mid,
    plane_out2,
    plane_got2,
    up_out1,
    up_got1,
    send,
    recv,
    loads=(),
):
    x, y, z, core = place()
    copies = Copies(send, recv)
    ready = hello(ring_peers(y, core) + plane_peers(x, z))
    order = (2, 1, -1, 0)
    operands, loads = loads, {}

    def load(k):
        slot = order.index(k)
        for at, owner in enumerate((core, 1 - core)):
            block = around(y + k) * 2 + owner
            rows = pl.ds(slot * 256 + at * 128, 128)
            for source, target in ((normed2_in, normed2), (low_in, grad_low)):
                loads.setdefault(k, []).append(copies.local(slab(source, block, 128), target.at[rows]))

    def lanes(at):
        return slice(at * PAD_FF, (at + 1) * PAD_FF)

    def load_tile(tile):
        cuts = [slice(at * PAD_FF + tile * TILE, at * PAD_FF + (tile + 1) * TILE) for at in range(3)]
        loads["w", tile] = [copies.local(weights_in.at[:, cut], weights.at[:, cut]) for cut in cuts]

    load(2)
    load(1)
    load_tile(0)
    ready()
    for copy in operands:
        copy.wait()

    def act_tile(half, tile):
        rows = slice(half * 512, (half + 1) * 512)
        here = slice(tile * TILE, (tile + 1) * TILE)

        def cut(at):
            return weights[:, at * PAD_FF + tile * TILE : at * PAD_FF + (tile + 1) * TILE]

        block = normed2[rows]
        gate = nn(block, cut(0))
        upward = nn(block, cut(1))
        grad_hidden = nn(grad_low[rows], cut(2))
        sigma = jax.nn.sigmoid(gate)
        silu = gate * sigma
        hidden[rows, here] = (silu * upward).astype(BF16)
        slope = sigma + silu * (1.0 - sigma)
        gate_act[rows, here] = (grad_hidden * upward * slope).astype(BF16)
        up_act[rows, here] = (grad_hidden * silu).astype(BF16)

    def part_pair(half, pairs, sib_ref):
        rows = slice(half * 512, (half + 1) * 512)

        @pl.loop(0, own.shape[-1] // 512)
        def _(tile):
            columns = pl.ds(pl.multiple_of(tile * 512, 512), 512)
            total = None
            for left, right in pairs:
                term = nt(left[rows, :], weights[columns, right])
                total = term if total is None else total + term
            for at in range(2):
                k = order[2 * half + at] % 4
                own[k, :, columns] = total[at * 256 : at * 256 + 128]
                sib_ref[k, :, columns] = total[at * 256 + 128 : at * 256 + 256].astype(BF16)

    def grad_block(at, left, right):
        @pl.loop(0, left.shape[1] // 512)
        def _(tile):
            columns = pl.ds(pl.multiple_of(tile * 512, 512), 512)
            weights[columns, lanes(at)] = tn(left[:, columns], right[...]).astype(BF16)

    sums = ReduceTokens(copies, None, y, core, own, sib, got_sib, out, got)
    acts = [(gate_act, lanes(0)), (up_act, lanes(1))]
    for copy in loads[2] + loads[1]:
        copy.wait()
    for tile in range(3):
        for copy in loads["w", tile]:
            copy.wait()
        if tile == 0:
            load_tile(1)
            load_tile(2)
            load(-1)
            load(0)
        act_tile(0, tile)
    part_pair(0, acts, sib)
    sums.share(2)
    sums.share(1)
    for copy in loads[-1] + loads[0]:
        copy.wait()
    act_tile(1, 0)
    sums.one()
    act_tile(1, 1)
    act_tile(1, 2)
    part_pair(1, acts, sib)
    sums.share(-1)
    sums.share(0)
    sums.two()
    grad_block(0, normed2, gate_act)
    plane = ReducePlane(
        copies, weights, lanes(0), x, z, core, plane_out1, plane_got1, plane_mid, plane_out2, plane_got2
    )
    stages = iter(plane.stages())
    next(stages)()
    grad_gain[...] = jnp.zeros_like(grad_gain)

    def back(rows, total):
        moved, terms = norm_back_rows(total, middle[rows], gains[1:2])
        grad_gain[...] += terms[:8] + terms[8:]
        value = top[rows].astype(F32) + moved
        grad_middle[rows] = value
        low[rows] = value.astype(BF16)

    sums.each(back)
    gather = GatherTokens(copies, low, middle_low, y, core)
    next(stages)()
    grad_block(1, normed2, up_act)
    up_plane = ReducePlane(
        copies, weights, lanes(1), x, z, core, up_out1, up_got1, up_mid, None, None
    )
    up_stages = iter(up_plane.first_stages())
    next(up_stages)()
    for _ in range(4):
        next(stages)()
    layers = ReduceTokens(copies, None, y, core, own, sib2, got_sib2, None, None)
    part_pair(0, [(hidden, lanes(2))], sib2)
    layers.share(2)
    layers.share(1)
    gather.forward()
    next(up_stages)()
    part_pair(1, [(hidden, lanes(2))], sib2)
    layers.share(-1)
    layers.share(0)
    for _ in range(4):
        next(up_stages)()
    for _ in range(4):
        next(stages)()
    gather.near()
    grad_block(2, grad_low, hidden)
    stored = [copies.local(weights.at[:, lanes(2)], grads)]
    gather.far()
    for stage in stages:
        stage()
    for stage in up_stages:
        stage()
    for k in order:
        layers.shared[k].wait_recv()

        def add(rows, k=k):
            layer[k % 4, rows] = layers.read(k, rows).astype(BF16)

        row_steps(0, 128, add)
    stored.append(copies.local(layer, layer_parts))

    def take(rows, total):
        gate_sum[rows] = total.astype(BF16)

    plane.each(take)
    gather.finish()
    for copy in stored:
        copy.wait()
    copies.finish()


def back_kernel(
    low_in,
    raw_in,
    att,
    qs,
    ks,
    values,
    attended,
    shares,
    inverses,
    raw,
    grad_middle,
    middle,
    gains,
    grad_gain2,
    grads_in,
    layer_in,
    gate_sum,
    up_mid,
    late_out,
    early_out,
    gate_out,
    up_out,
    grad_in,
    layer_out,
    gain_out,
    tokens,
    early,
    late,
    layer_parts,
    grad_numer,
    grad_denom,
    grad_q,
    grad_k,
    grad_v,
    grad_qk,
    grad_values,
    scaled_qk,
    scaled_values,
    own,
    sib,
    got_sib,
    out,
    got,
    layer_sent,
    layer_got,
    early_out1,
    early_got1,
    early_mid,
    early_out2,
    early_got2,
    late_out1,
    late_got1,
    late_mid,
    late_out2,
    late_got2,
    up_out2,
    up_got2,
    up_sum,
    early_sum,
    late_sum,
    last,
    layer,
    gain_part,
    gain_got,
    gain_sum,
    gain_back,
    send,
    recv,
    loads=(),
):
    x, y, z, core = place()
    zhi = z // 2
    partner = {"core": 1 - core, "zhi": 1 - zhi}
    swaps = core != zhi
    copies = Copies(send, recv)
    peers = group_peers(y, core)
    planes = [
        (lax.rem(x + dx, 4), lax.rem(z + dz, 4))
        for dx in range(4)
        for dz in range(4)
        if (dx, dz) != (0, 0)
    ]
    ready = hello(
        [{"core": c, "y": d} for c, d in peers] + [at_xz(a, b) for a, b in planes], partner, swaps
    )
    load_low = copies.local(low_in, tokens)
    load_early = copies.local(grads_in, early.at[:, 0:PAD_FF])
    load_layer = copies.local(layer_in, layer_parts)
    ready()
    for copy in loads:
        copy.wait()
    layers = ReduceRing(
        copies,
        at_y,
        y,
        lambda k, rows: layer_parts[k % 4, rows].astype(F32),
        layer_sent,
        layer_got,
        128,
        lambda k, span: layer_in.at[k % 4, span],
    )
    layers.far()
    layers.direct(1)
    layers.direct(-1)
    ups = second_ring(copies, up_mid, x, z, core, up_out2, up_got2)
    ups.far()
    ups.direct(1)
    ups.direct(-1)
    load_low.wait()

    @pl.loop(0, tokens.shape[1] // 512)
    def _(tile):
        columns = pl.ds(pl.multiple_of(tile * 512, 512), 512)
        early[columns, PAD_FF:EARLY_W] = tn(tokens[:, columns], attended[...]).astype(BF16)

    load_early.wait()
    early_plane = ReducePlane(
        copies,
        early,
        slice(0, EARLY_W),
        x,
        z,
        core,
        early_out1,
        early_got1,
        early_mid,
        early_out2,
        early_got2,
    )
    early_stages = iter(early_plane.stages())
    next(early_stages)()
    me = core * 4 + y
    back_copies, local = [], []

    def send_back(sums_ref, out_ref):
        def cut(index):
            return sums_ref.at[pl.ds(pl.multiple_of(index * 16, 16), 16)]

        local.append(copies.local(cut(me), out_ref.at[me]))
        for c, d in peers:
            back_copies.append(copies.start(cut(c * 4 + d), out_ref.at[me], {"core": c, "y": d}))

    send_back(gate_sum, gate_out)

    @pl.loop(0, 2, unroll=True)
    def _(half):
        rows = pl.ds(pl.multiple_of(half * 512, 512), 512)
        grad_mixed = nn(tokens[rows], att[:, OUT_AT]).astype(BF16).astype(F32)
        numer = grad_mixed * shares[rows]
        grad_numer[rows] = numer.astype(BF16)
        product = numer * attended[rows].astype(F32)
        for head in range(2):
            lanes = slice(head * HEAD_V, (head + 1) * HEAD_V)
            total = -jnp.sum(product[:, lanes], axis=-1, keepdims=True)
            grad_denom[rows, lanes] = jnp.broadcast_to(total, (512, HEAD_V))

    load_raw = copies.local(raw_in, tokens)
    grad_k[...] = jnp.zeros_like(grad_k)
    grad_v[...] = jnp.zeros_like(grad_v)

    def attend_back(head, block):
        lanes = slice(head * HEAD_V, (head + 1) * HEAD_V)
        rows, extent = slice(block * 256, (block + 1) * 256), (block + 1) * 256
        q = jnp.where(head_lanes(head), qs[rows], 0)
        k = ks[0:extent]
        half, scores, keep = scores_of(q, k, block, extent)
        numer = grad_numer[rows, lanes]
        total = grad_denom[rows, head * HEAD_V : head * HEAD_V + 1]
        grad_scores = nt(numer, values[0:extent, lanes]) + total
        grad_s = jnp.where(keep, grad_scores * (0.25 + 0.25 * half), 0.0).astype(BF16)
        moved = nn(grad_s, k)
        if head == 0:
            grad_q[rows] = jnp.where(head_lanes(0), moved, 0.0)
        else:
            grad_q[rows] += jnp.where(head_lanes(1), moved, 0.0)
        grad_k[0:extent] += tn(grad_s, q)
        grad_v[0:extent, lanes] += tn(scores.astype(BF16), numer)

    for block in range(4):
        attend_back(0, block)
    next(early_stages)()
    ups.onward(1)
    ups.onward(-1)
    for block in range(4):
        attend_back(1, block)

    def join(rows):
        inverse = inverses[rows]
        both = grad_q[rows] + pltpu.roll(grad_k[rows], 32, 1)
        grad_qk[rows] = both.astype(BF16)
        scaled_qk[rows] = (both * inverse).astype(BF16)
        both = grad_v[rows]
        grad_values[rows] = both.astype(BF16)
        scaled_values[rows] = (both * jnp.concatenate((inverse, inverse), axis=1)).astype(BF16)

    row_steps(0, 1024, join, 128)
    sums = ReduceTokens(
        copies,
        part_maker([(grad_values, att, VALUE_AT), (grad_qk, att, QK_AT)], y, core),
        y,
        core,
        own,
        sib,
        got_sib,
        out,
        got,
    )
    sums.part(2)
    sums.part(1)
    for _ in range(4):
        next(early_stages)()
    sums.one()
    sums.part(-1)
    sums.part(0)
    load_layer.wait()
    layers.onward(1)
    layers.onward(-1)
    load_raw.wait()

    @pl.loop(0, tokens.shape[1] // 512)
    def _(tile):
        columns = pl.ds(pl.multiple_of(tile * 512, 512), 512)
        left = tokens[:, columns]
        gain = att[columns, 576:577].astype(F32)
        late[columns, 0:256] = (tn(left, scaled_values[...]) * gain).astype(BF16)
        late[columns, 256:LATE_W] = (tn(left, scaled_qk[...]) * gain).astype(BF16)

    late_plane = ReducePlane(
        copies,
        late,
        slice(0, LATE_W),
        x,
        z,
        core,
        late_out1,
        late_got1,
        late_mid,
        late_out2,
        late_got2,
    )
    late_stages = iter(late_plane.stages())
    next(late_stages)()
    def take(target):
        def act(rows, total):
            target[rows] = total.astype(BF16)

        return act

    ups.each(take(up_sum))
    send_back(up_sum, up_out)
    sums.two()
    next(late_stages)()
    for _ in range(4):
        next(late_stages)()
    gain_part[...] = jnp.zeros_like(gain_part)

    def back(rows, total):
        moved, terms = norm_back_rows(total, raw[rows].astype(F32), gains[0:1])
        gain_part[...] += terms[:8] + terms[8:]
        last[rows] = (grad_middle[rows] + moved).astype(BF16)

    sums.each(back)
    waits = [copies.swap(last, grad_in, partner, swaps)]
    row = lax.broadcasted_iota(jnp.int32, (8, 1), 0)
    gain_part[...] = jnp.where(
        row == 0,
        jnp.sum(gain_part[...], axis=0, keepdims=True),
        jnp.where(row == 1, jnp.sum(grad_gain2[...], axis=0, keepdims=True), 0.0),
    )
    here = 4 * z + x

    def lanes_of(block):
        return pl.ds(pl.multiple_of(block * 128, 128), 128)

    gain_copies = [
        copies.start(gain_part.at[:, lanes_of(4 * b + a)], gain_got.at[here], at_xz(a, b))
        for a, b in planes
    ]
    gain_own = copies.local(gain_part.at[:, lanes_of(here)], gain_got.at[here])
    for stage in early_stages:
        stage()
    for _ in range(4):
        next(late_stages)()
    for piece in range(PIECES):
        layers.arrive(piece)

    def add(rows):
        layer[rows] = (middle[rows] + layers.total(rows)).astype(BF16)

    row_steps(0, 128, add)
    waits.append(copies.swap(layer, layer_out, partner, swaps))
    early_plane.each(take(early_sum))
    send_back(early_sum, early_out)
    for stage in late_stages:
        stage()
    for copy in gain_copies:
        copy.wait_recv()
    gain_own.wait()
    gain_sum[...] = jnp.sum(gain_got[...], axis=0)
    for c, d in peers:
        back_copies.append(copies.start(gain_sum, gain_back.at[me], {"core": c, "y": d}))
    local.append(copies.local(gain_sum, gain_back.at[me]))
    late_plane.each(take(late_sum))
    send_back(late_sum, late_out)
    for copy in back_copies:
        copy.wait_recv()
    for copy in local:
        copy.wait()
    gain_out[...] = jnp.sum(gain_back[...], axis=0)
    for wait in waits:
        wait()
    copies.finish()


def unpack_kernel(
    late, early, gates, ups, layer, last, hot, query, key, value, out, gate, up, down, layer_out, grad_in
):
    here = gate.shape[1] // 8
    for block in range(8):
        for source, at, grad in ((gates, 0, gate), (ups, 0, up), (early, 0, down)):
            cut = source[block, :, at : at + here]
            grad[:, block * here : (block + 1) * here] = cut.astype(F32)
        value[:, block * 256 : (block + 1) * 256] = late[block, :, 0:256].astype(F32)
        out[:, block * 256 : (block + 1) * 256] = early[block, :, PAD_FF:EARLY_W].astype(F32)
        query[:, block * 32 : (block + 1) * 32] = late[block, :, 256:288].astype(F32)
        key[:, block * 32 : (block + 1) * 32] = late[block, :, 288:320].astype(F32)
    runs = layer.shape[1] // 256
    for run in range(runs):
        for source, target in ((layer, layer_out), (last, grad_in)):
            low = source[:, run * 128 : (run + 1) * 128]
            high = source[:, (runs + run) * 128 : (runs + run + 1) * 128]
            both = jnp.concatenate((low, high), axis=1)
            target[:, run * 256 : (run + 1) * 256] = nn(both, hot[...]).astype(target.dtype)


HBM, VMEM, LOAD = pl.ANY, pltpu.VMEM, "load"


def call(kernel, number, ins, outs, scratch, sems, flops):
    def spec(space):
        return pl.BlockSpec(memory_space=space)

    remote = {}
    given = kernel
    if any(space == LOAD for _, space in ins):
        places = [at for at, (_, space) in enumerate(ins) if space == LOAD]
        held = [VMEM(ins[at][0].shape, ins[at][0].dtype) for at in places]
        scratch = list(scratch) + held + [pltpu.SemaphoreType.DMA((len(held),))]

        def kernel(*refs):
            refs = list(refs)
            send, recv = refs[-2:]
            first = len(refs) - 3 - len(held)
            buffers, arrived = refs[first:-3], refs[-3]
            loads = []
            for index, at in enumerate(places):
                loads.append(pltpu.make_async_copy(refs[at], buffers[index], arrived.at[index]))
                loads[-1].start()
                refs[at] = buffers[index]
            given(*refs[:first], send, recv, loads=loads)

        ins = [(array, HBM if space == LOAD else space) for array, space in ins]
    if number is not None:
        scratch = list(scratch) + [pltpu.SemaphoreType.DMA((sems,)), pltpu.SemaphoreType.DMA((sems,))]
        remote = dict(collective_id=number, has_side_effects=True)
    return pl.pallas_call(
        kernel,
        out_shape=[jax.ShapeDtypeStruct(shape, dtype) for shape, dtype, _ in outs],
        in_specs=[spec(space) for _, space in ins],
        out_specs=[spec(space) for _, _, space in outs],
        scratch_shapes=scratch,
        compiler_params=pltpu.CompilerParams(vmem_limit_bytes=VMEM_LIMIT, **remote),
        cost_estimate=pl.CostEstimate(flops=flops, bytes_accessed=2**26, transcendentals=0),
        name=given.__name__,
    )(*[array for array, _ in ins])


def ring_scratch(width, own=True):
    sums = [VMEM((4, 128, width), F32)] if own else []
    return sums + [
        VMEM((4, 128, width), BF16),
        VMEM((4, 128, width), BF16),
        VMEM((3, 128, width), BF16),
        VMEM((3, 128, width), BF16),
    ]


def plane_scratch(width):
    return [
        VMEM((4, 1, 128, width), BF16),
        VMEM((4, 3, 128, width), BF16),
        VMEM((4, 128, width), BF16),
        VMEM((1, 128, width), BF16),
        VMEM((3, 128, width), BF16),
    ]


def body(
    hidden_in,
    norm1_gain,
    query_weight,
    key_weight,
    value_weight,
    out_weight,
    norm2_gain,
    gate_weight,
    up_weight,
    down_weight,
    cotangent,
    source_id,
    source_counts,
):
    rows, toks, width = hidden_in.shape
    depth, ff = gate_weight.shape
    length, held = 8 * toks, 8 * depth
    mlp_w = 3 * PAD_FF
    scale = row_scale(source_id, source_counts).reshape(1, 1)
    (
        att,
        weights,
        raw_all,
        low,
        qs,
        ks,
        values,
        attended,
        shares,
        inverses,
        gains,
        raw,
        top,
        middle,
        normed2,
    ) = call(
        forward_kernel,
        0,
        [
            (array, VMEM)
            for array in (
                hidden_in.reshape(toks, width),
                cotangent.reshape(toks, width),
                scale,
                lane_order(False),
                query_weight,
                key_weight,
                value_weight,
                out_weight,
                gate_weight,
                up_weight,
                down_weight,
                jnp.stack((norm1_gain, norm2_gain), axis=1),
            )
        ],
        [
            ((width, ATT_W), BF16, HBM),
            ((width, mlp_w), BF16, HBM),
            ((length, width), BF16, HBM),
            ((length, width), BF16, HBM),
            ((length, 128), BF16, HBM),
            ((length, 128), BF16, HBM),
            ((length, 256), BF16, HBM),
            ((length, 256), BF16, HBM),
            ((length, 256), F32, HBM),
            ((length, 128), F32, HBM),
            ((8, width), F32, VMEM),
            ((toks, width), BF16, VMEM),
            ((toks, width), BF16, VMEM),
            ((toks, width), F32, VMEM),
            ((length, width), BF16, HBM),
        ],
        [
            VMEM((8, depth, ATT_W), BF16),
            VMEM((8, depth, mlp_w), BF16),
            VMEM((toks, width), BF16),
            VMEM((toks, width), BF16),
            VMEM((held, ATT_W), BF16),
            VMEM((held, mlp_w), BF16),
            VMEM((length, width), BF16),
            VMEM((width, ATT_W), BF16),
            VMEM((width, 384), BF16),
        ]
        + ring_scratch(width)
        + [
            VMEM((toks, width), BF16),
            VMEM((length, 128), BF16),
            VMEM((length, 128), BF16),
            VMEM((length, 256), BF16),
            VMEM((length, 256), BF16),
            VMEM((length, 256), F32),
            VMEM((length, 128), F32),
        ],
        250,
        4 * 10**9,
    )
    grad_middle, grad_gain2, middle_low, grads, gate_sum, up_mid, layer_parts = call(
        mlp_kernel,
        1,
        [
            (normed2, HBM),
            (low, HBM),
            (weights, HBM),
            (middle, LOAD),
            (top, LOAD),
            (gains, LOAD),
        ],
        [
            ((toks, width), F32, VMEM),
            ((8, width), F32, VMEM),
            ((length, width), BF16, HBM),
            ((width, PAD_FF), BF16, HBM),
            ((held, PAD_FF), BF16, VMEM),
            ((4, held, PAD_FF), BF16, VMEM),
            ((4, toks, width), BF16, HBM),
        ],
        [
            VMEM((length, width), BF16),
            VMEM((length, width), BF16),
            VMEM((width, mlp_w), BF16),
            VMEM((length, PAD_FF), BF16),
            VMEM((length, PAD_FF), BF16),
            VMEM((length, PAD_FF), BF16),
        ]
        + ring_scratch(width)
        + [
            VMEM((4, toks, width), BF16),
            VMEM((4, toks, width), BF16),
            VMEM((4, toks, width), BF16),
            VMEM((toks, width), BF16),
        ]
        + plane_scratch(PAD_FF)
        + plane_scratch(PAD_FF)[:2],
        200,
        30 * 10**9,
    )
    late_back, early_back, gate_back, up_back, last, layer, gain_sums = call(
        back_kernel,
        2,
        [
            (middle_low, HBM),
            (raw_all, HBM),
            (att, LOAD),
            (qs, LOAD),
            (ks, LOAD),
            (values, LOAD),
            (attended, LOAD),
            (shares, LOAD),
            (inverses, LOAD),
            (raw, LOAD),
            (grad_middle, LOAD),
            (middle, LOAD),
            (gains, LOAD),
            (grad_gain2, LOAD),
            (grads, HBM),
            (layer_parts, HBM),
            (gate_sum, LOAD),
            (up_mid, LOAD),
        ],
        [
            ((8, depth, LATE_W), BF16, HBM),
            ((8, depth, EARLY_W), BF16, HBM),
            ((8, depth, PAD_FF), BF16, HBM),
            ((8, depth, PAD_FF), BF16, HBM),
            ((toks, width), BF16, HBM),
            ((toks, width), BF16, HBM),
            ((8, 128), F32, VMEM),
        ],
        [
            VMEM((length, width), BF16),
            VMEM((width, EARLY_W), BF16),
            VMEM((width, LATE_W), BF16),
            VMEM((4, toks, width), BF16),
            VMEM((length, 256), BF16),
            VMEM((length, 256), F32),
            VMEM((length, 128), F32),
            VMEM((length, 128), F32),
            VMEM((length, 256), F32),
            VMEM((length, 128), BF16),
            VMEM((length, 256), BF16),
            VMEM((length, 128), BF16),
            VMEM((length, 256), BF16),
        ]
        + ring_scratch(width)
        + [VMEM((1, toks, width), BF16), VMEM((3, toks, width), BF16)]
        + plane_scratch(EARLY_W)
        + plane_scratch(LATE_W)
        + [
            VMEM((1, held, PAD_FF), BF16),
            VMEM((3, held, PAD_FF), BF16),
            VMEM((held, PAD_FF), BF16),
            VMEM((held, EARLY_W), BF16),
            VMEM((held, LATE_W), BF16),
            VMEM((toks, width), BF16),
            VMEM((toks, width), BF16),
            VMEM((8, width), F32),
            VMEM((16, 8, 128), F32),
            VMEM((8, 128), F32),
            VMEM((8, 8, 128), F32),
        ],
        240,
        8 * 10**9,
    )
    grads_out = call(
        unpack_kernel,
        None,
        [(array, VMEM) for array in (late_back, early_back, gate_back, up_back, layer, last, lane_order(True))],
        [
            ((depth, query_weight.shape[1]), F32, VMEM),
            ((depth, key_weight.shape[1]), F32, VMEM),
            ((depth, value_weight.shape[1]), F32, VMEM),
            ((depth, out_weight.shape[1]), F32, VMEM),
            ((depth, ff), F32, VMEM),
            ((depth, ff), F32, VMEM),
            ((depth, ff), F32, VMEM),
            ((toks, width), BF16, VMEM),
            ((toks, width), F32, VMEM),
        ],
        [],
        0,
        0,
    )
    grad_query, grad_key, grad_value, grad_out, grad_gate, grad_up, grad_down = grads_out[:7]
    at = (lax.axis_index("core") * 4 + lax.axis_index("y")) * depth
    pair = lax.dynamic_slice(gain_sums, (0, at), (8, depth))
    return (
        grads_out[7].reshape(rows, toks, width),
        grads_out[8].reshape(rows, toks, width),
        pair[0],
        grad_query,
        grad_key,
        grad_value,
        grad_out,
        pair[1],
        grad_gate,
        grad_up,
        grad_down,
    )


def solution(mesh):
    zlo, chips_x, cores, chips_y, zhi = 2, 4, 2, 4, 2
    whole = Mesh(mesh.devices.reshape(zlo, chips_x, cores, chips_y, zhi), AXES)
    weight = P(AXES, None)
    gain = P(AXES)
    tokens = P(DP, SEQ, None)
    return jax.shard_map(
        body,
        mesh=whole,
        in_specs=(
            tokens,
            gain,
            weight,
            weight,
            weight,
            weight,
            gain,
            weight,
            weight,
            weight,
            tokens,
            P(DP),
            P(),
        ),
        out_specs=(
            tokens,
            tokens,
            gain,
            weight,
            weight,
            weight,
            weight,
            gain,
            weight,
            weight,
            weight,
        ),
        check_vma=False,
    )
```

```python
import jax
import jax.numpy as jnp
import numpy as np
from jax import lax
from jax.experimental import pallas as pl
from jax.experimental.pallas import tpu as pltpu
from jax.sharding import Mesh, PartitionSpec as P

FEAT = 16
HEAD_V = 128
PAD_FF = 768
ATT_W = 640
QK_AT = slice(512, 640)
OUT_AT = slice(256, 512)
VALUE_AT = slice(0, 256)
EARLY_W = PAD_FF + 256
LATE_W = 384

norm_eps = 1e-05
AXES = ("zlo", "x", "core", "y", "zhi")
DP = ("zlo", "x", "core")
SEQ = ("y", "zhi")

MESH = pl.DeviceIdType.MESH
VMEM_LIMIT = 61 * 2**20
PIECES = 4
PLANE_PIECES = 2
TILE = 256
STEP = 16
BF16, F32 = jnp.bfloat16, jnp.float32


def row_scale(source_id, source_counts):
    picked = jnp.sum(
        jnp.where(
            source_id[:, None] == jnp.arange(source_counts.shape[0], dtype=jnp.int32)[None, :],
            source_counts[None, :],
            0,
        ),
        axis=1,
    )
    return 4.0 / jnp.sqrt(picked.astype(F32))


def lane_order(back):
    at = np.arange(256)
    to = (at // 16 % 2) * 128 + (at // 32) * 16 + at % 16
    hot = np.zeros((256, 256), np.float32)
    hot[at, to] = 1.0
    return jnp.asarray(hot.T if back else hot, BF16)


def place():
    z = lax.axis_index("zhi") * 2 + lax.axis_index("zlo")
    return lax.axis_index("x"), lax.axis_index("y"), z, lax.axis_index("core")


def around(index):
    return lax.rem(index + 8, 4)


def at_y(y):
    return {"y": around(y)}


def at_core(core):
    return {"core": core}


def at_xz(x, z):
    x, z = around(x), around(z)
    return {"x": x, "zhi": z // 2, "zlo": lax.rem(z, 2)}


def ring_peers(y, core):
    return [at_y(y + 1), at_y(y - 1), at_core(1 - core)]


def plane_peers(x, z):
    return [at_xz(x + 1, z), at_xz(x - 1, z), at_xz(x, z + 1), at_xz(x, z - 1)]


def group_peers(y, core):
    return [
        (lax.rem(core + dc, 2), lax.rem(y + dy, 4))
        for dc in (0, 1)
        for dy in range(4)
        if (dc, dy) != (0, 0)
    ]


def hello(devices, partner=None, swaps=None):
    barrier = pltpu.get_barrier_semaphore()
    for device in devices:
        pl.semaphore_signal(barrier, inc=1, device_id=device, device_id_type=MESH)
    count = len(devices)
    if partner is not None:

        @pl.when(swaps)
        def _():
            pl.semaphore_signal(barrier, inc=1, device_id=partner, device_id_type=MESH)

        count = count + jnp.where(swaps, 1, 0)

    def wait():
        pl.semaphore_wait(barrier, count)

    return wait


class Copies:
    def __init__(self, send, recv):
        self.send, self.recv, self.used, self.open = send, recv, 0, []

    def start(self, src, dst, device):
        copy = pltpu.make_async_remote_copy(
            src_ref=src,
            dst_ref=dst,
            send_sem=self.send.at[self.used],
            recv_sem=self.recv.at[self.used],
            device_id=device,
            device_id_type=MESH,
        )
        copy.start()
        self.used += 1
        self.open.append(copy)
        return copy

    def local(self, src, dst):
        copy = pltpu.make_async_copy(src, dst, self.send.at[self.used])
        copy.start()
        self.used += 1
        return copy

    def swap(self, src, dst, partner, swaps):
        at = self.used
        self.used += 1

        def over():
            return pltpu.make_async_remote_copy(
                src_ref=src,
                dst_ref=dst,
                send_sem=self.send.at[at],
                recv_sem=self.recv.at[at],
                device_id=partner,
                device_id_type=MESH,
            )

        def stay():
            return pltpu.make_async_copy(src, dst, self.send.at[at])

        @pl.when(swaps)
        def _():
            over().start()

        @pl.when(jnp.logical_not(swaps))
        def _():
            stay().start()

        def wait():
            @pl.when(swaps)
            def _():
                over().wait()

            @pl.when(jnp.logical_not(swaps))
            def _():
                stay().wait()

        return wait

    def finish(self):
        for copy in self.open:
            copy.wait_send()


def way(piece):
    return 1 if piece % 2 == 0 else -1


def slab(ref, block, rows, piece=None, pieces=PIECES):
    if piece is None:
        return ref.at[pl.ds(pl.multiple_of(block * rows, 128), rows)]
    size = rows // pieces
    return ref.at[pl.ds(pl.multiple_of(block * rows + piece * size, 32), size)]


def row_steps(start, size, act, step=STEP):
    @pl.loop(0, size // step, unroll=min(4, size // step))
    def _(at):
        act(pl.ds(pl.multiple_of(start + at * step, step), step))


class GatherRing:
    def __init__(self, copies, to, mine, full, block_of, me, rows, pieces=PIECES):
        self.copies, self.to, self.full, self.block_of = copies, to, full, block_of
        self.me, self.rows, self.sent, self.onward = me, rows, {}, {}
        self.pieces = pieces
        size = rows // pieces
        for piece in range(pieces):
            for step in (way(piece), -way(piece)):
                self.sent[step, piece] = copies.start(
                    mine.at[pl.ds(piece * size, size)],
                    slab(full, block_of(me), rows, piece, pieces),
                    to(me + step),
                )

    def forward(self):
        for piece in range(self.pieces):
            step = way(piece)
            self.sent[step, piece].wait_recv()
            here = slab(self.full, self.block_of(self.me - step), self.rows, piece, self.pieces)
            self.onward[piece] = self.copies.start(here, here, self.to(self.me + step))

    def near(self):
        for piece in range(self.pieces):
            self.sent[-way(piece), piece].wait_recv()

    def far(self):
        for piece in range(self.pieces):
            self.onward[piece].wait_recv()


class GatherTokens:
    def __init__(self, copies, mine, full, y, core):
        self.copies, self.full, self.y, self.core = copies, full, y, core
        self.rows = mine.shape[0]
        self.shared = {}
        self.own = copies.local(mine, slab(full, self.block_of(y), self.rows))
        self.shared[0] = copies.start(mine, slab(full, self.block_of(y), self.rows), at_core(1 - core))
        self.ring = GatherRing(copies, at_y, mine, full, self.block_of, y, self.rows)

    def block_of(self, index):
        return around(index) * 2 + self.core

    def share(self, k):
        here = slab(self.full, self.block_of(self.y + k), self.rows)
        self.shared[k] = self.copies.start(here, here, at_core(1 - self.core))

    def forward(self):
        self.ring.forward()

    def near(self):
        self.ring.near()
        self.share(1)
        self.share(-1)

    def far(self):
        self.ring.far()
        self.share(2)

    def finish(self):
        self.own.wait()
        for copy in self.shared.values():
            copy.wait_recv()


class GatherPlane:
    def __init__(self, copies, mine, full, x, z, core):
        self.copies, self.full = copies, full
        rows = mine.shape[0]

        def block(a, b):
            a, b = around(a), around(b)
            return jnp.where(core == 0, 4 * b + a, 4 * a + b)

        first, second = jnp.where(core == 0, x, z), jnp.where(core == 0, z, x)

        def to_first(index):
            return at_xz(jnp.where(core == 0, index, x), jnp.where(core == 0, z, index))

        def to_second(index):
            return at_xz(jnp.where(core == 0, x, index), jnp.where(core == 0, index, z))

        def onto(k, source=None):
            a = first + k
            if source is None:
                source = slab(full, block(a, second), rows)
            return GatherRing(
                copies, to_second, source, full, lambda b: block(a, b), second, rows, PLANE_PIECES
            )

        self.onto = onto
        self.own = copies.local(mine, slab(full, block(first, second), rows))
        self.ring = GatherRing(
            copies, to_first, mine, full, lambda a: block(a, second), first, rows, PLANE_PIECES
        )
        self.rings = {0: onto(0, mine)}

    def stages(self):
        def one():
            self.ring.forward()

        def two():
            self.ring.near()
            self.rings[1] = self.onto(1)
            self.rings[-1] = self.onto(-1)

        def three():
            self.rings[0].forward()

        def four():
            self.ring.far()
            self.rings[2] = self.onto(2)

        def five():
            self.rings[1].forward()
            self.rings[-1].forward()

        def six():
            self.rings[2].forward()
            self.rings[0].near()
            self.rings[0].far()

        def seven():
            for k in (1, -1, 2):
                self.rings[k].near()
                self.rings[k].far()
            self.own.wait()

        return [one, two, three, four, five, six, seven]


class ReduceRing:
    def __init__(self, copies, to, me, read, out, got, rows, source=None, pieces=PIECES):
        self.copies, self.to, self.me, self.read = copies, to, me, read
        self.out, self.got, self.rows, self.source, self.sent = out, got, rows, source, {}
        self.pieces = pieces
        self.size = rows // pieces

    def span(self, piece):
        return pl.ds(piece * self.size, self.size)

    def push(self, slot, k, piece, device):
        span = self.span(piece)
        if self.source is not None:
            ref = self.source(k, span)
        else:

            def fill(rows):
                self.out[slot, rows] = self.read(k, rows).astype(BF16)

            row_steps(piece * self.size, self.size, fill)
            ref = self.out.at[slot, span]
        self.sent[slot, piece] = self.copies.start(ref, self.got.at[slot, span], device)

    def far(self):
        for piece in range(self.pieces):
            self.push(0, 2, piece, self.to(self.me + way(piece)))

    def direct(self, k):
        for piece in range(self.pieces):
            if way(piece) == -k:
                self.push(1, k, piece, self.to(self.me + k))

    def onward(self, k):
        slot = 2 if self.source is None else 0
        for piece in range(self.pieces):
            if way(piece) == k:
                self.sent[0, piece].wait_recv()

                def fill(rows):
                    self.out[slot, rows] = (
                        self.read(k, rows) + self.got[0, rows].astype(F32)
                    ).astype(BF16)

                row_steps(piece * self.size, self.size, fill)
                span = self.span(piece)
                self.sent[2, piece] = self.copies.start(
                    self.out.at[slot, span], self.got.at[2, span], self.to(self.me + k)
                )

    def arrive(self, piece):
        self.sent[1, piece].wait_recv()
        self.sent[2, piece].wait_recv()

    def each(self, act):
        for piece in range(self.pieces):
            self.arrive(piece)

            def take(rows):
                act(rows, self.total(rows))

            row_steps(piece * self.size, self.size, take)

    def total(self, rows):
        return self.read(0, rows) + self.got[1, rows].astype(F32) + self.got[2, rows].astype(F32)


class ReduceTokens:
    def __init__(self, copies, make, y, core, own, sib, got_sib, out, got):
        self.copies, self.make, self.y, self.core = copies, make, y, core
        self.own, self.sib, self.got_sib, self.shared = own, sib, got_sib, {}
        self.ring = ReduceRing(copies, at_y, y, self.read, out, got, own.shape[1])

    def read(self, k, rows):
        return self.own[k % 4, rows] + self.got_sib[k % 4, rows].astype(F32)

    def share(self, k):
        self.shared[k] = self.copies.start(
            self.sib.at[k % 4], self.got_sib.at[k % 4], at_core(1 - self.core)
        )

    def part(self, k):
        self.make(k, self.own.at[k % 4], self.sib.at[k % 4])
        self.share(k)

    def one(self):
        self.shared[2].wait_recv()
        self.ring.far()
        self.shared[1].wait_recv()
        self.ring.direct(1)

    def two(self):
        self.shared[-1].wait_recv()
        self.ring.direct(-1)
        self.ring.onward(1)
        self.ring.onward(-1)
        self.shared[0].wait_recv()

    def each(self, act):
        for piece in range(PIECES):
            self.ring.arrive(piece)

            def take(rows):
                act(rows, self.ring.total(rows))

            row_steps(piece * self.ring.size, self.ring.size, take)


def second_ring(copies, mid, x, z, core, out2, got2):
    last = jnp.where(core == 0, x, z)

    def to_last(index):
        return at_xz(jnp.where(core == 0, index, x), jnp.where(core == 0, z, index))

    def read(step, span):
        return mid[step % 4, span].astype(F32)

    def source(step, span):
        return mid.at[step % 4, span]

    rows = mid.shape[1]
    return ReduceRing(copies, to_last, last, read, out2, got2, rows, source, PLANE_PIECES)


class ReducePlane:
    def __init__(self, copies, parts, lanes, x, z, core, out1, got1, mid, out2, got2, sent=None):
        rows = mid.shape[1]
        sent = parts if sent is None else sent

        def block(a, b):
            a, b = around(a), around(b)
            return jnp.where(core == 0, 4 * b + a, 4 * a + b)

        last, first = jnp.where(core == 0, x, z), jnp.where(core == 0, z, x)

        def to_first(index):
            return at_xz(jnp.where(core == 0, x, index), jnp.where(core == 0, index, z))

        def ring(k):
            def place_of(step, span):
                start = block(last + k, first + step) * rows + span.start
                return pl.ds(pl.multiple_of(start, STEP), span.size)

            def read(step, span):
                return parts[place_of(step, span), lanes].astype(F32)

            def source(step, span):
                return sent.at[place_of(step, span), lanes]

            return ReduceRing(
                copies,
                to_first,
                first,
                read,
                out1.at[k % 4],
                got1.at[k % 4],
                rows,
                source,
                PLANE_PIECES,
            )

        self.mid = mid
        self.rings = {k: ring(k) for k in (2, 1, -1, 0)}

        if got2 is not None:
            self.ring = second_ring(copies, mid, x, z, core, out2, got2)

    def start(self):
        for ring in self.rings.values():
            ring.far()

    def direct(self):
        for ring in self.rings.values():
            ring.direct(1)
            ring.direct(-1)

    def onward(self, k):
        self.rings[k].onward(1)
        self.rings[k].onward(-1)

    def middle(self, k):
        ring = self.rings[k]
        for piece in range(PLANE_PIECES):
            ring.arrive(piece)

            def fill(rows):
                self.mid[k % 4, rows] = ring.total(rows).astype(BF16)

            row_steps(piece * ring.size, ring.size, fill)

    def stages(self):
        def ends(k, then):
            def act():
                self.middle(k)
                then()

            return act

        return (
            [self.start, self.direct]
            + [lambda k=k: self.onward(k) for k in (2, 1, -1, 0)]
            + [
                ends(2, self.ring.far),
                ends(1, lambda: self.ring.direct(1)),
                ends(-1, lambda: self.ring.direct(-1)),
                ends(0, lambda: None),
                lambda: (self.ring.onward(1), self.ring.onward(-1)),
            ]
        )

    def first_stages(self):
        return (
            [self.start, self.direct]
            + [lambda k=k: self.onward(k) for k in (2, 1, -1, 0)]
            + [lambda k=k: self.middle(k) for k in (2, 1, -1, 0)]
        )

    def each(self, act):
        self.ring.each(act)


def nt(left, right):
    return lax.dot_general(left, right, (((1,), (1,)), ((), ())), preferred_element_type=F32)


def tn(left, right):
    return lax.dot_general(left, right, (((0,), (0,)), ((), ())), preferred_element_type=F32)


def nn(left, right):
    return jnp.dot(left, right, preferred_element_type=F32)


def chip_rows(block):
    return pl.ds(pl.multiple_of(block * 256, 256), 256)


def part_maker(pairs, y, core):
    def make(k, mine, theirs):
        rows = chip_rows(around(y + k))

        @pl.loop(0, mine.shape[-1] // TILE)
        def _(tile):
            columns = pl.ds(pl.multiple_of(tile * TILE, TILE), TILE)
            total = None
            for left, right, lanes in pairs:
                term = nt(left[rows, :], right[columns, lanes])
                total = term if total is None else total + term
            low, high = total[:128], total[128:]
            mine[:, columns] = jnp.where(core == 0, low, high)
            theirs[:, columns] = jnp.where(core == 0, high, low).astype(BF16)

    return make


def inverse_of(value):
    return lax.rsqrt(jnp.mean(value * value, axis=-1, keepdims=True) + norm_eps)


def norm_back_rows(grad, value, gain):
    inverse = inverse_of(value)
    unit = value * inverse
    scaled = grad * gain
    moved = inverse * (scaled - unit * jnp.mean(scaled * unit, axis=-1, keepdims=True))
    return moved, grad * unit


def reorder_into(target, source, hot):
    runs = source.shape[1] // 256
    for run in range(runs):
        moved = nn(source[:, run * 256 : (run + 1) * 256], hot[...]).astype(BF16)
        target[:, run * 128 : (run + 1) * 128] = moved[:, :128]
        target[:, (runs + run) * 128 : (runs + run + 1) * 128] = moved[:, 128:]


def gain_rows(att):
    row = lax.broadcasted_iota(jnp.int32, (8, 128), 0)
    lane = lax.broadcasted_iota(jnp.int32, (8, 128), 1)
    pick = jnp.where((lane == row + 64) & (row < 2), 1.0, 0.0).astype(BF16)
    return nt(pick, att[:, QK_AT])


def head_lanes(head):
    lane = lax.broadcasted_iota(jnp.int32, (1, 128), 1)
    return (lane >= head * FEAT) & (lane < (head + 1) * FEAT)


def scores_of(q, k, block, extent):
    x = nt(q, k) * 0.25
    row = lax.broadcasted_iota(jnp.int32, (256, extent), 0) + block * 256
    keep = row >= lax.broadcasted_iota(jnp.int32, (256, extent), 1)
    return x, jnp.where(keep, 1.0 + x + 0.5 * (x * x), 0.0), keep


def forward_kernel(
    hidden,
    cotangent,
    scale,
    hot,
    query,
    key,
    value,
    out_weight,
    gate,
    up,
    down,
    gain_pair,
    att_out,
    weights,
    raw_out,
    low_out,
    qs_out,
    ks_out,
    values_out,
    attended_out,
    shares_out,
    inverses_out,
    gains,
    raw,
    top,
    middle,
    normed2,
    att_cut,
    mlp_cut,
    raw_cut,
    top_cut,
    att_own,
    mlp_own,
    raw_all,
    att_all,
    att_scaled,
    own,
    sib,
    got_sib,
    out,
    got,
    low,
    qs,
    ks,
    values,
    attended,
    shares,
    inverses,
    send,
    recv,
):
    x, y, z, core = place()
    zhi = z // 2
    partner = {"core": 1 - core, "zhi": 1 - zhi}
    swaps = core != zhi
    peers = group_peers(y, core)
    ready = hello(
        [{"core": c, "y": d} for c, d in peers] + plane_peers(x, z), partner, swaps
    )
    copies = Copies(send, recv)
    me = core * 4 + y
    depth, here = gate.shape[0], gate.shape[1] // 8

    def spread(cuts, target):
        rows = pl.ds(pl.multiple_of(me * depth, depth), depth)
        kept = copies.local(cuts.at[me], target.at[rows])
        got = [
            copies.start(cuts.at[c * 4 + d], target.at[rows], {"core": c, "y": d}) for c, d in peers
        ]

        def wait():
            kept.wait()
            for copy in got:
                copy.wait_recv()

        return wait

    reorder_into(raw_cut, hidden, hot)
    gap = jnp.zeros((depth, 62), BF16)
    for block in range(8):
        att_cut[block, :, VALUE_AT] = value[:, block * 256 : (block + 1) * 256]
        att_cut[block, :, OUT_AT] = out_weight[:, block * 256 : (block + 1) * 256]
        att_cut[block, :, QK_AT] = jnp.concatenate(
            (
                query[:, block * 32 : (block + 1) * 32],
                key[:, block * 32 : (block + 1) * 32],
                gain_pair[...],
                gap,
            ),
            axis=1,
        )
    ready()
    wait_raw = copies.swap(raw_cut, raw, partner, swaps)
    wait_att = spread(att_cut, att_own)
    gap = jnp.zeros((depth, PAD_FF - here), BF16)
    for block in range(8):
        for at, weight in enumerate((gate, up, down)):
            cut = weight[:, block * here : (block + 1) * here]
            mlp_cut[block, :, at * PAD_FF : (at + 1) * PAD_FF] = jnp.concatenate((cut, gap), axis=1)
    wait_raw()
    tokens = GatherTokens(copies, raw, raw_all, y, core)
    wait_mlp = spread(mlp_cut, mlp_own)

    def weigh(rows):
        top_cut[rows] = (cotangent[rows].astype(F32) * scale[...]).astype(BF16)

    row_steps(0, top_cut.shape[0], weigh)
    reorder_into(top_cut, top_cut[...], hot)
    wait_att()
    plane = GatherPlane(copies, att_own, att_all, x, z, core)
    wait_top = copies.swap(top_cut, top, partner, swaps)

    def invert(block):
        def act(rows):
            inverse = inverse_of(raw_all[rows].astype(F32))
            inverses[rows] = jnp.broadcast_to(inverse, (STEP, 128))

        row_steps(block * 128, 128, act)

    one, two, three, four, five, six, seven = plane.stages()
    one()
    two()
    tokens.forward()
    three()
    four()
    tokens.shared[0].wait_recv()
    tokens.own.wait()
    invert(2 * y)
    invert(2 * y + 1)
    five()
    six()
    wait_mlp()
    mlp_plane = GatherPlane(copies, mlp_own, weights, x, z, core)
    mlp_stages = iter(mlp_plane.stages())
    tokens.near()
    invert(2 * around(y + 1) + core)
    invert(2 * around(y - 1) + core)
    tokens.far()
    wait_top()
    tops = GatherTokens(copies, top, low_out, y, core)
    invert(2 * around(y + 2) + core)
    seven()
    gains[...] = gain_rows(att_all)

    def scale_rows(rows):
        gain = att_all[rows, 576:577].astype(F32)
        att_scaled[rows, 0:256] = (att_all[rows, VALUE_AT].astype(F32) * gain).astype(BF16)
        att_scaled[rows, 256:384] = (att_all[rows, QK_AT].astype(F32) * gain).astype(BF16)

    row_steps(0, att_all.shape[0], scale_rows, 128)
    tokens.shared[1].wait_recv()
    tokens.shared[-1].wait_recv()
    invert(2 * around(y + 1) + 1 - core)
    invert(2 * around(y - 1) + 1 - core)
    tokens.shared[2].wait_recv()
    invert(2 * around(y + 2) + 1 - core)
    kept = [copies.local(att_all, att_out), copies.local(raw_all, raw_out)]

    def stores():
        pairs = (
            (qs, qs_out),
            (ks, ks_out),
            (values, values_out),
            (attended, attended_out),
            (shares, shares_out),
            (inverses, inverses_out),
        )
        for source, target in pairs:
            kept.append(copies.local(source, target))


    @pl.loop(0, 2, unroll=True)
    def _(half):
        rows = pl.ds(pl.multiple_of(half * 512, 512), 512)
        inverse = inverses[rows]
        block = raw_all[rows]
        both = nn(block, att_scaled[:, 0:256])
        values[rows] = (both * jnp.concatenate((inverse, inverse), axis=1)).astype(BF16)
        both = nn(block, att_scaled[:, 256:384]) * inverse
        lane = lax.broadcasted_iota(jnp.int32, (1, 128), 1)
        qs[rows] = jnp.where(lane < 32, both, 0.0).astype(BF16)
        ks[rows] = jnp.where(lane < 32, pltpu.roll(both, 96, 1), 0.0).astype(BF16)

    for head in range(2):
        lanes = slice(head * HEAD_V, (head + 1) * HEAD_V)
        for block in range(4):
            rows, extent = slice(block * 256, (block + 1) * 256), (block + 1) * 256
            q = jnp.where(head_lanes(head), qs[rows], 0)
            unused, scores, unused_keep = scores_of(q, ks[0:extent], block, extent)
            share = 1.0 / jnp.sum(scores, axis=-1, keepdims=True)
            numer = nn(scores.astype(BF16), values[0:extent, lanes])
            attended[rows, lanes] = (numer * share).astype(BF16)
            shares[rows, lanes] = jnp.broadcast_to(share, (256, HEAD_V))
        if head == 0:
            tops.forward()
    stores()
    sums = ReduceTokens(
        copies, part_maker([(attended, att_all, OUT_AT)], y, core), y, core, own, sib, got_sib, out, got
    )
    sums.part(2)
    sums.part(1)
    for _ in range(3):
        next(mlp_stages)()
    sums.part(-1)
    sums.one()
    sums.part(0)
    next(mlp_stages)()
    sums.two()
    next(mlp_stages)()
    tops.near()

    def norm2(rows, total):
        value = raw[rows].astype(F32) + total
        middle[rows] = value
        low[rows] = (value * inverse_of(value) * gains[1:2]).astype(BF16)

    sums.each(norm2)
    back = GatherTokens(copies, low, normed2, y, core)
    next(mlp_stages)()
    tops.far()
    back.forward()
    back.near()
    back.far()
    next(mlp_stages)()
    tops.finish()
    back.finish()
    for copy in kept:
        copy.wait()
    copies.finish()


def mlp_kernel(
    normed2_in,
    low_in,
    weights_in,
    middle,
    top,
    gains,
    grad_middle,
    grad_gain,
    middle_low,
    grads,
    gate_sum,
    up_mid,
    layer_parts,
    normed2,
    grad_low,
    weights,
    hidden,
    gate_act,
    up_act,
    own,
    sib,
    got_sib,
    out,
    got,
    sib2,
    got_sib2,
    layer,
    low,
    plane_out1,
    plane_got1,
    plane_mid,
    plane_out2,
    plane_got2,
    up_out1,
    up_got1,
    send,
    recv,
    loads=(),
):
    x, y, z, core = place()
    copies = Copies(send, recv)
    ready = hello(ring_peers(y, core) + plane_peers(x, z))
    order = (2, 1, -1, 0)
    operands, loads = loads, {}

    def load(k):
        slot = order.index(k)
        for at, owner in enumerate((core, 1 - core)):
            block = around(y + k) * 2 + owner
            rows = pl.ds(slot * 256 + at * 128, 128)
            for source, target in ((normed2_in, normed2), (low_in, grad_low)):
                loads.setdefault(k, []).append(copies.local(slab(source, block, 128), target.at[rows]))

    def lanes(at):
        return slice(at * PAD_FF, (at + 1) * PAD_FF)

    def load_tile(tile):
        cuts = [slice(at * PAD_FF + tile * TILE, at * PAD_FF + (tile + 1) * TILE) for at in range(3)]
        loads["w", tile] = [copies.local(weights_in.at[:, cut], weights.at[:, cut]) for cut in cuts]

    load(2)
    load(1)
    load_tile(0)
    ready()
    for copy in operands:
        copy.wait()

    def act_tile(half, tile):
        rows = slice(half * 512, (half + 1) * 512)
        here = slice(tile * TILE, (tile + 1) * TILE)

        def cut(at):
            return weights[:, at * PAD_FF + tile * TILE : at * PAD_FF + (tile + 1) * TILE]

        block = normed2[rows]
        gate = nn(block, cut(0))
        upward = nn(block, cut(1))
        grad_hidden = nn(grad_low[rows], cut(2))
        sigma = jax.nn.sigmoid(gate)
        silu = gate * sigma
        hidden[rows, here] = (silu * upward).astype(BF16)
        slope = sigma + silu * (1.0 - sigma)
        gate_act[rows, here] = (grad_hidden * upward * slope).astype(BF16)
        up_act[rows, here] = (grad_hidden * silu).astype(BF16)

    def part_pair(half, pairs, sib_ref):
        rows = slice(half * 512, (half + 1) * 512)

        @pl.loop(0, own.shape[-1] // 512)
        def _(tile):
            columns = pl.ds(pl.multiple_of(tile * 512, 512), 512)
            total = None
            for left, right in pairs:
                term = nt(left[rows, :], weights[columns, right])
                total = term if total is None else total + term
            for at in range(2):
                k = order[2 * half + at] % 4
                own[k, :, columns] = total[at * 256 : at * 256 + 128]
                sib_ref[k, :, columns] = total[at * 256 + 128 : at * 256 + 256].astype(BF16)

    def grad_block(at, left, right):
        @pl.loop(0, left.shape[1] // 512)
        def _(tile):
            columns = pl.ds(pl.multiple_of(tile * 512, 512), 512)
            weights[columns, lanes(at)] = tn(left[:, columns], right[...]).astype(BF16)

    sums = ReduceTokens(copies, None, y, core, own, sib, got_sib, out, got)
    acts = [(gate_act, lanes(0)), (up_act, lanes(1))]
    for copy in loads[2] + loads[1]:
        copy.wait()
    for tile in range(3):
        for copy in loads["w", tile]:
            copy.wait()
        if tile == 0:
            load_tile(1)
            load_tile(2)
            load(-1)
            load(0)
        act_tile(0, tile)
    part_pair(0, acts, sib)
    sums.share(2)
    sums.share(1)
    for copy in loads[-1] + loads[0]:
        copy.wait()
    act_tile(1, 0)
    sums.one()
    act_tile(1, 1)
    act_tile(1, 2)
    part_pair(1, acts, sib)
    sums.share(-1)
    sums.share(0)
    sums.two()
    grad_block(0, normed2, gate_act)
    plane = ReducePlane(
        copies, weights, lanes(0), x, z, core, plane_out1, plane_got1, plane_mid, plane_out2, plane_got2
    )
    stages = iter(plane.stages())
    next(stages)()
    grad_gain[...] = jnp.zeros_like(grad_gain)

    def back(rows, total):
        moved, terms = norm_back_rows(total, middle[rows], gains[1:2])
        grad_gain[...] += terms[:8] + terms[8:]
        value = top[rows].astype(F32) + moved
        grad_middle[rows] = value
        low[rows] = value.astype(BF16)

    sums.each(back)
    gather = GatherTokens(copies, low, middle_low, y, core)
    next(stages)()
    grad_block(1, normed2, up_act)
    up_plane = ReducePlane(
        copies, weights, lanes(1), x, z, core, up_out1, up_got1, up_mid, None, None
    )
    up_stages = iter(up_plane.first_stages())
    next(up_stages)()
    for _ in range(4):
        next(stages)()
    layers = ReduceTokens(copies, None, y, core, own, sib2, got_sib2, None, None)
    part_pair(0, [(hidden, lanes(2))], sib2)
    layers.share(2)
    layers.share(1)
    gather.forward()
    next(up_stages)()
    part_pair(1, [(hidden, lanes(2))], sib2)
    layers.share(-1)
    layers.share(0)
    for _ in range(4):
        next(up_stages)()
    for _ in range(4):
        next(stages)()
    gather.near()
    grad_block(2, grad_low, hidden)
    stored = [copies.local(weights.at[:, lanes(2)], grads)]
    gather.far()
    for stage in stages:
        stage()
    for stage in up_stages:
        stage()
    for k in order:
        layers.shared[k].wait_recv()

        def add(rows, k=k):
            layer[k % 4, rows] = layers.read(k, rows).astype(BF16)

        row_steps(0, 128, add)
    stored.append(copies.local(layer, layer_parts))

    def take(rows, total):
        gate_sum[rows] = total.astype(BF16)

    plane.each(take)
    gather.finish()
    for copy in stored:
        copy.wait()
    copies.finish()


def back_kernel(
    low_in,
    raw_in,
    att,
    qs,
    ks,
    values,
    attended,
    shares,
    inverses,
    raw,
    grad_middle,
    middle,
    gains,
    grad_gain2,
    grads_in,
    layer_in,
    gate_sum,
    up_mid,
    late_out,
    early_out,
    gate_out,
    up_out,
    grad_in,
    layer_out,
    gain_out,
    tokens,
    early,
    late,
    layer_parts,
    grad_numer,
    grad_denom,
    grad_q,
    grad_k,
    grad_v,
    grad_qk,
    grad_values,
    scaled_qk,
    scaled_values,
    own,
    sib,
    got_sib,
    out,
    got,
    layer_sent,
    layer_got,
    early_out1,
    early_got1,
    early_mid,
    early_out2,
    early_got2,
    late_out1,
    late_got1,
    late_mid,
    late_out2,
    late_got2,
    up_out2,
    up_got2,
    up_sum,
    early_sum,
    late_sum,
    last,
    layer,
    gain_part,
    gain_got,
    gain_sum,
    gain_back,
    send,
    recv,
    loads=(),
):
    x, y, z, core = place()
    zhi = z // 2
    partner = {"core": 1 - core, "zhi": 1 - zhi}
    swaps = core != zhi
    copies = Copies(send, recv)
    peers = group_peers(y, core)
    planes = [
        (lax.rem(x + dx, 4), lax.rem(z + dz, 4))
        for dx in range(4)
        for dz in range(4)
        if (dx, dz) != (0, 0)
    ]
    ready = hello(
        [{"core": c, "y": d} for c, d in peers] + [at_xz(a, b) for a, b in planes], partner, swaps
    )
    load_low = copies.local(low_in, tokens)
    load_early = copies.local(grads_in, early.at[:, 0:PAD_FF])
    load_layer = copies.local(layer_in, layer_parts)
    ready()
    for copy in loads:
        copy.wait()
    layers = ReduceRing(
        copies,
        at_y,
        y,
        lambda k, rows: layer_parts[k % 4, rows].astype(F32),
        layer_sent,
        layer_got,
        128,
        lambda k, span: layer_in.at[k % 4, span],
    )
    layers.far()
    layers.direct(1)
    layers.direct(-1)
    ups = second_ring(copies, up_mid, x, z, core, up_out2, up_got2)
    ups.far()
    ups.direct(1)
    ups.direct(-1)
    load_low.wait()

    @pl.loop(0, tokens.shape[1] // 512)
    def _(tile):
        columns = pl.ds(pl.multiple_of(tile * 512, 512), 512)
        early[columns, PAD_FF:EARLY_W] = tn(tokens[:, columns], attended[...]).astype(BF16)

    load_early.wait()
    early_plane = ReducePlane(
        copies,
        early,
        slice(0, EARLY_W),
        x,
        z,
        core,
        early_out1,
        early_got1,
        early_mid,
        early_out2,
        early_got2,
    )
    early_stages = iter(early_plane.stages())
    next(early_stages)()
    me = core * 4 + y
    back_copies, local = [], []

    def send_back(sums_ref, out_ref):
        def cut(index):
            return sums_ref.at[pl.ds(pl.multiple_of(index * 16, 16), 16)]

        local.append(copies.local(cut(me), out_ref.at[me]))
        for c, d in peers:
            back_copies.append(copies.start(cut(c * 4 + d), out_ref.at[me], {"core": c, "y": d}))

    send_back(gate_sum, gate_out)

    @pl.loop(0, 2, unroll=True)
    def _(half):
        rows = pl.ds(pl.multiple_of(half * 512, 512), 512)
        grad_mixed = nn(tokens[rows], att[:, OUT_AT]).astype(BF16).astype(F32)
        numer = grad_mixed * shares[rows]
        grad_numer[rows] = numer.astype(BF16)
        product = numer * attended[rows].astype(F32)
        for head in range(2):
            lanes = slice(head * HEAD_V, (head + 1) * HEAD_V)
            total = -jnp.sum(product[:, lanes], axis=-1, keepdims=True)
            grad_denom[rows, lanes] = jnp.broadcast_to(total, (512, HEAD_V))

    load_raw = copies.local(raw_in, tokens)
    grad_k[...] = jnp.zeros_like(grad_k)
    grad_v[...] = jnp.zeros_like(grad_v)

    def attend_back(head, block):
        lanes = slice(head * HEAD_V, (head + 1) * HEAD_V)
        rows, extent = slice(block * 256, (block + 1) * 256), (block + 1) * 256
        q = jnp.where(head_lanes(head), qs[rows], 0)
        k = ks[0:extent]
        half, scores, keep = scores_of(q, k, block, extent)
        numer = grad_numer[rows, lanes]
        total = grad_denom[rows, head * HEAD_V : head * HEAD_V + 1]
        grad_scores = nt(numer, values[0:extent, lanes]) + total
        grad_s = jnp.where(keep, grad_scores * (0.25 + 0.25 * half), 0.0).astype(BF16)
        moved = nn(grad_s, k)
        if head == 0:
            grad_q[rows] = jnp.where(head_lanes(0), moved, 0.0)
        else:
            grad_q[rows] += jnp.where(head_lanes(1), moved, 0.0)
        grad_k[0:extent] += tn(grad_s, q)
        grad_v[0:extent, lanes] += tn(scores.astype(BF16), numer)

    for block in range(4):
        attend_back(0, block)
    next(early_stages)()
    ups.onward(1)
    ups.onward(-1)
    for block in range(4):
        attend_back(1, block)

    def join(rows):
        inverse = inverses[rows]
        both = grad_q[rows] + pltpu.roll(grad_k[rows], 32, 1)
        grad_qk[rows] = both.astype(BF16)
        scaled_qk[rows] = (both * inverse).astype(BF16)
        both = grad_v[rows]
        grad_values[rows] = both.astype(BF16)
        scaled_values[rows] = (both * jnp.concatenate((inverse, inverse), axis=1)).astype(BF16)

    row_steps(0, 1024, join, 128)
    sums = ReduceTokens(
        copies,
        part_maker([(grad_values, att, VALUE_AT), (grad_qk, att, QK_AT)], y, core),
        y,
        core,
        own,
        sib,
        got_sib,
        out,
        got,
    )
    sums.part(2)
    sums.part(1)
    for _ in range(4):
        next(early_stages)()
    sums.one()
    sums.part(-1)
    sums.part(0)
    load_layer.wait()
    layers.onward(1)
    layers.onward(-1)
    load_raw.wait()

    @pl.loop(0, tokens.shape[1] // 512)
    def _(tile):
        columns = pl.ds(pl.multiple_of(tile * 512, 512), 512)
        left = tokens[:, columns]
        gain = att[columns, 576:577].astype(F32)
        late[columns, 0:256] = (tn(left, scaled_values[...]) * gain).astype(BF16)
        late[columns, 256:LATE_W] = (tn(left, scaled_qk[...]) * gain).astype(BF16)

    late_plane = ReducePlane(
        copies,
        late,
        slice(0, LATE_W),
        x,
        z,
        core,
        late_out1,
        late_got1,
        late_mid,
        late_out2,
        late_got2,
    )
    late_stages = iter(late_plane.stages())
    next(late_stages)()
    def take(target):
        def act(rows, total):
            target[rows] = total.astype(BF16)

        return act

    sums.two()
    next(late_stages)()
    ups.each(take(up_sum))
    send_back(up_sum, up_out)
    for _ in range(4):
        next(late_stages)()
    gain_part[...] = jnp.zeros_like(gain_part)

    def back(rows, total):
        moved, terms = norm_back_rows(total, raw[rows].astype(F32), gains[0:1])
        gain_part[...] += terms[:8] + terms[8:]
        last[rows] = (grad_middle[rows] + moved).astype(BF16)

    sums.each(back)
    waits = [copies.swap(last, grad_in, partner, swaps)]
    row = lax.broadcasted_iota(jnp.int32, (8, 1), 0)
    gain_part[...] = jnp.where(
        row == 0,
        jnp.sum(gain_part[...], axis=0, keepdims=True),
        jnp.where(row == 1, jnp.sum(grad_gain2[...], axis=0, keepdims=True), 0.0),
    )
    here = 4 * z + x

    def lanes_of(block):
        return pl.ds(pl.multiple_of(block * 128, 128), 128)

    gain_copies = [
        copies.start(gain_part.at[:, lanes_of(4 * b + a)], gain_got.at[here], at_xz(a, b))
        for a, b in planes
    ]
    gain_own = copies.local(gain_part.at[:, lanes_of(here)], gain_got.at[here])
    for stage in early_stages:
        stage()
    for _ in range(4):
        next(late_stages)()
    for piece in range(PIECES):
        layers.arrive(piece)

    def add(rows):
        layer[rows] = (middle[rows] + layers.total(rows)).astype(BF16)

    row_steps(0, 128, add)
    waits.append(copies.swap(layer, layer_out, partner, swaps))
    early_plane.each(take(early_sum))
    send_back(early_sum, early_out)
    for stage in late_stages:
        stage()
    for copy in gain_copies:
        copy.wait_recv()
    gain_own.wait()
    gain_sum[...] = jnp.sum(gain_got[...], axis=0)
    for c, d in peers:
        back_copies.append(copies.start(gain_sum, gain_back.at[me], {"core": c, "y": d}))
    local.append(copies.local(gain_sum, gain_back.at[me]))
    late_plane.each(take(late_sum))
    send_back(late_sum, late_out)
    for copy in back_copies:
        copy.wait_recv()
    for copy in local:
        copy.wait()
    gain_out[...] = jnp.sum(gain_back[...], axis=0)
    for wait in waits:
        wait()
    copies.finish()


def unpack_kernel(
    late, early, gates, ups, layer, last, hot, query, key, value, out, gate, up, down, layer_out, grad_in
):
    here = gate.shape[1] // 8
    for block in range(8):
        for source, at, grad in ((gates, 0, gate), (ups, 0, up), (early, 0, down)):
            cut = source[block, :, at : at + here]
            grad[:, block * here : (block + 1) * here] = cut.astype(F32)
        value[:, block * 256 : (block + 1) * 256] = late[block, :, 0:256].astype(F32)
        out[:, block * 256 : (block + 1) * 256] = early[block, :, PAD_FF:EARLY_W].astype(F32)
        query[:, block * 32 : (block + 1) * 32] = late[block, :, 256:288].astype(F32)
        key[:, block * 32 : (block + 1) * 32] = late[block, :, 288:320].astype(F32)
    runs = layer.shape[1] // 256
    for run in range(runs):
        for source, target in ((layer, layer_out), (last, grad_in)):
            low = source[:, run * 128 : (run + 1) * 128]
            high = source[:, (runs + run) * 128 : (runs + run + 1) * 128]
            both = jnp.concatenate((low, high), axis=1)
            target[:, run * 256 : (run + 1) * 256] = nn(both, hot[...]).astype(target.dtype)


HBM, VMEM, LOAD = pl.ANY, pltpu.VMEM, "load"


def call(kernel, number, ins, outs, scratch, sems, flops):
    def spec(space):
        return pl.BlockSpec(memory_space=space)

    remote = {}
    given = kernel
    if any(space == LOAD for _, space in ins):
        places = [at for at, (_, space) in enumerate(ins) if space == LOAD]
        held = [VMEM(ins[at][0].shape, ins[at][0].dtype) for at in places]
        scratch = list(scratch) + held + [pltpu.SemaphoreType.DMA((len(held),))]

        def kernel(*refs):
            refs = list(refs)
            send, recv = refs[-2:]
            first = len(refs) - 3 - len(held)
            buffers, arrived = refs[first:-3], refs[-3]
            loads = []
            for index, at in enumerate(places):
                loads.append(pltpu.make_async_copy(refs[at], buffers[index], arrived.at[index]))
                loads[-1].start()
                refs[at] = buffers[index]
            given(*refs[:first], send, recv, loads=loads)

        ins = [(array, HBM if space == LOAD else space) for array, space in ins]
    if number is not None:
        scratch = list(scratch) + [pltpu.SemaphoreType.DMA((sems,)), pltpu.SemaphoreType.DMA((sems,))]
        remote = dict(collective_id=number, has_side_effects=True)
    return pl.pallas_call(
        kernel,
        out_shape=[jax.ShapeDtypeStruct(shape, dtype) for shape, dtype, _ in outs],
        in_specs=[spec(space) for _, space in ins],
        out_specs=[spec(space) for _, _, space in outs],
        scratch_shapes=scratch,
        compiler_params=pltpu.CompilerParams(vmem_limit_bytes=VMEM_LIMIT, **remote),
        cost_estimate=pl.CostEstimate(flops=flops, bytes_accessed=2**26, transcendentals=0),
        name=given.__name__,
    )(*[array for array, _ in ins])


def ring_scratch(width, own=True):
    sums = [VMEM((4, 128, width), F32)] if own else []
    return sums + [
        VMEM((4, 128, width), BF16),
        VMEM((4, 128, width), BF16),
        VMEM((3, 128, width), BF16),
        VMEM((3, 128, width), BF16),
    ]


def plane_scratch(width):
    return [
        VMEM((4, 1, 128, width), BF16),
        VMEM((4, 3, 128, width), BF16),
        VMEM((4, 128, width), BF16),
        VMEM((1, 128, width), BF16),
        VMEM((3, 128, width), BF16),
    ]


def body(
    hidden_in,
    norm1_gain,
    query_weight,
    key_weight,
    value_weight,
    out_weight,
    norm2_gain,
    gate_weight,
    up_weight,
    down_weight,
    cotangent,
    source_id,
    source_counts,
):
    rows, toks, width = hidden_in.shape
    depth, ff = gate_weight.shape
    length, held = 8 * toks, 8 * depth
    mlp_w = 3 * PAD_FF
    scale = row_scale(source_id, source_counts).reshape(1, 1)
    (
        att,
        weights,
        raw_all,
        low,
        qs,
        ks,
        values,
        attended,
        shares,
        inverses,
        gains,
        raw,
        top,
        middle,
        normed2,
    ) = call(
        forward_kernel,
        0,
        [
            (array, VMEM)
            for array in (
                hidden_in.reshape(toks, width),
                cotangent.reshape(toks, width),
                scale,
                lane_order(False),
                query_weight,
                key_weight,
                value_weight,
                out_weight,
                gate_weight,
                up_weight,
                down_weight,
                jnp.stack((norm1_gain, norm2_gain), axis=1),
            )
        ],
        [
            ((width, ATT_W), BF16, HBM),
            ((width, mlp_w), BF16, HBM),
            ((length, width), BF16, HBM),
            ((length, width), BF16, HBM),
            ((length, 128), BF16, HBM),
            ((length, 128), BF16, HBM),
            ((length, 256), BF16, HBM),
            ((length, 256), BF16, HBM),
            ((length, 256), F32, HBM),
            ((length, 128), F32, HBM),
            ((8, width), F32, VMEM),
            ((toks, width), BF16, VMEM),
            ((toks, width), BF16, VMEM),
            ((toks, width), F32, VMEM),
            ((length, width), BF16, HBM),
        ],
        [
            VMEM((8, depth, ATT_W), BF16),
            VMEM((8, depth, mlp_w), BF16),
            VMEM((toks, width), BF16),
            VMEM((toks, width), BF16),
            VMEM((held, ATT_W), BF16),
            VMEM((held, mlp_w), BF16),
            VMEM((length, width), BF16),
            VMEM((width, ATT_W), BF16),
            VMEM((width, 384), BF16),
        ]
        + ring_scratch(width)
        + [
            VMEM((toks, width), BF16),
            VMEM((length, 128), BF16),
            VMEM((length, 128), BF16),
            VMEM((length, 256), BF16),
            VMEM((length, 256), BF16),
            VMEM((length, 256), F32),
            VMEM((length, 128), F32),
        ],
        250,
        4 * 10**9,
    )
    grad_middle, grad_gain2, middle_low, grads, gate_sum, up_mid, layer_parts = call(
        mlp_kernel,
        1,
        [
            (normed2, HBM),
            (low, HBM),
            (weights, HBM),
            (middle, LOAD),
            (top, LOAD),
            (gains, LOAD),
        ],
        [
            ((toks, width), F32, VMEM),
            ((8, width), F32, VMEM),
            ((length, width), BF16, HBM),
            ((width, PAD_FF), BF16, HBM),
            ((held, PAD_FF), BF16, VMEM),
            ((4, held, PAD_FF), BF16, VMEM),
            ((4, toks, width), BF16, HBM),
        ],
        [
            VMEM((length, width), BF16),
            VMEM((length, width), BF16),
            VMEM((width, mlp_w), BF16),
            VMEM((length, PAD_FF), BF16),
            VMEM((length, PAD_FF), BF16),
            VMEM((length, PAD_FF), BF16),
        ]
        + ring_scratch(width)
        + [
            VMEM((4, toks, width), BF16),
            VMEM((4, toks, width), BF16),
            VMEM((4, toks, width), BF16),
            VMEM((toks, width), BF16),
        ]
        + plane_scratch(PAD_FF)
        + plane_scratch(PAD_FF)[:2],
        200,
        30 * 10**9,
    )
    late_back, early_back, gate_back, up_back, last, layer, gain_sums = call(
        back_kernel,
        2,
        [
            (middle_low, HBM),
            (raw_all, HBM),
            (att, LOAD),
            (qs, LOAD),
            (ks, LOAD),
            (values, LOAD),
            (attended, LOAD),
            (shares, LOAD),
            (inverses, LOAD),
            (raw, LOAD),
            (grad_middle, LOAD),
            (middle, LOAD),
            (gains, LOAD),
            (grad_gain2, LOAD),
            (grads, HBM),
            (layer_parts, HBM),
            (gate_sum, LOAD),
            (up_mid, LOAD),
        ],
        [
            ((8, depth, LATE_W), BF16, HBM),
            ((8, depth, EARLY_W), BF16, HBM),
            ((8, depth, PAD_FF), BF16, HBM),
            ((8, depth, PAD_FF), BF16, HBM),
            ((toks, width), BF16, HBM),
            ((toks, width), BF16, HBM),
            ((8, 128), F32, VMEM),
        ],
        [
            VMEM((length, width), BF16),
            VMEM((width, EARLY_W), BF16),
            VMEM((width, LATE_W), BF16),
            VMEM((4, toks, width), BF16),
            VMEM((length, 256), BF16),
            VMEM((length, 256), F32),
            VMEM((length, 128), F32),
            VMEM((length, 128), F32),
            VMEM((length, 256), F32),
            VMEM((length, 128), BF16),
            VMEM((length, 256), BF16),
            VMEM((length, 128), BF16),
            VMEM((length, 256), BF16),
        ]
        + ring_scratch(width)
        + [VMEM((1, toks, width), BF16), VMEM((3, toks, width), BF16)]
        + plane_scratch(EARLY_W)
        + plane_scratch(LATE_W)
        + [
            VMEM((1, held, PAD_FF), BF16),
            VMEM((3, held, PAD_FF), BF16),
            VMEM((held, PAD_FF), BF16),
            VMEM((held, EARLY_W), BF16),
            VMEM((held, LATE_W), BF16),
            VMEM((toks, width), BF16),
            VMEM((toks, width), BF16),
            VMEM((8, width), F32),
            VMEM((16, 8, 128), F32),
            VMEM((8, 128), F32),
            VMEM((8, 8, 128), F32),
        ],
        240,
        8 * 10**9,
    )
    grads_out = call(
        unpack_kernel,
        None,
        [(array, VMEM) for array in (late_back, early_back, gate_back, up_back, layer, last, lane_order(True))],
        [
            ((depth, query_weight.shape[1]), F32, VMEM),
            ((depth, key_weight.shape[1]), F32, VMEM),
            ((depth, value_weight.shape[1]), F32, VMEM),
            ((depth, out_weight.shape[1]), F32, VMEM),
            ((depth, ff), F32, VMEM),
            ((depth, ff), F32, VMEM),
            ((depth, ff), F32, VMEM),
            ((toks, width), BF16, VMEM),
            ((toks, width), F32, VMEM),
        ],
        [],
        0,
        0,
    )
    grad_query, grad_key, grad_value, grad_out, grad_gate, grad_up, grad_down = grads_out[:7]
    at = (lax.axis_index("core") * 4 + lax.axis_index("y")) * depth
    pair = lax.dynamic_slice(gain_sums, (0, at), (8, depth))
    return (
        grads_out[7].reshape(rows, toks, width),
        grads_out[8].reshape(rows, toks, width),
        pair[0],
        grad_query,
        grad_key,
        grad_value,
        grad_out,
        pair[1],
        grad_gate,
        grad_up,
        grad_down,
    )


def solution(mesh):
    zlo, chips_x, cores, chips_y, zhi = 2, 4, 2, 4, 2
    whole = Mesh(mesh.devices.reshape(zlo, chips_x, cores, chips_y, zhi), AXES)
    weight = P(AXES, None)
    gain = P(AXES)
    tokens = P(DP, SEQ, None)
    return jax.shard_map(
        body,
        mesh=whole,
        in_specs=(
            tokens,
            gain,
            weight,
            weight,
            weight,
            weight,
            gain,
            weight,
            weight,
            weight,
            tokens,
            P(DP),
            P(),
        ),
        out_specs=(
            tokens,
            tokens,
            gain,
            weight,
            weight,
            weight,
            weight,
            gain,
            weight,
            weight,
            weight,
        ),
        check_vma=False,
    )
```
